128 devices in a mesh: grp: 8 (over x_lo, y), blk: 16 (over z, x_hi, core).
Axes of the slice: x: 4 (x_hi: 2, x_lo: 2; x = x_hi * 2 + x_lo), y: 4, z: 4, core: 2. Of those that a mesh axis runs over, the one named last changes fastest.
Arguments:
- features: bfloat16 [16384, 4096], P('blk', 'grp'), may hold values from -6 to 6
- grad_out: bfloat16 [16384, 4096], P('blk', 'grp'), may hold values from -6 to 6
- scores: float32 [16384], P('blk'), may hold values from 0.05 to 1
- counts: int32 [16, 2], P('blk'), may hold values from 0 to 1024, as said below
- w_gate: bfloat16 [2, 1536, 4096], P(None, 'grp', 'blk'), may hold values from -0.09375 to 0.09375
- w_up: bfloat16 [2, 1536, 4096], P(None, 'grp', 'blk'), may hold values from -0.09375 to 0.09375
- w_down: bfloat16 [2, 1536, 4096], P(None, 'grp', 'blk'), may hold values from -0.15625 to 0.15625
Outputs:
- grad_features: bfloat16 [16384, 4096], P('blk', 'grp')
- grad_scores: float32 [16384], P('blk')
- grad_gate: float32 [2, 1536, 4096], P(None, 'grp', 'blk')
- grad_up: float32 [2, 1536, 4096], P(None, 'grp', 'blk')
- grad_down: float32 [2, 1536, 4096], P(None, 'grp', 'blk')
The draws below stay inside these ranges and needn't reach their ends.
Inputs may be any that keep to these rules, and one draw needn't show every extreme that they name: Every count is a multiple of 128; the counts of one row block sum to at most 1024, and in every draw some row block sends all 1024 rows to one expert.
All inputs are finite; a program needn't handle non-finite values.
Results may differ from the reference program's by a relative error of at most 0.019.
Values may be sent and summed in bfloat16 or wider, within the bound.
No kernel may reach another device: no remote copies, remote signals or barrier semaphores. Data moves between devices by JAX's collectives and lax.ppermute only.
A program may use at most 256 MiB of HBM per device.

```python
import math
import jax
import jax.numpy as jnp
from jax import lax

D = 4096
F = 1536
ROWS_DEV = 1024
EXP = 2
BLOCK = 128
ROWS = 16384
N_BLK = 16


def draw_counts(key, part):
    key = jax.random.fold_in(key, 11)
    key_live, key_full, key_cut = jax.random.split(key, 3)
    block_count = ROWS_DEV // BLOCK
    live = jax.random.randint(key_live, (N_BLK,), 1, block_count + 1)
    fullest = jax.random.randint(key_full, (), 0, N_BLK)
    is_full = jnp.arange(N_BLK) == fullest
    live = jnp.where(is_full, block_count, live)
    cuts = jax.random.randint(key_cut, (N_BLK, EXP - 1), 0, live[:, None] + 1)
    cuts = jnp.where(is_full[:, None], block_count, cuts)
    cuts = jnp.sort(cuts, axis=1)
    edges = jnp.concatenate([jnp.zeros((N_BLK, 1), jnp.int32), cuts.astype(jnp.int32), live[:, None].astype(jnp.int32)], axis=1)
    return ((edges[:, 1:] - edges[:, :-1]) * BLOCK).astype(jnp.int32)


def spiked(values, rng, source, target, shards_of, factor):
    owner, partner = [(jnp.arange(values.shape[position]) // (values.shape[position] // shards_of)).reshape([-1 if axis == position else 1 for axis in range(values.ndim)]) for position in (source, target)]
    chosen = jax.random.permutation(rng, shards_of)[partner]
    strong = (owner == chosen) | (owner == (partner + shards_of // 2) % shards_of)
    return jnp.where(strong, factor * values, values)


def block_levels(rng, extent, shards, least, high):
    loudness, own = 1.0, jax.random.fold_in(rng, 6)
    for dim, shards_of in shards:
        draws = jnp.exp(jax.random.uniform(jax.random.fold_in(own, dim), (shards_of,), jnp.float32, least / len(shards), high / len(shards)))
        loudness = loudness * jnp.repeat(draws, extent[dim] // shards_of).reshape([-1 if axis == dim else 1 for axis in range(len(extent))])
    return loudness


def scatter_about(own_key, extent, deviation, most, shards=(), kind=jnp.bfloat16):
    result = jax.random.normal(own_key, extent, jnp.float32) * deviation
    if len(shards) > 0:
        result = block_levels(own_key, extent, shards, -0.22, 0.18) * result
    return jnp.clip(result, min=-most, max=most).astype(kind)


def noise_with(own_key, extent, spread, limit, pieces, heavy, kind=jnp.bfloat16):
    entries = spread * jax.random.normal(own_key, extent, jnp.float32)
    if pieces:
        entries = entries * block_levels(own_key, extent, pieces, -0.22, 0.18)
    return jnp.clip(spiked(entries, jax.random.fold_in(own_key, 3), *heavy), -limit, limit).astype(kind)


def setup_inputs(seed: int = 0) -> dict:
    streams_of = jax.random.split(jax.random.key(seed), 8)
    features = noise_with(streams_of[0], (ROWS, D), 1.0, 6.0, ((0, 16), (1, 8)), (0, 1, 16, 2.0))
    grad_out = noise_with(streams_of[1], (ROWS, D), 1.0, 6.0, ((0, 16), (1, 8)), (0, 1, 16, 2.0))
    scores = jnp.clip(jnp.exp(math.log(1.0) - 2.9957323 * jax.random.uniform(streams_of[2], (ROWS,), jnp.float32) ** block_levels(streams_of[2], (ROWS,), ((0, 16),), -0.2, 0.2)), 0.05, 1.0)
    counts = draw_counts(jax.random.fold_in(streams_of[7], 71), 0)
    w_gate = scatter_about(streams_of[4], (EXP, F, D), D ** -0.5, 0.09375, ((1, 8), (2, 16)))
    w_up = scatter_about(streams_of[5], (EXP, F, D), D ** -0.5, 0.09375, ((1, 8), (2, 16)))
    w_down = scatter_about(streams_of[6], (EXP, F, D), F ** -0.5, 0.15625, ((1, 8), (2, 16)))
    return {"features": features, "grad_out": grad_out, "scores": scores, "counts": counts, "w_gate": w_gate, "w_up": w_up, "w_down": w_down}


def expert_layout(counts):
    block_count = ROWS_DEV // BLOCK
    bounds = jnp.cumsum(counts, axis=1).astype(jnp.int32)
    starts = jnp.arange(block_count, dtype=jnp.int32) * BLOCK
    above = (starts[None, :, None] >= bounds[:, None, :]).astype(jnp.int32)
    expert_ids = jnp.minimum(jnp.sum(above, axis=2), EXP - 1).astype(jnp.int32)
    live_flags = starts[None, :] < bounds[:, EXP - 1:EXP]
    return expert_ids, live_flags


def block_grads(row_block, grad_block, score_block, gate_mat, up_mat, down_mat, live_flag):
    contract = (((1,), (1,)), ((), ()))
    gate_pre = lax.dot_general(row_block, gate_mat, contract, preferred_element_type=jnp.float32)
    up_pre = lax.dot_general(row_block, up_mat, contract, preferred_element_type=jnp.float32)
    back_grad = lax.dot_general(grad_block, down_mat, contract, preferred_element_type=jnp.float32)
    sig_gate = jax.nn.sigmoid(gate_pre)
    act_gate = gate_pre * sig_gate
    hidden = lax.optimization_barrier((act_gate * up_pre).astype(jnp.bfloat16))
    hidden_wide = hidden.astype(jnp.float32)
    row_mask = jnp.where(live_flag, 1.0, 0.0).astype(jnp.float32)
    row_scale = score_block * row_mask
    score_grad = jnp.sum(hidden_wide * back_grad, axis=1) * row_mask
    hid_grad = row_scale[:, None] * back_grad
    gate_grad = (hid_grad * up_pre * sig_gate * (1.0 + gate_pre * (1.0 - sig_gate))).astype(jnp.bfloat16)
    up_grad = (hid_grad * act_gate).astype(jnp.bfloat16)
    scaled = (row_scale[:, None] * hidden_wide).astype(jnp.bfloat16)
    return score_grad, gate_grad, up_grad, scaled


def add_expert(accum, part, expert_id):
    current = lax.dynamic_index_in_dim(accum, expert_id, 0, False)
    return lax.dynamic_update_index_in_dim(accum, current + part, expert_id, 0)


def reference(features, grad_out, scores, counts, w_gate, w_up, w_down):
    block_count = ROWS_DEV // BLOCK
    expert_ids, live_flags = expert_layout(counts)
    row_blocks = features.reshape(N_BLK, block_count, BLOCK, D)
    grad_blocks = grad_out.reshape(N_BLK, block_count, BLOCK, D)
    score_blocks = scores.reshape(N_BLK, block_count, BLOCK)
    zeros_acc = jnp.zeros((EXP, F, D), jnp.float32)
    tcon = (((0,), (0,)), ((), ()))

    def block_step(carried, inputs):
        row_block, grad_block, score_block, expert_id, live_flag = inputs
        gate_mat = lax.dynamic_index_in_dim(w_gate, expert_id, 0, False)
        up_mat = lax.dynamic_index_in_dim(w_up, expert_id, 0, False)
        down_mat = lax.dynamic_index_in_dim(w_down, expert_id, 0, False)
        score_grad, gate_grad, up_grad, scaled = block_grads(row_block, grad_block, score_block, gate_mat, up_mat, down_mat, live_flag)
        input_grad = (jnp.dot(gate_grad, gate_mat, preferred_element_type=jnp.float32) + jnp.dot(up_grad, up_mat, preferred_element_type=jnp.float32)).astype(jnp.bfloat16)
        part_gate = lax.dot_general(gate_grad, row_block, tcon, preferred_element_type=jnp.float32)
        part_up = lax.dot_general(up_grad, row_block, tcon, preferred_element_type=jnp.float32)
        part_down = lax.dot_general(scaled, grad_block, tcon, preferred_element_type=jnp.float32)
        carried = (add_expert(carried[0], part_gate, expert_id), add_expert(carried[1], part_up, expert_id), add_expert(carried[2], part_down, expert_id))
        return carried, (score_grad, input_grad)

    def device_step(totals, inputs):
        accums, outputs = lax.scan(block_step, (zeros_acc, zeros_acc, zeros_acc), inputs)
        rounded = tuple(lax.optimization_barrier(accum.astype(jnp.bfloat16)).astype(jnp.float32) for accum in accums)
        totals = (totals[0] + rounded[0], totals[1] + rounded[1], totals[2] + rounded[2])
        return totals, outputs

    totals, (score_grads, input_grads) = lax.scan(device_step, (zeros_acc, zeros_acc, zeros_acc), (row_blocks, grad_blocks, score_blocks, expert_ids, live_flags))
    return input_grads.reshape(ROWS, D), score_grads.reshape(ROWS), totals[0], totals[1], totals[2]
```

```python
import functools

import jax
import jax.numpy as jnp
from jax import lax
from jax.experimental import pallas as pl
from jax.experimental.pallas import tpu as pltpu
from jax.sharding import Mesh
from jax.sharding import PartitionSpec as P

EXP = 2
BLOCK = 128
TILE = 256
BF = jnp.bfloat16
F32 = jnp.float32
NT = (((1,), (1,)), ((), ()))
OFFS = (0, 3, 1, 2)
ANY = pl.BlockSpec(memory_space=pl.ANY)
VM = pl.BlockSpec(memory_space=pltpu.VMEM)
SM = pl.BlockSpec(memory_space=pltpu.SMEM)


def ring(n, k):
    return [(i, (i + k) % n) for i in range(n)]


def home(xl, z):
    return (xl, z) if z // 2 == xl else (1 - xl, (z + 2) % 4)


def swap_pairs(flip):
    pairs = []
    for xl in range(2):
        for z in range(4):
            for xh in range(2):
                a, b = home(xl, z)
                pairs.append(((xl * 4 + z) * 2 + xh, (a * 4 + b) * 2 + (xh ^ flip)))
    return pairs


def y_of(sc, p):
    return lax.rem(sc[0] + OFFS[p], 4)


def load_rows(sc, pieces, dst, sem):
    rows, width = pieces[0].shape
    half = rows // 2
    copies = []
    for p in range(3):
        at = pl.ds(pl.multiple_of(y_of(sc, p) * width, width), width)
        copies.append(pltpu.make_async_copy(pieces[p], dst.at[:, at], sem.at[p]))
    at = pl.ds(pl.multiple_of(y_of(sc, 3) * width, width), width)
    copies.append(pltpu.make_async_copy(pieces[3], dst.at[pl.ds(0, half), at], sem.at[3]))
    copies.append(pltpu.make_async_copy(pieces[4], dst.at[pl.ds(half, half), at], sem.at[4]))
    return copies


def load_weights(w_ref, lo, nw, dst, sem):
    hid, cols = w_ref.shape[4], w_ref.shape[5]
    copies = []
    for w in range(nw):
        for h in range(2):
            for cb in range(8):
                at = (w * 2 + h) * hid
                copies.append(
                    pltpu.make_async_copy(
                        w_ref.at[h, cb, lo + w],
                        dst.at[:, pl.ds(at, hid), pl.ds(cb * cols, cols)],
                        sem.at[(w * 2 + h) * 8 + cb],
                    )
                )
    return copies


def expert_of(sc, block):
    return (block * BLOCK >= sc[2]).astype(jnp.int32)


def by_tile(sc, tile, work):
    low, high = expert_of(sc, 2 * tile), expert_of(sc, 2 * tile + 1)
    start = tile * TILE

    @pl.when(low == high)
    def _():
        work(pl.multiple_of(start, TILE), TILE, low)

    @pl.when(low != high)
    def _():
        work(pl.multiple_of(start, BLOCK), BLOCK, low)
        work(pl.multiple_of(start + BLOCK, BLOCK), BLOCK, high)


def pre_kernel(lo, nw, sc, x0, x1, x2, x3, x4, w_ref, own, send, xv, wv, xsem, wsem):
    copies = load_rows(sc, (x0, x1, x2, x3, x4), xv, xsem) + load_weights(w_ref, lo, nw, wv, wsem)
    for c in copies:
        c.start()
    for c in copies:
        c.wait()

    def work(start, size, expert):
        at = pl.ds(start, size)
        part = lax.dot_general(xv[at, :], wv[expert], NT, preferred_element_type=F32)
        own[at, :] = part
        send[at, :] = part.astype(BF)

    @pl.loop(0, xv.shape[0] // TILE)
    def _(t):
        by_tile(sc, t, work)


def pre_part(sc, pieces, w_all, lo, nw):
    rows, width = pieces[0].shape
    n = nw * 384
    return pl.pallas_call(
        functools.partial(pre_kernel, lo, nw),
        out_shape=(
            jax.ShapeDtypeStruct((rows, n), F32),
            jax.ShapeDtypeStruct((rows, n), BF),
        ),
        in_specs=[SM] + [ANY] * 6,
        out_specs=(VM, VM),
        scratch_shapes=[
            pltpu.VMEM((rows, 4 * width), BF),
            pltpu.VMEM((EXP, n, 4 * width), BF),
            pltpu.SemaphoreType.DMA((5,)),
            pltpu.SemaphoreType.DMA((nw * 16,)),
        ],
        compiler_params=pltpu.CompilerParams(vmem_limit_bytes=40 << 20),
        cost_estimate=pl.CostEstimate(
            flops=2 * rows * n * 4 * width, bytes_accessed=12 << 20, transcendentals=0
        ),
    )(sc, *pieces, w_all)


def back_kernel(
    sc, scores, own_gu, got_gu, own_b, got_b,
    x0, x1, x2, x3, x4, g0, g1, g2, g3, g4, w_ref,
    sgrad, dx, keep, away,
    xv, gv, wv, gu, gut, st, dxv, dgu, dd, xsem, gsem, wsem, osem, dsem,
):
    rows, wide = xv.shape
    width = wide // 4
    hid = 192
    wload = load_weights(w_ref, 0, 2, wv, wsem)
    gload = load_rows(sc, (g0, g1, g2, g3, g4), gv, gsem)
    xload = load_rows(sc, (x0, x1, x2, x3, x4), xv, xsem)
    for c in wload + gload + xload:
        c.start()

    @pl.loop(0, rows // BLOCK)
    def _(b):
        at = pl.ds(pl.multiple_of(b * BLOCK, BLOCK), BLOCK)
        live = (b * BLOCK < sc[3]).astype(F32)
        both = own_gu[at, :] + got_gu[at, :].astype(F32)
        gate, up = both[:, :384], both[:, 384:]
        back = own_b[at, :] + got_b[at, :].astype(F32)
        sig = jax.nn.sigmoid(gate)
        act = gate * sig
        hidden = (act * up).astype(BF).astype(F32)
        mine = (lax.broadcasted_iota(jnp.int32, hidden.shape, 1) >= hid).astype(jnp.int32) == sc[1]
        total = jnp.sum(jnp.where(mine, hidden * back, 0.0), axis=1, keepdims=True) * live
        sgrad[pl.ds(b, 1), :] = jnp.transpose(jnp.broadcast_to(total, (BLOCK, BLOCK)))[:1]
        scale = jnp.transpose(jnp.broadcast_to(scores[pl.ds(b, 1), :], (BLOCK, BLOCK)))[:, :1] * live
        hid_grad = scale * back
        gate_grad = (hid_grad * up * sig * (1.0 + gate * (1.0 - sig))).astype(BF)
        up_grad = (hid_grad * act).astype(BF)
        scaled = (scale * hidden).astype(BF)
        gu[at, :384] = gate_grad
        gu[at, 384:] = up_grad
        tg, tu, ts = jnp.transpose(gate_grad), jnp.transpose(up_grad), jnp.transpose(scaled)
        expert = expert_of(sc, b)
        other = 1 - expert
        gut[expert, :384, at] = tg
        gut[expert, 384:, at] = tu
        st[expert, :, at] = ts
        gut[other, :, at] = jnp.zeros((768, BLOCK), BF)
        st[other, :, at] = jnp.zeros((384, BLOCK), BF)

    for c in gload + xload:
        c.wait()

    def weight_out(src, w, e, h, slot):
        outs = []
        for rel, out in enumerate((keep, away)):
            for zz in range(2):
                for xh in range(2):
                    core = sc[4] if rel == 0 else 1 - sc[4]
                    cols = pl.ds(pl.multiple_of(((zz * 2 + xh) * 2 + core) * 256, 256), 256)
                    outs.append(
                        pltpu.make_async_copy(
                            src.at[e, pl.ds(h * hid, hid), cols],
                            out.at[h * 2 + zz, xh, w, e],
                            dsem.at[slot * 8 + rel * 4 + zz * 2 + xh],
                        )
                    )
        return outs

    outs = []
    for e in range(EXP):
        for n in range(4):
            at = pl.ds(n * width, width)
            dd[e, :, at] = jnp.dot(st[e], gv[:, at], preferred_element_type=F32).astype(BF)
        for h in range(2):
            now = weight_out(dd, 2, e, h, (2 * EXP + e) * 2 + h)
            for c in now:
                c.start()
            outs += now
    for e in range(EXP):
        for n in range(4):
            at = pl.ds(n * width, width)
            dgu[e, :, at] = jnp.dot(gut[e], xv[:, at], preferred_element_type=F32).astype(BF)
        for w in range(2):
            for h in range(2):
                now = []
                for c in weight_out(dgu.at[:, pl.ds(w * 384, 384), :], w, e, h, (w * EXP + e) * 2 + h):
                    c.start()
                    now.append(c)
                outs += now

    for c in wload:
        c.wait()

    def work(start, size, expert):
        at = pl.ds(start, size)
        dxv[at, :] = jnp.dot(gu[at, :], wv[expert], preferred_element_type=F32).astype(BF)

    @pl.loop(0, rows // TILE)
    def _(t):
        by_tile(sc, t, work)

    for p in range(4):
        at = pl.ds(pl.multiple_of(y_of(sc, p) * width, width), width)
        c = pltpu.make_async_copy(dxv.at[:, at], dx.at[p], osem.at[p])
        c.start()
        outs.append(c)
    for c in outs:
        c.wait()


def back_part(sc, scores, own_gu, got_gu, own_b, got_b, feats, grads, w_all):
    rows, width = feats[0].shape
    wide = 4 * width
    return pl.pallas_call(
        back_kernel,
        out_shape=(
            jax.ShapeDtypeStruct((rows // BLOCK, BLOCK), F32),
            jax.ShapeDtypeStruct((4, rows, width), BF),
            jax.ShapeDtypeStruct((4, 2, 3, EXP, 192, 256), BF),
            jax.ShapeDtypeStruct((4, 2, 3, EXP, 192, 256), BF),
        ),
        in_specs=[SM] + [VM] * 5 + [ANY] * 11,
        out_specs=(VM, ANY, ANY, ANY),
        scratch_shapes=[
            pltpu.VMEM((rows, wide), BF),
            pltpu.VMEM((rows, wide), BF),
            pltpu.VMEM((EXP, 768, wide), BF),
            pltpu.VMEM((rows, 768), BF),
            pltpu.VMEM((EXP, 768, rows), BF),
            pltpu.VMEM((EXP, 384, rows), BF),
            pltpu.VMEM((rows, wide), BF),
            pltpu.VMEM((EXP, 768, wide), BF),
            pltpu.VMEM((EXP, 384, wide), BF),
            pltpu.SemaphoreType.DMA((5,)),
            pltpu.SemaphoreType.DMA((5,)),
            pltpu.SemaphoreType.DMA((32,)),
            pltpu.SemaphoreType.DMA((4,)),
            pltpu.SemaphoreType.DMA((96,)),
        ],
        compiler_params=pltpu.CompilerParams(vmem_limit_bytes=56 << 20),
        cost_estimate=pl.CostEstimate(
            flops=2 * rows * 768 * wide * 4, bytes_accessed=40 << 20, transcendentals=rows * 384
        ),
    )(sc, scores, own_gu, got_gu, own_b, got_b, *feats, *grads, w_all)


def spread_rows(x):
    half = x.shape[0] // 2
    below = lax.ppermute(x, "y", ring(4, 1))
    above = lax.ppermute(x, "y", ring(4, 3))
    return (
        x,
        below,
        above,
        lax.ppermute(below[:half], "y", ring(4, 1)),
        lax.ppermute(above[half:], "y", ring(4, 3)),
    )


def on_device(features, grad_out, scores, counts, w_gate, w_up, w_down):
    rows = features.shape[0]
    xl, y, xh, core = (lax.axis_index(a) for a in ("xl", "y", "xh", "core"))
    sc = jnp.stack(
        [y, xl, counts[0, 0], counts[0, 0] + counts[0, 1], core]
    ).astype(jnp.int32)
    shard = jnp.stack([w_gate, w_up, w_down])
    shard = lax.ppermute(shard, ("xl", "z", "xh"), swap_pairs(0))
    w_all = lax.all_gather(shard, ("z", "xh", "core"), axis=0, tiled=False)
    w_all = w_all.reshape(2, 8, 3, EXP, 192, 256)
    feats = spread_rows(features)
    grads = spread_rows(grad_out)

    own_gu, send_gu = pre_part(sc, feats, w_all, 0, 2)
    got_gu = lax.ppermute(send_gu, "xl", ring(2, 1))
    own_b, send_b = pre_part(sc, grads, w_all, 2, 1)
    got_b = lax.ppermute(send_b, "xl", ring(2, 1))
    sgrad, dx, keep, away = back_part(
        sc, scores.reshape(rows // BLOCK, BLOCK), own_gu, got_gu, own_b, got_b, feats, grads, w_all
    )

    got = lax.ppermute(away, "core", ring(2, 1))
    both = (keep.astype(F32) + got.astype(F32)).astype(BF)
    part = lax.psum_scatter(both, "z", scatter_dimension=0, tiled=False)
    straight = lax.dynamic_index_in_dim(part, xh, 0, False)
    crossed = lax.dynamic_index_in_dim(part, 1 - xh, 0, False)
    straight = lax.ppermute(straight, ("xl", "z", "xh"), swap_pairs(0))
    crossed = lax.ppermute(crossed, ("xl", "z", "xh"), swap_pairs(1))
    weights = straight.astype(F32) + crossed.astype(F32)

    from_below = lax.ppermute(dx[2], "y", ring(4, 1))
    from_above = lax.ppermute(dx[1], "y", ring(4, 3))
    opposite = lax.ppermute(dx[3], "y", ring(4, 2))
    grad_features = (
        (dx[0].astype(F32) + from_below.astype(F32)) + (from_above.astype(F32) + opposite.astype(F32))
    ).astype(BF)

    total = sgrad
    total = total + lax.ppermute(total, "xl", ring(2, 1))
    total = total + lax.ppermute(total, "y", [(i, i ^ 1) for i in range(4)])
    total = total + lax.ppermute(total, "y", [(i, i ^ 2) for i in range(4)])
    return grad_features, total.reshape(rows), weights[0], weights[1], weights[2]


def solution(mesh):
    fine = Mesh(mesh.devices.reshape(2, 4, 4, 2, 2), ("xl", "y", "z", "xh", "core"))
    grp, blk = ("xl", "y"), ("z", "xh", "core")
    weight = P(None, grp, blk)
    return jax.shard_map(
        on_device,
        mesh=fine,
        in_specs=(P(blk, grp), P(blk, grp), P(blk), P(blk, None), weight, weight, weight),
        out_specs=(P(blk, grp), P(blk), weight, weight, weight),
        check_vma=False,
    )
```

```python
import functools

import jax
import jax.numpy as jnp
from jax import lax
from jax.experimental import pallas as pl
from jax.experimental.pallas import tpu as pltpu
from jax.sharding import Mesh
from jax.sharding import PartitionSpec as P

EXP = 2
BLOCK = 128
TILE = 256
HID = 192
COLS = 256
BF = jnp.bfloat16
F32 = jnp.float32
NT = (((1,), (1,)), ((), ()))
OFFS = (0, 3, 1, 2)
SLOTS = ((0, 0), (0, 1), (3, 0), (3, 1), (1, 0), (1, 1), (2, 0), (2, 1))
ANY = pl.BlockSpec(memory_space=pl.ANY)
VM = pl.BlockSpec(memory_space=pltpu.VMEM)
SM = pl.BlockSpec(memory_space=pltpu.SMEM)
Y, XL, FIRST, LIVE, CORE, Z, XH = range(7)


def ring(n, k):
    return [(i, (i + k) % n) for i in range(n)]


def home(xl, z):
    return (xl, z) if z // 2 == xl else (1 - xl, (z + 2) % 4)


def swap_pairs(flip):
    pairs = []
    for xl in range(2):
        for z in range(4):
            for xh in range(2):
                a, b = home(xl, z)
                pairs.append(((xl * 4 + z) * 2 + xh, (a * 4 + b) * 2 + (xh ^ flip)))
    return pairs


def after(x, *others):
    return lax.optimization_barrier((x, *others))[0]


def aligned(i, unit):
    return pl.ds(pl.multiple_of(i * unit, unit), unit)


def y_of(sc, p):
    return lax.rem(sc[Y] + OFFS[p], 4)


def load_rows(sc, pieces, dst, sem):
    rows, width = pieces[0].shape
    half = rows // 2
    copies = []
    for p in range(3):
        at = aligned(y_of(sc, p), width)
        copies.append(pltpu.make_async_copy(pieces[p], dst.at[:, at], sem.at[p]))
    at = aligned(y_of(sc, 3), width)
    copies.append(pltpu.make_async_copy(pieces[3], dst.at[pl.ds(0, half), at], sem.at[3]))
    copies.append(pltpu.make_async_copy(pieces[4], dst.at[pl.ds(half, half), at], sem.at[4]))
    return copies


def load_weight(sc, pair, row, dst, sem, at_sem):
    copies = []
    for c, ref in enumerate(pair):
        core = sc[CORE] if c == 0 else 1 - sc[CORE]
        for i, (step, flip) in enumerate(SLOTS):
            slot = lax.rem(sc[Z] + step, 4)
            xh = 1 - sc[XH] if flip else sc[XH]
            cb = lax.rem(slot, 2) * 4 + xh * 2 + core
            rows = pl.ds(pl.multiple_of(row + lax.div(slot, 2) * HID, 64), HID)
            copies.append(
                pltpu.make_async_copy(
                    ref.at[i], dst.at[:, rows, aligned(cb, COLS)], sem.at[at_sem + c * 8 + i]
                )
            )
    return copies


def expert_of(sc, block):
    return (block * BLOCK >= sc[FIRST]).astype(jnp.int32)


def by_tile(sc, tile, work):
    low, high = expert_of(sc, 2 * tile), expert_of(sc, 2 * tile + 1)
    start = tile * TILE

    @pl.when(low == high)
    def _():
        work(pl.multiple_of(start, TILE), TILE, low)

    @pl.when(low != high)
    def _():
        work(pl.multiple_of(start, BLOCK), BLOCK, low)
        work(pl.multiple_of(start + BLOCK, BLOCK), BLOCK, high)


def start_all(copies):
    for c in copies:
        c.start()
    return copies


def wait_all(copies):
    for c in copies:
        c.wait()


def pre_kernel(sc, x0, x1, x2, x3, x4, w0, w1, own, send, xv, wv, xsem, wsem):
    wait_all(
        start_all(
            load_weight(sc, (w0, w1), 0, wv, wsem, 0) + load_rows(sc, (x0, x1, x2, x3, x4), xv, xsem)
        )
    )

    def work(start, size, expert):
        at = pl.ds(start, size)
        part = lax.dot_general(xv[at, :], wv[expert], NT, preferred_element_type=F32)
        own[at, :] = part
        send[at, :] = part.astype(BF)

    @pl.loop(0, xv.shape[0] // TILE)
    def _(t):
        by_tile(sc, t, work)


def pre_part(sc, pieces, weight):
    rows, width = pieces[0].shape
    wide, n = 4 * width, 2 * HID
    return pl.pallas_call(
        pre_kernel,
        out_shape=(jax.ShapeDtypeStruct((rows, n), F32), jax.ShapeDtypeStruct((rows, n), BF)),
        in_specs=[SM] + [ANY] * 7,
        out_specs=(VM, VM),
        scratch_shapes=[
            pltpu.VMEM((rows, wide), BF),
            pltpu.VMEM((EXP, n, wide), BF),
            pltpu.SemaphoreType.DMA((5,)),
            pltpu.SemaphoreType.DMA((16,)),
        ],
        compiler_params=pltpu.CompilerParams(vmem_limit_bytes=32 << 20),
        cost_estimate=pl.CostEstimate(
            flops=4 * rows * n * wide, bytes_accessed=10 << 20, transcendentals=0
        ),
    )(sc, *pieces, *weight)


def column(row):
    return jnp.transpose(jnp.broadcast_to(row, (BLOCK, BLOCK)))[:, :1]


def transposed_into(dst, sc, b, at, rows, value):
    expert = expert_of(sc, b)
    dst[expert, rows, at] = jnp.transpose(value)
    dst[1 - expert, rows, at] = jnp.zeros((rows.stop - rows.start, BLOCK), value.dtype)


def weight_out(sc, src, row, e, keep, away, w, sem):
    outs = []
    for rel, out in enumerate((keep, away)):
        core = sc[CORE] if rel == 0 else 1 - sc[CORE]
        for h in range(2):
            for zz in range(2):
                for xh in range(2):
                    i = (((w * EXP + e) * 2 + rel) * 2 + h) * 4 + zz * 2 + xh
                    outs.append(
                        pltpu.make_async_copy(
                            src.at[e, pl.ds(row + h * HID, HID), aligned((zz * 2 + xh) * 2 + core, COLS)],
                            out.at[h * 2 + zz, xh, w, e],
                            sem.at[i],
                        )
                    )
    return outs


def down_kernel(
    sc, scores, own_g, got_g, own_u, got_u, g0, g1, g2, g3, g4, keep, away, gv, st, dd, gsem, dsem
):
    rows, width = g0.shape
    gload = start_all(load_rows(sc, (g0, g1, g2, g3, g4), gv, gsem))

    @pl.loop(0, rows // BLOCK)
    def _(b):
        at = aligned(b, BLOCK)
        live = (b * BLOCK < sc[LIVE]).astype(F32)
        gate = own_g[at, :] + got_g[at, :].astype(F32)
        up = own_u[at, :] + got_u[at, :].astype(F32)
        hidden = (gate * jax.nn.sigmoid(gate) * up).astype(BF).astype(F32)
        scaled = (column(scores[pl.ds(b, 1), :]) * live * hidden).astype(BF)
        transposed_into(st, sc, b, at, slice(0, 2 * HID), scaled)

    wait_all(gload)
    outs = []
    for e in range(EXP):
        for n in range(4):
            at = pl.ds(n * width, width)
            dd[e, :, at] = jnp.dot(st[e], gv[:, at], preferred_element_type=F32).astype(BF)
        outs += start_all(weight_out(sc, dd, 0, e, keep, away, 0, dsem))
    wait_all(outs)


def down_part(sc, scores, own_g, got_g, own_u, got_u, grads):
    rows, width = grads[0].shape
    out = jax.ShapeDtypeStruct((4, 2, 1, EXP, HID, COLS), BF)
    return pl.pallas_call(
        down_kernel,
        out_shape=(out, out),
        in_specs=[SM] + [VM] * 5 + [ANY] * 5,
        out_specs=(ANY, ANY),
        scratch_shapes=[
            pltpu.VMEM((rows, 4 * width), BF),
            pltpu.VMEM((EXP, 2 * HID, rows), BF),
            pltpu.VMEM((EXP, 2 * HID, 4 * width), BF),
            pltpu.SemaphoreType.DMA((5,)),
            pltpu.SemaphoreType.DMA((32,)),
        ],
        compiler_params=pltpu.CompilerParams(vmem_limit_bytes=40 << 20),
        cost_estimate=pl.CostEstimate(
            flops=8 * rows * HID * 4 * width, bytes_accessed=14 << 20, transcendentals=rows * 384
        ),
    )(sc, scores, own_g, got_g, own_u, got_u, *grads)


def gate_up_kernel(
    sc, scores, own_g, got_g, own_u, got_u, own_b, got_b, x0, x1, x2, x3, x4,
    sgrad, gu, keep, away, xv, gut, dgu, xsem, dsem,
):
    rows, width = x0.shape
    n = 2 * HID
    xload = start_all(load_rows(sc, (x0, x1, x2, x3, x4), xv, xsem))

    @pl.loop(0, rows // BLOCK)
    def _(b):
        at = aligned(b, BLOCK)
        live = (b * BLOCK < sc[LIVE]).astype(F32)
        gate = own_g[at, :] + got_g[at, :].astype(F32)
        up = own_u[at, :] + got_u[at, :].astype(F32)
        back = own_b[at, :] + got_b[at, :].astype(F32)
        sig = jax.nn.sigmoid(gate)
        act = gate * sig
        hidden = (act * up).astype(BF).astype(F32)
        mine = (lax.broadcasted_iota(jnp.int32, hidden.shape, 1) >= HID).astype(jnp.int32) == sc[XL]
        total = jnp.sum(jnp.where(mine, hidden * back, 0.0), axis=1, keepdims=True) * live
        sgrad[pl.ds(b, 1), :] = jnp.transpose(jnp.broadcast_to(total, (BLOCK, BLOCK)))[:1]
        hid_grad = column(scores[pl.ds(b, 1), :]) * live * back
        gate_grad = (hid_grad * up * sig * (1.0 + gate * (1.0 - sig))).astype(BF)
        up_grad = (hid_grad * act).astype(BF)
        gu[at, :n] = gate_grad
        gu[at, n:] = up_grad
        transposed_into(gut, sc, b, at, slice(0, n), gate_grad)
        transposed_into(gut, sc, b, at, slice(n, 2 * n), up_grad)

    wait_all(xload)
    outs = []
    for e in range(EXP):
        for k in range(4):
            at = pl.ds(k * width, width)
            dgu[e, :, at] = jnp.dot(gut[e], xv[:, at], preferred_element_type=F32).astype(BF)
        for w in range(2):
            outs += start_all(weight_out(sc, dgu, w * n, e, keep, away, w, dsem))
    wait_all(outs)


def gate_up_part(sc, scores, own_g, got_g, own_u, got_u, own_b, got_b, feats):
    rows, width = feats[0].shape
    out = jax.ShapeDtypeStruct((4, 2, 2, EXP, HID, COLS), BF)
    return pl.pallas_call(
        gate_up_kernel,
        out_shape=(
            jax.ShapeDtypeStruct((rows // BLOCK, BLOCK), F32),
            jax.ShapeDtypeStruct((rows, 4 * HID), BF),
            out,
            out,
        ),
        in_specs=[SM] + [VM] * 7 + [ANY] * 5,
        out_specs=(VM, VM, ANY, ANY),
        scratch_shapes=[
            pltpu.VMEM((rows, 4 * width), BF),
            pltpu.VMEM((EXP, 4 * HID, rows), BF),
            pltpu.VMEM((EXP, 4 * HID, 4 * width), BF),
            pltpu.SemaphoreType.DMA((5,)),
            pltpu.SemaphoreType.DMA((64,)),
        ],
        compiler_params=pltpu.CompilerParams(vmem_limit_bytes=48 << 20),
        cost_estimate=pl.CostEstimate(
            flops=16 * rows * HID * 4 * width, bytes_accessed=20 << 20, transcendentals=rows * 384
        ),
    )(sc, scores, own_g, got_g, own_u, got_u, own_b, got_b, *feats)


def rows_kernel(sc, gu, g0, g1, u0, u1, dx, wv, dxv, wsem, osem):
    rows, wide = dxv.shape
    width = wide // 4
    wait_all(
        start_all(
            load_weight(sc, (g0, g1), 0, wv, wsem, 0) + load_weight(sc, (u0, u1), 2 * HID, wv, wsem, 16)
        )
    )

    def work(start, size, expert):
        at = pl.ds(start, size)
        dxv[at, :] = jnp.dot(gu[at, :], wv[expert], preferred_element_type=F32).astype(BF)

    @pl.loop(0, rows // TILE)
    def _(t):
        by_tile(sc, t, work)

    wait_all(
        start_all(
            [
                pltpu.make_async_copy(dxv.at[:, aligned(y_of(sc, p), width)], dx.at[p], osem.at[p])
                for p in range(4)
            ]
        )
    )


def rows_part(sc, gu, w_gate, w_up):
    rows, width = gu.shape[0], 512
    return pl.pallas_call(
        rows_kernel,
        out_shape=jax.ShapeDtypeStruct((4, rows, width), BF),
        in_specs=[SM, VM] + [ANY] * 4,
        out_specs=ANY,
        scratch_shapes=[
            pltpu.VMEM((EXP, 4 * HID, 4 * width), BF),
            pltpu.VMEM((rows, 4 * width), BF),
            pltpu.SemaphoreType.DMA((32,)),
            pltpu.SemaphoreType.DMA((4,)),
        ],
        compiler_params=pltpu.CompilerParams(vmem_limit_bytes=32 << 20),
        cost_estimate=pl.CostEstimate(
            flops=8 * rows * HID * 4 * width, bytes_accessed=14 << 20, transcendentals=0
        ),
    )(sc, gu, *w_gate, *w_up)


def spread_rows(x):
    half = x.shape[0] // 2
    below = lax.ppermute(x, "y", ring(4, 1))
    above = lax.ppermute(x, "y", ring(4, 3))
    return (
        x,
        below,
        above,
        lax.ppermute(below[:half], "y", ring(4, 1)),
        lax.ppermute(above[half:], "y", ring(4, 3)),
    )


def spread_weight(w, *before):
    straight = lax.ppermute(w, ("xl", "z", "xh"), swap_pairs(0))
    crossed = lax.ppermute(w, ("xl", "z", "xh"), swap_pairs(1))
    pair = jnp.stack([straight, crossed])
    if before:
        pair = after(pair, *before)
    below = lax.ppermute(pair, "z", ring(4, 1))
    above = lax.ppermute(pair, "z", ring(4, 3))
    far0 = lax.ppermute(below[:1], "z", ring(4, 1))
    far1 = lax.ppermute(above[1:], "z", ring(4, 3))
    here = jnp.concatenate([pair, below, above, far0, far1])
    return (here, lax.ppermute(here, "core", ring(2, 1))), below


def sum_weights(keep, away, xh):
    got = lax.ppermute(away, "core", ring(2, 1))
    both = (keep.astype(F32) + got.astype(F32)).astype(BF)
    part = lax.psum_scatter(both, "z", scatter_dimension=0, tiled=False)
    straight = lax.dynamic_index_in_dim(part, xh, 0, False)
    crossed = lax.dynamic_index_in_dim(part, 1 - xh, 0, False)
    straight = lax.ppermute(straight, ("xl", "z", "xh"), swap_pairs(0))
    crossed = lax.ppermute(crossed, ("xl", "z", "xh"), swap_pairs(1))
    return straight.astype(F32) + crossed.astype(F32)


def on_device(features, grad_out, scores, counts, w_gate, w_up, w_down):
    rows = features.shape[0]
    xh = lax.axis_index("xh")
    y, xl, core, z = (lax.axis_index(a) for a in ("y", "xl", "core", "z"))
    sc = jnp.stack([y, xl, counts[0, 0], counts[0, 0] + counts[0, 1], core, z, xh]).astype(jnp.int32)
    scores = scores.reshape(rows // BLOCK, BLOCK)

    feats = spread_rows(features)
    gate_all, gate_step = spread_weight(w_gate)
    up_all, up_step = spread_weight(w_up, gate_step)
    down_all, _ = spread_weight(w_down, up_step)
    grads = spread_rows(after(grad_out, feats[3], feats[4]))

    own_g, send_g = pre_part(sc, feats, gate_all)
    got_g = lax.ppermute(send_g, "xl", ring(2, 1))
    own_u, send_u = pre_part(sc, feats, up_all)
    got_u = lax.ppermute(after(send_u, got_g), "xl", ring(2, 1))
    own_b, send_b = pre_part(sc, grads, down_all)
    got_b = lax.ppermute(after(send_b, got_u), "xl", ring(2, 1))

    down = down_part(sc, scores, own_g, got_g, own_u, got_u, grads)
    grad_down = sum_weights(*down, xh)
    sgrad, gu, keep, away = gate_up_part(
        sc, scores, own_g, got_g, own_u, got_u, own_b, got_b, feats
    )
    grad_gate_up = sum_weights(keep, away, xh)

    dx = rows_part(sc, gu, gate_all, up_all)
    from_below = lax.ppermute(dx[2], "y", ring(4, 1))
    from_above = lax.ppermute(dx[1], "y", ring(4, 3))
    opposite = lax.ppermute(dx[3], "y", ring(4, 2))
    grad_features = (
        (dx[0].astype(F32) + from_below.astype(F32)) + (from_above.astype(F32) + opposite.astype(F32))
    ).astype(BF)

    total = sgrad
    total = total + lax.ppermute(total, "xl", ring(2, 1))
    total = total + lax.ppermute(total, "y", [(i, i ^ 1) for i in range(4)])
    total = total + lax.ppermute(total, "y", [(i, i ^ 2) for i in range(4)])
    return grad_features, total.reshape(rows), grad_gate_up[0], grad_gate_up[1], grad_down[0]


def solution(mesh):
    fine = Mesh(mesh.devices.reshape(2, 4, 4, 2, 2), ("xl", "y", "z", "xh", "core"))
    grp, blk = ("xl", "y"), ("z", "xh", "core")
    weight = P(None, grp, blk)
    return jax.shard_map(
        on_device,
        mesh=fine,
        in_specs=(P(blk, grp), P(blk, grp), P(blk), P(blk, None), weight, weight, weight),
        out_specs=(P(blk, grp), P(blk), weight, weight, weight),
        check_vma=False,
    )
```

```python
import functools

import jax
import jax.numpy as jnp
from jax import lax
from jax.experimental import pallas as pl
from jax.experimental.pallas import tpu as pltpu
from jax.sharding import Mesh
from jax.sharding import PartitionSpec as P

EXP = 2
BLOCK = 128
TILE = 256
HID = 192
COLS = 256
BF = jnp.bfloat16
F32 = jnp.float32
NT = (((1,), (1,)), ((), ()))
OFFS = (0, 3, 1, 2)
ANY = pl.BlockSpec(memory_space=pl.ANY)
VM = pl.BlockSpec(memory_space=pltpu.VMEM)
SM = pl.BlockSpec(memory_space=pltpu.SMEM)
Y, XL, FIRST, LIVE, CORE, XH = range(6)


def ring(n, k):
    return [(i, (i + k) % n) for i in range(n)]


def home(xl, z):
    return (xl, z) if z // 2 == xl else (1 - xl, (z + 2) % 4)


def swap_pairs(flip):
    pairs = []
    for xl in range(2):
        for z in range(4):
            for xh in range(2):
                a, b = home(xl, z)
                pairs.append(((xl * 4 + z) * 2 + xh, (a * 4 + b) * 2 + (xh ^ flip)))
    return pairs


def after(x, *others):
    return lax.optimization_barrier((x, *others))[0]


def aligned(i, unit):
    return pl.ds(pl.multiple_of(i * unit, unit), unit)


def y_of(sc, p):
    return lax.rem(sc[Y] + OFFS[p], 4)


def load_rows(sc, pieces, dst, sem):
    rows, width = pieces[0].shape
    half = rows // 2
    copies = []
    for i, piece in enumerate(pieces):
        where = aligned(y_of(sc, (i + 1) // 2), width)
        some = pl.ds(0, rows) if i == 0 else pl.ds((i - 1) % 2 * half, half)
        copies.append(pltpu.make_async_copy(piece, dst.at[some, where], sem.at[i]))
    return copies


def load_weight(sc, pair, w, row, dst, sem, at_sem):
    copies = []
    for c, ref in enumerate(pair):
        core = sc[CORE] if c == 0 else 1 - sc[CORE]
        for slot in range(4):
            for flip in range(2):
                xh = 1 - sc[XH] if flip else sc[XH]
                cb = slot % 2 * 4 + xh * 2 + core
                copies.append(
                    pltpu.make_async_copy(
                        ref.at[slot, flip, w],
                        dst.at[:, pl.ds(row + slot // 2 * HID, HID), aligned(cb, COLS)],
                        sem.at[at_sem + c * 8 + slot * 2 + flip],
                    )
                )
    return copies


def expert_of(sc, block):
    return (block * BLOCK >= sc[FIRST]).astype(jnp.int32)


def by_tile(sc, tile, work):
    low, high = expert_of(sc, 2 * tile), expert_of(sc, 2 * tile + 1)
    start = tile * TILE

    @pl.when(low == high)
    def _():
        work(pl.multiple_of(start, TILE), TILE, low)

    @pl.when(low != high)
    def _():
        work(pl.multiple_of(start, BLOCK), BLOCK, low)
        work(pl.multiple_of(start + BLOCK, BLOCK), BLOCK, high)


def start_all(copies):
    for c in copies:
        c.start()
    return copies


def wait_all(copies):
    for c in copies:
        c.wait()


def pre_kernel(w, sc, x0, x1, x2, x3, x4, x5, x6, w0, w1, own, send, xv, wv, xsem, wsem):
    wait_all(
        start_all(
            load_weight(sc, (w0, w1), w, 0, wv, wsem, 0) + load_rows(sc, (x0, x1, x2, x3, x4, x5, x6), xv, xsem)
        )
    )

    def work(start, size, expert):
        at = pl.ds(start, size)
        part = lax.dot_general(xv[at, :], wv[expert], NT, preferred_element_type=F32)
        own[at, :] = part
        send[at, :] = part.astype(BF)

    @pl.loop(0, xv.shape[0] // TILE)
    def _(t):
        by_tile(sc, t, work)


def pre_part(sc, pieces, weight, w):
    rows, width = pieces[0].shape
    wide, n = 4 * width, 2 * HID
    return pl.pallas_call(
        functools.partial(pre_kernel, w),
        out_shape=(jax.ShapeDtypeStruct((rows, n), F32), jax.ShapeDtypeStruct((rows, n), BF)),
        in_specs=[SM] + [ANY] * 9,
        out_specs=(VM, VM),
        scratch_shapes=[
            pltpu.VMEM((rows, wide), BF),
            pltpu.VMEM((EXP, n, wide), BF),
            pltpu.SemaphoreType.DMA((7,)),
            pltpu.SemaphoreType.DMA((16,)),
        ],
        compiler_params=pltpu.CompilerParams(vmem_limit_bytes=32 << 20),
        cost_estimate=pl.CostEstimate(
            flops=4 * rows * n * wide, bytes_accessed=10 << 20, transcendentals=0
        ),
    )(sc, *pieces, *weight)


def column(row):
    return jnp.transpose(jnp.broadcast_to(row, (BLOCK, BLOCK)))[:, :1]


def transposed_into(dst, sc, b, at, rows, value):
    expert = expert_of(sc, b)
    dst[expert, rows, at] = jnp.transpose(value)
    dst[1 - expert, rows, at] = jnp.zeros((rows.stop - rows.start, BLOCK), value.dtype)


def weight_out(sc, src, row, e, keep, away, w, sem):
    outs = []
    for rel, out in enumerate((keep, away)):
        core = sc[CORE] if rel == 0 else 1 - sc[CORE]
        for h in range(2):
            for zz in range(2):
                for xh in range(2):
                    i = (((w * EXP + e) * 2 + rel) * 2 + h) * 4 + zz * 2 + xh
                    outs.append(
                        pltpu.make_async_copy(
                            src.at[e, pl.ds(row + h * HID, HID), aligned((zz * 2 + xh) * 2 + core, COLS)],
                            out.at[h * 2 + zz, xh, w, e],
                            sem.at[i],
                        )
                    )
    return outs


def down_kernel(
    sc, scores, own_g, got_g, own_u, got_u, g0, g1, g2, g3, g4, g5, g6, keep, away, gv, st, dd, gsem, dsem
):
    rows, width = g0.shape
    gload = start_all(load_rows(sc, (g0, g1, g2, g3, g4, g5, g6), gv, gsem))

    @pl.loop(0, rows // BLOCK)
    def _(b):
        at = aligned(b, BLOCK)
        live = (b * BLOCK < sc[LIVE]).astype(F32)
        gate = own_g[at, :] + got_g[at, :].astype(F32)
        up = own_u[at, :] + got_u[at, :].astype(F32)
        hidden = (gate * jax.nn.sigmoid(gate) * up).astype(BF).astype(F32)
        scaled = (column(scores[pl.ds(b, 1), :]) * live * hidden).astype(BF)
        transposed_into(st, sc, b, at, slice(0, 2 * HID), scaled)

    wait_all(gload)
    outs = []
    for e in range(EXP):
        for n in range(4):
            at = pl.ds(n * width, width)
            dd[e, :, at] = jnp.dot(st[e], gv[:, at], preferred_element_type=F32).astype(BF)
        outs += start_all(weight_out(sc, dd, 0, e, keep, away, 0, dsem))
    wait_all(outs)


def down_part(sc, scores, own_g, got_g, own_u, got_u, grads):
    rows, width = grads[0].shape
    out = jax.ShapeDtypeStruct((4, 2, 1, EXP, HID, COLS), BF)
    return pl.pallas_call(
        down_kernel,
        out_shape=(out, out),
        in_specs=[SM] + [VM] * 5 + [ANY] * 7,
        out_specs=(ANY, ANY),
        scratch_shapes=[
            pltpu.VMEM((rows, 4 * width), BF),
            pltpu.VMEM((EXP, 2 * HID, rows), BF),
            pltpu.VMEM((EXP, 2 * HID, 4 * width), BF),
            pltpu.SemaphoreType.DMA((7,)),
            pltpu.SemaphoreType.DMA((32,)),
        ],
        compiler_params=pltpu.CompilerParams(vmem_limit_bytes=40 << 20),
        cost_estimate=pl.CostEstimate(
            flops=8 * rows * HID * 4 * width, bytes_accessed=14 << 20, transcendentals=rows * 384
        ),
    )(sc, scores, own_g, got_g, own_u, got_u, *grads)


def gate_up_kernel(
    sc, scores, own_g, got_g, own_u, got_u, own_b, got_b, x0, x1, x2, x3, x4, x5, x6,
    sgrad, gu, keep, away, xv, gut, dgu, xsem, dsem,
):
    rows, width = x0.shape
    n = 2 * HID
    xload = start_all(load_rows(sc, (x0, x1, x2, x3, x4, x5, x6), xv, xsem))

    @pl.loop(0, rows // BLOCK)
    def _(b):
        at = aligned(b, BLOCK)
        live = (b * BLOCK < sc[LIVE]).astype(F32)
        gate = own_g[at, :] + got_g[at, :].astype(F32)
        up = own_u[at, :] + got_u[at, :].astype(F32)
        back = own_b[at, :] + got_b[at, :].astype(F32)
        sig = jax.nn.sigmoid(gate)
        act = gate * sig
        hidden = (act * up).astype(BF).astype(F32)
        mine = (lax.broadcasted_iota(jnp.int32, hidden.shape, 1) >= HID).astype(jnp.int32) == sc[XL]
        total = jnp.sum(jnp.where(mine, hidden * back, 0.0), axis=1, keepdims=True) * live
        sgrad[pl.ds(b, 1), :] = jnp.transpose(jnp.broadcast_to(total, (BLOCK, BLOCK)))[:1]
        hid_grad = column(scores[pl.ds(b, 1), :]) * live * back
        gate_grad = (hid_grad * up * sig * (1.0 + gate * (1.0 - sig))).astype(BF)
        up_grad = (hid_grad * act).astype(BF)
        gu[at, :n] = gate_grad
        gu[at, n:] = up_grad
        transposed_into(gut, sc, b, at, slice(0, n), gate_grad)
        transposed_into(gut, sc, b, at, slice(n, 2 * n), up_grad)

    wait_all(xload)
    outs = []
    for e in range(EXP):
        for k in range(4):
            at = pl.ds(k * width, width)
            dgu[e, :, at] = jnp.dot(gut[e], xv[:, at], preferred_element_type=F32).astype(BF)
        for w in range(2):
            outs += start_all(weight_out(sc, dgu, w * n, e, keep, away, w, dsem))
    wait_all(outs)


def gate_up_part(sc, scores, own_g, got_g, own_u, got_u, own_b, got_b, feats):
    rows, width = feats[0].shape
    out = jax.ShapeDtypeStruct((4, 2, 2, EXP, HID, COLS), BF)
    return pl.pallas_call(
        gate_up_kernel,
        out_shape=(
            jax.ShapeDtypeStruct((rows // BLOCK, BLOCK), F32),
            jax.ShapeDtypeStruct((rows, 4 * HID), BF),
            out,
            out,
        ),
        in_specs=[SM] + [VM] * 7 + [ANY] * 7,
        out_specs=(VM, VM, ANY, ANY),
        scratch_shapes=[
            pltpu.VMEM((rows, 4 * width), BF),
            pltpu.VMEM((EXP, 4 * HID, rows), BF),
            pltpu.VMEM((EXP, 4 * HID, 4 * width), BF),
            pltpu.SemaphoreType.DMA((7,)),
            pltpu.SemaphoreType.DMA((64,)),
        ],
        compiler_params=pltpu.CompilerParams(vmem_limit_bytes=48 << 20),
        cost_estimate=pl.CostEstimate(
            flops=16 * rows * HID * 4 * width, bytes_accessed=20 << 20, transcendentals=rows * 384
        ),
    )(sc, scores, own_g, got_g, own_u, got_u, own_b, got_b, *feats)


def rows_kernel(sc, gu, w0, w1, d0, d1, d2, d3, wv, dxv, wsem, osem):
    rows, wide = dxv.shape
    width = wide // 4
    wait_all(
        start_all(
            load_weight(sc, (w0, w1), 0, 0, wv, wsem, 0) + load_weight(sc, (w0, w1), 1, 2 * HID, wv, wsem, 16)
        )
    )

    def work(start, size, expert):
        at = pl.ds(start, size)
        dxv[at, :] = jnp.dot(gu[at, :], wv[expert], preferred_element_type=F32).astype(BF)

    @pl.loop(0, rows // TILE)
    def _(t):
        by_tile(sc, t, work)

    wait_all(
        start_all(
            [
                pltpu.make_async_copy(dxv.at[:, aligned(y_of(sc, p), width)], d, osem.at[p])
                for p, d in enumerate((d0, d1, d2, d3))
            ]
        )
    )


def rows_part(sc, gu, weight):
    rows, width = gu.shape[0], 512
    return pl.pallas_call(
        rows_kernel,
        out_shape=(jax.ShapeDtypeStruct((rows, width), BF),) * 4,
        in_specs=[SM, VM] + [ANY] * 2,
        out_specs=(ANY,) * 4,
        scratch_shapes=[
            pltpu.VMEM((EXP, 4 * HID, 4 * width), BF),
            pltpu.VMEM((rows, 4 * width), BF),
            pltpu.SemaphoreType.DMA((32,)),
            pltpu.SemaphoreType.DMA((4,)),
        ],
        compiler_params=pltpu.CompilerParams(vmem_limit_bytes=32 << 20),
        cost_estimate=pl.CostEstimate(
            flops=8 * rows * HID * 4 * width, bytes_accessed=14 << 20, transcendentals=0
        ),
    )(sc, gu, *weight)


def halves_over(x):
    half = x.shape[0] // 2
    near = [lax.ppermute(x[:half], "y", ring(4, k)) for k in (1, 3)]
    rest = [lax.ppermute(x[half:], "y", ring(4, k)) for k in (1, 3)]
    return x, near[0], rest[0], near[1], rest[1]


def opposite_over(pieces):
    return lax.ppermute(pieces[1], "y", ring(4, 1)), lax.ppermute(pieces[4], "y", ring(4, 3))


def plane_pair(w):
    straight = lax.ppermute(w, ("xl", "z", "xh"), swap_pairs(0))
    crossed = lax.ppermute(w, ("xl", "z", "xh"), swap_pairs(1))
    return jnp.stack([straight, crossed])


def spread_pair(pair, *before):
    here = after(lax.all_gather(pair, "z", axis=0, tiled=False), *before)
    return here, lax.ppermute(here, "core", ring(2, 1))


def over_cores(keep, away):
    got = lax.ppermute(away, "core", ring(2, 1))
    return (keep.astype(F32) + got.astype(F32)).astype(BF)


def over_chips(part, xh):
    straight = lax.dynamic_index_in_dim(part, xh, 0, False)
    crossed = lax.dynamic_index_in_dim(part, 1 - xh, 0, False)
    straight = lax.ppermute(straight, ("xl", "z", "xh"), swap_pairs(0))
    crossed = lax.ppermute(crossed, ("xl", "z", "xh"), swap_pairs(1))
    return straight.astype(F32) + crossed.astype(F32)


def scatter_z(both):
    return lax.psum_scatter(both, "z", scatter_dimension=0, tiled=False)


def on_device(features, grad_out, scores, counts, w_gate, w_up, w_down):
    rows = features.shape[0]
    y, xl, core, xh = (lax.axis_index(a) for a in ("y", "xl", "core", "xh"))
    sc = jnp.stack([y, xl, counts[0, 0], counts[0, 0] + counts[0, 1], core, xh]).astype(jnp.int32)
    scores = scores.reshape(rows // BLOCK, BLOCK)

    feats = halves_over(features)
    feats += opposite_over(feats)
    pair_gu = after(plane_pair(jnp.stack([w_gate, w_up])), feats[1], feats[3])
    pair_d = plane_pair(after(w_down, pair_gu)[None])
    grads = halves_over(after(grad_out, feats[5], feats[6]))
    w_gu = spread_pair(pair_gu, feats[2], feats[4], pair_d, grads[1], grads[3])
    w_d = spread_pair(pair_d)

    own_g, send_g = pre_part(sc, feats, w_gu, 0)
    got_g = lax.ppermute(send_g, "xl", ring(2, 1))
    own_u, send_u = pre_part(after(sc, send_g, grads[2], grads[4]), feats, w_gu, 1)
    got_u = lax.ppermute(after(send_u, got_g), "xl", ring(2, 1))
    grads += opposite_over(after(grads, send_g))
    own_b, send_b = pre_part(sc, grads, w_d, 0)
    got_b = lax.ppermute(after(send_b, got_u), "xl", ring(2, 1))

    both_d = over_cores(
        *down_part(after(sc, send_b), scores, own_g, got_g, own_u, got_u, grads)
    )
    part_d = scatter_z(both_d)
    total, gu, keep, away = gate_up_part(
        sc, scores, own_g, got_g, own_u, got_u, own_b, after(got_b, both_d), feats
    )
    both_gu = over_cores(keep, away)
    part_gu = scatter_z(both_gu)
    total = total + lax.ppermute(total, "y", [(i, i ^ 1) for i in range(4)])

    dx = rows_part(sc, after(gu, total, both_gu), w_gu)
    total = total + lax.ppermute(total, "y", [(i, i ^ 2) for i in range(4)])
    dx, _ = lax.optimization_barrier((dx, total))
    total = total + lax.ppermute(total, "xl", ring(2, 1))
    from_below = lax.ppermute(dx[2], "y", ring(4, 1))
    from_above = lax.ppermute(dx[1], "y", ring(4, 3))
    opposite = lax.ppermute(dx[3], "y", ring(4, 2))
    grad_features = (
        (dx[0].astype(F32) + from_below.astype(F32)) + (from_above.astype(F32) + opposite.astype(F32))
    ).astype(BF)

    grad_down = over_chips(part_d, xh)
    grad_gu = over_chips(after(part_gu, grad_down, total), xh)
    return grad_features, total.reshape(rows), grad_gu[0], grad_gu[1], grad_down[0]


def solution(mesh):
    fine = Mesh(mesh.devices.reshape(2, 4, 4, 2, 2), ("xl", "y", "z", "xh", "core"))
    grp, blk = ("xl", "y"), ("z", "xh", "core")
    weight = P(None, grp, blk)
    return jax.shard_map(
        on_device,
        mesh=fine,
        in_specs=(P(blk, grp), P(blk, grp), P(blk), P(blk, None), weight, weight, weight),
        out_specs=(P(blk, grp), P(blk), weight, weight, weight),
        check_vma=False,
    )
```

```python
import jax
import jax.numpy as jnp
from jax import lax
from jax.experimental import pallas as pl
from jax.experimental.pallas import tpu as pltpu
from jax.sharding import Mesh
from jax.sharding import PartitionSpec as P

EXP = 2
BLOCK = 128
TILE = 256
HID = 192
VMEM = 28 << 20
COLS = 256
BF = jnp.bfloat16
F32 = jnp.float32
NT = (((1,), (1,)), ((), ()))
OFFS = (0, 3, 1, 2)
ANY = pl.BlockSpec(memory_space=pl.ANY)
VM = pl.BlockSpec(memory_space=pltpu.VMEM)
SM = pl.BlockSpec(memory_space=pltpu.SMEM)
Y, XL, FIRST, LIVE, CORE, XH = range(6)


def ring(n, k):
    return [(i, (i + k) % n) for i in range(n)]


def home(xl, z):
    return (xl, z) if z // 2 == xl else (1 - xl, (z + 2) % 4)


def swap_pairs(flip):
    pairs = []
    for xl in range(2):
        for z in range(4):
            for xh in range(2):
                a, b = home(xl, z)
                pairs.append(((xl * 4 + z) * 2 + xh, (a * 4 + b) * 2 + (xh ^ flip)))
    return pairs


def after(x, *others):
    return lax.optimization_barrier((x, *others))[0]


def aligned(i, unit):
    return pl.ds(pl.multiple_of(i * unit, unit), unit)


def y_of(sc, p):
    return lax.rem(sc[Y] + OFFS[p], 4)


def load_rows(sc, pieces, dst, sem):
    rows, width = pieces[0].shape
    half = rows // 2
    copies = []
    for i, piece in enumerate(pieces):
        where = aligned(y_of(sc, (i + 1) // 2), width)
        some = pl.ds(0, rows) if i == 0 else pl.ds((i - 1) % 2 * half, half)
        copies.append(pltpu.make_async_copy(piece, dst.at[some, where], sem.at[i]))
    return copies


def load_weight(sc, pair, row, dst, sem, at_sem):
    copies = []
    for c, ref in enumerate(pair):
        core = sc[CORE] if c == 0 else 1 - sc[CORE]
        for slot in range(4):
            for flip in range(2):
                xh = 1 - sc[XH] if flip else sc[XH]
                cb = slot % 2 * 4 + xh * 2 + core
                copies.append(
                    pltpu.make_async_copy(
                        ref.at[slot, flip],
                        dst.at[:, pl.ds(row + slot // 2 * HID, HID), aligned(cb, COLS)],
                        sem.at[at_sem + c * 8 + slot * 2 + flip],
                    )
                )
    return copies


def expert_of(sc, block):
    return (block * BLOCK >= sc[FIRST]).astype(jnp.int32)


def by_tile(sc, tile, work):
    low, high = expert_of(sc, 2 * tile), expert_of(sc, 2 * tile + 1)
    start = tile * TILE

    @pl.when(low == high)
    def _():
        work(pl.multiple_of(start, TILE), TILE, low)

    @pl.when(low != high)
    def _():
        work(pl.multiple_of(start, BLOCK), BLOCK, low)
        work(pl.multiple_of(start + BLOCK, BLOCK), BLOCK, high)


def start_all(copies):
    for c in copies:
        c.start()
    return copies


def wait_all(copies):
    for c in copies:
        c.wait()


def pre_kernel(sc, x0, x1, x2, x3, x4, x5, x6, w0, w1, own, send, xv, wv, xsem, wsem):
    wait_all(
        start_all(
            load_weight(sc, (w0, w1), 0, wv, wsem, 0) + load_rows(sc, (x0, x1, x2, x3, x4, x5, x6), xv, xsem)
        )
    )

    def work(start, size, expert):
        at = pl.ds(start, size)
        part = lax.dot_general(xv[at, :], wv[expert], NT, preferred_element_type=F32)
        own[at, :] = part
        send[at, :] = part.astype(BF)

    @pl.loop(0, xv.shape[0] // TILE)
    def _(t):
        by_tile(sc, t, work)


def pre_part(sc, pieces, weight):
    rows, width = pieces[0].shape
    wide, n = 4 * width, 2 * HID
    return pl.pallas_call(
        pre_kernel,
        out_shape=(jax.ShapeDtypeStruct((rows, n), F32), jax.ShapeDtypeStruct((rows, n), BF)),
        in_specs=[SM] + [ANY] * 9,
        out_specs=(VM, VM),
        scratch_shapes=[
            pltpu.VMEM((rows, wide), BF),
            pltpu.VMEM((EXP, n, wide), BF),
            pltpu.SemaphoreType.DMA((7,)),
            pltpu.SemaphoreType.DMA((16,)),
        ],
        compiler_params=pltpu.CompilerParams(vmem_limit_bytes=VMEM),
        cost_estimate=pl.CostEstimate(
            flops=4 * rows * n * wide, bytes_accessed=10 << 20, transcendentals=0
        ),
    )(sc, *pieces, *weight)


def column(row):
    return jnp.transpose(jnp.broadcast_to(row, (BLOCK, BLOCK)))[:, :1]


def transposed_into(dst, sc, b, at, rows, value):
    expert = expert_of(sc, b)
    dst[expert, rows, at] = jnp.transpose(value)
    dst[1 - expert, rows, at] = jnp.zeros((rows.stop - rows.start, BLOCK), value.dtype)


def weight_out(sc, src, row, e, keep, away, w, sem):
    outs = []
    for rel, out in enumerate((keep, away)):
        core = sc[CORE] if rel == 0 else 1 - sc[CORE]
        for h in range(2):
            for zz in range(2):
                for xh in range(2):
                    i = (((w * EXP + e) * 2 + rel) * 2 + h) * 4 + zz * 2 + xh
                    outs.append(
                        pltpu.make_async_copy(
                            src.at[e, pl.ds(row + h * HID, HID), aligned((zz * 2 + xh) * 2 + core, COLS)],
                            out.at[h * 2 + zz, xh, w, e],
                            sem.at[i],
                        )
                    )
    return outs


def down_kernel(
    sc, scores, own_g, got_g, own_u, got_u, g0, g1, g2, g3, g4, g5, g6, keep, away, gv, st, dd, gsem, dsem
):
    rows, width = g0.shape
    gload = start_all(load_rows(sc, (g0, g1, g2, g3, g4, g5, g6), gv, gsem))

    @pl.loop(0, rows // BLOCK)
    def _(b):
        at = aligned(b, BLOCK)
        live = (b * BLOCK < sc[LIVE]).astype(F32)
        gate = own_g[at, :] + got_g[at, :].astype(F32)
        up = own_u[at, :] + got_u[at, :].astype(F32)
        hidden = (gate * jax.nn.sigmoid(gate) * up).astype(BF).astype(F32)
        scaled = (column(scores[pl.ds(b, 1), :]) * live * hidden).astype(BF)
        transposed_into(st, sc, b, at, slice(0, 2 * HID), scaled)

    wait_all(gload)
    outs = []
    for e in range(EXP):
        for n in range(4):
            at = pl.ds(n * width, width)
            dd[e, :, at] = jnp.dot(st[e], gv[:, at], preferred_element_type=F32).astype(BF)
        outs += start_all(weight_out(sc, dd, 0, e, keep, away, 0, dsem))
    wait_all(outs)


def down_part(sc, scores, own_g, got_g, own_u, got_u, grads):
    rows, width = grads[0].shape
    out = jax.ShapeDtypeStruct((4, 2, 1, EXP, HID, COLS), BF)
    return pl.pallas_call(
        down_kernel,
        out_shape=(out, out),
        in_specs=[SM] + [VM] * 5 + [ANY] * 7,
        out_specs=(ANY, ANY),
        scratch_shapes=[
            pltpu.VMEM((rows, 4 * width), BF),
            pltpu.VMEM((EXP, 2 * HID, rows), BF),
            pltpu.VMEM((EXP, 2 * HID, 4 * width), BF),
            pltpu.SemaphoreType.DMA((7,)),
            pltpu.SemaphoreType.DMA((32,)),
        ],
        compiler_params=pltpu.CompilerParams(vmem_limit_bytes=VMEM),
        cost_estimate=pl.CostEstimate(
            flops=8 * rows * HID * 4 * width, bytes_accessed=14 << 20, transcendentals=rows * 384
        ),
    )(sc, scores, own_g, got_g, own_u, got_u, *grads)


def gate_up_kernel(
    sc, scores, own_g, got_g, own_u, got_u, own_b, got_b, x0, x1, x2, x3, x4, x5, x6,
    sgrad, gu, keep, away, xv, gut, dgu, xsem, dsem,
):
    rows, width = x0.shape
    n = 2 * HID
    xload = start_all(load_rows(sc, (x0, x1, x2, x3, x4, x5, x6), xv, xsem))

    @pl.loop(0, rows // BLOCK)
    def _(b):
        at = aligned(b, BLOCK)
        live = (b * BLOCK < sc[LIVE]).astype(F32)
        gate = own_g[at, :] + got_g[at, :].astype(F32)
        up = own_u[at, :] + got_u[at, :].astype(F32)
        back = own_b[at, :] + got_b[at, :].astype(F32)
        sig = jax.nn.sigmoid(gate)
        act = gate * sig
        hidden = (act * up).astype(BF).astype(F32)
        mine = (lax.broadcasted_iota(jnp.int32, hidden.shape, 1) >= HID).astype(jnp.int32) == sc[XL]
        total = jnp.sum(jnp.where(mine, hidden * back, 0.0), axis=1, keepdims=True) * live
        sgrad[pl.ds(b, 1), :] = jnp.transpose(jnp.broadcast_to(total, (BLOCK, BLOCK)))[:1]
        hid_grad = column(scores[pl.ds(b, 1), :]) * live * back
        gate_grad = (hid_grad * up * sig * (1.0 + gate * (1.0 - sig))).astype(BF)
        up_grad = (hid_grad * act).astype(BF)
        gu[at, :n] = gate_grad
        gu[at, n:] = up_grad
        transposed_into(gut, sc, b, at, slice(0, n), gate_grad)
        transposed_into(gut, sc, b, at, slice(n, 2 * n), up_grad)

    wait_all(xload)
    outs = []
    for e in range(EXP):
        for k in range(4):
            at = pl.ds(k * width, width)
            dgu[e, :, at] = jnp.dot(gut[e], xv[:, at], preferred_element_type=F32).astype(BF)
        for w in range(2):
            outs += start_all(weight_out(sc, dgu, w * n, e, keep, away, w, dsem))
    wait_all(outs)


def gate_up_part(sc, scores, own_g, got_g, own_u, got_u, own_b, got_b, feats):
    rows, width = feats[0].shape
    out = jax.ShapeDtypeStruct((4, 2, 2, EXP, HID, COLS), BF)
    return pl.pallas_call(
        gate_up_kernel,
        out_shape=(
            jax.ShapeDtypeStruct((rows // BLOCK, BLOCK), F32),
            jax.ShapeDtypeStruct((rows, 4 * HID), BF),
            out,
            out,
        ),
        in_specs=[SM] + [VM] * 7 + [ANY] * 7,
        out_specs=(VM, VM, ANY, ANY),
        scratch_shapes=[
            pltpu.VMEM((rows, 4 * width), BF),
            pltpu.VMEM((EXP, 4 * HID, rows), BF),
            pltpu.VMEM((EXP, 4 * HID, 4 * width), BF),
            pltpu.SemaphoreType.DMA((7,)),
            pltpu.SemaphoreType.DMA((64,)),
        ],
        compiler_params=pltpu.CompilerParams(vmem_limit_bytes=VMEM),
        cost_estimate=pl.CostEstimate(
            flops=16 * rows * HID * 4 * width, bytes_accessed=20 << 20, transcendentals=rows * 384
        ),
    )(sc, scores, own_g, got_g, own_u, got_u, own_b, got_b, *feats)


def rows_kernel(sc, gu, g0, g1, u0, u1, d0, d1, d2, d3, wv, dxv, wsem, osem):
    rows, wide = dxv.shape
    width = wide // 4
    wait_all(
        start_all(
            load_weight(sc, (g0, g1), 0, wv, wsem, 0) + load_weight(sc, (u0, u1), 2 * HID, wv, wsem, 16)
        )
    )

    def work(start, size, expert):
        at = pl.ds(start, size)
        dxv[at, :] = jnp.dot(gu[at, :], wv[expert], preferred_element_type=F32).astype(BF)

    @pl.loop(0, rows // TILE)
    def _(t):
        by_tile(sc, t, work)

    wait_all(
        start_all(
            [
                pltpu.make_async_copy(dxv.at[:, aligned(y_of(sc, p), width)], d, osem.at[p])
                for p, d in enumerate((d0, d1, d2, d3))
            ]
        )
    )


def rows_part(sc, gu, w_gate, w_up):
    rows, width = gu.shape[0], 512
    return pl.pallas_call(
        rows_kernel,
        out_shape=(jax.ShapeDtypeStruct((rows, width), BF),) * 4,
        in_specs=[SM, VM] + [ANY] * 4,
        out_specs=(ANY,) * 4,
        scratch_shapes=[
            pltpu.VMEM((EXP, 4 * HID, 4 * width), BF),
            pltpu.VMEM((rows, 4 * width), BF),
            pltpu.SemaphoreType.DMA((32,)),
            pltpu.SemaphoreType.DMA((4,)),
        ],
        compiler_params=pltpu.CompilerParams(vmem_limit_bytes=VMEM),
        cost_estimate=pl.CostEstimate(
            flops=8 * rows * HID * 4 * width, bytes_accessed=14 << 20, transcendentals=0
        ),
    )(sc, gu, *w_gate, *w_up)


def halves_over(x):
    half = x.shape[0] // 2
    near = [lax.ppermute(x[:half], "y", ring(4, k)) for k in (1, 3)]
    rest = [lax.ppermute(x[half:], "y", ring(4, k)) for k in (1, 3)]
    return x, near[0], rest[0], near[1], rest[1]


def opposite_over(pieces):
    return lax.ppermute(pieces[1], "y", ring(4, 1)), lax.ppermute(pieces[4], "y", ring(4, 3))


def to_plane(w):
    return (
        lax.ppermute(w, ("xl", "z", "xh"), swap_pairs(0)),
        lax.ppermute(w, ("xl", "z", "xh"), swap_pairs(1)),
    )


def spread_pair(pair, *before):
    here = after(lax.all_gather(pair, "z", axis=0, tiled=False), *before)
    return here, lax.ppermute(here, "core", ring(2, 1))


def over_cores(keep, got):
    return (keep.astype(F32) + got.astype(F32)).astype(BF)


def over_chips(part, xh):
    straight = lax.dynamic_index_in_dim(part, xh, 0, False)
    crossed = lax.dynamic_index_in_dim(part, 1 - xh, 0, False)
    straight = lax.ppermute(straight, ("xl", "z", "xh"), swap_pairs(0))
    crossed = lax.ppermute(crossed, ("xl", "z", "xh"), swap_pairs(1))
    return straight.astype(F32) + crossed.astype(F32)


def scatter_z(both):
    return lax.psum_scatter(both, "z", scatter_dimension=0, tiled=False)


def on_device(features, grad_out, scores, counts, w_gate, w_up, w_down):
    rows = features.shape[0]
    y, xl, core, xh = (lax.axis_index(a) for a in ("y", "xl", "core", "xh"))
    sc = jnp.stack([y, xl, counts[0, 0], counts[0, 0] + counts[0, 1], core, xh]).astype(jnp.int32)
    scores = scores.reshape(rows // BLOCK, BLOCK)

    feats = halves_over(features)
    feats += opposite_over(feats)
    pair_g = after(jnp.stack(to_plane(w_gate)), feats[1], feats[3])
    straight, crossed = to_plane(after(jnp.stack([w_up, w_down]), pair_g))
    pair_u, pair_d = (jnp.stack([straight[i], crossed[i]]) for i in range(2))
    grads = halves_over(after(grad_out, feats[5], feats[6]))
    gate_all = spread_pair(pair_g, *feats[1:], pair_u, pair_d)

    own_g, send_g = pre_part(sc, feats, gate_all)
    got_g = lax.ppermute(send_g, "xl", ring(2, 1))
    up_all = spread_pair(pair_u, send_g, *grads[1:])
    own_u, send_u = pre_part(after(sc, got_g), feats, up_all)
    got_u = lax.ppermute(send_u, "xl", ring(2, 1))
    grads += opposite_over(after(grads, send_g))
    own_b, send_b = pre_part(sc, grads, spread_pair(pair_d, send_u))
    got_b = lax.ppermute(send_b, "xl", ring(2, 1))

    keep, away = down_part(after(sc, send_b), scores, own_g, got_g, own_u, got_u, grads)
    both_d = over_cores(keep, lax.ppermute(away, "core", ring(2, 1)))
    part_d = scatter_z(both_d)
    total, gu, keep, away = gate_up_part(
        sc, scores, own_g, got_g, own_u, got_u, own_b, after(got_b, both_d), feats
    )
    got = lax.ppermute(after(away, part_d), "core", ring(2, 1))
    total = total + lax.ppermute(total, "y", [(i, i ^ 1) for i in range(4)])
    both_gu = over_cores(after(keep, total), got)
    part_gu = scatter_z(both_gu)

    dx = rows_part(sc, after(gu, both_gu), gate_all, up_all)
    total = total + lax.ppermute(total, "y", [(i, i ^ 2) for i in range(4)])
    dx, _ = lax.optimization_barrier((dx, total))
    total = total + lax.ppermute(total, "xl", ring(2, 1))
    from_below = lax.ppermute(dx[2], "y", ring(4, 1))
    from_above = lax.ppermute(dx[1], "y", ring(4, 3))
    opposite = lax.ppermute(dx[3], "y", ring(4, 2))
    grad_features = (
        (dx[0].astype(F32) + from_below.astype(F32)) + (from_above.astype(F32) + opposite.astype(F32))
    ).astype(BF)

    grad_down = over_chips(part_d, xh)
    grad_gu = over_chips(after(part_gu, grad_down, total), xh)
    return grad_features, total.reshape(rows), grad_gu[0], grad_gu[1], grad_down[0]


def solution(mesh):
    fine = Mesh(mesh.devices.reshape(2, 4, 4, 2, 2), ("xl", "y", "z", "xh", "core"))
    grp, blk = ("xl", "y"), ("z", "xh", "core")
    weight = P(None, grp, blk)
    return jax.shard_map(
        on_device,
        mesh=fine,
        in_specs=(P(blk, grp), P(blk, grp), P(blk), P(blk, None), weight, weight, weight),
        out_specs=(P(blk, grp), P(blk), weight, weight, weight),
        check_vma=False,
    )
```

```python
import jax
import jax.numpy as jnp
from jax import lax
from jax.experimental import pallas as pl
from jax.experimental.pallas import tpu as pltpu
from jax.sharding import Mesh
from jax.sharding import PartitionSpec as P

EXP = 2
BLOCK = 128
TILE = 256
HID = 192
VMEM = 60 << 20
COLS = 256
BF = jnp.bfloat16
F32 = jnp.float32
NT = (((1,), (1,)), ((), ()))
OFFS = (0, 3, 1, 2)
ANY = pl.BlockSpec(memory_space=pl.ANY)
VM = pl.BlockSpec(memory_space=pltpu.VMEM)
SM = pl.BlockSpec(memory_space=pltpu.SMEM)
Y, XL, FIRST, LIVE, CORE, XH = range(6)


def ring(n, k):
    return [(i, (i + k) % n) for i in range(n)]


def home(xl, z):
    return (xl, z) if z // 2 == xl else (1 - xl, (z + 2) % 4)


def swap_pairs(flip):
    pairs = []
    for xl in range(2):
        for z in range(4):
            for xh in range(2):
                a, b = home(xl, z)
                pairs.append(((xl * 4 + z) * 2 + xh, (a * 4 + b) * 2 + (xh ^ flip)))
    return pairs


def after(x, *others):
    return lax.optimization_barrier((x, *others))[0]


def aligned(i, unit):
    return pl.ds(pl.multiple_of(i * unit, unit), unit)


def y_of(sc, p):
    return lax.rem(sc[Y] + OFFS[p], 4)


def load_rows(sc, pieces, dst, sem):
    rows, width = pieces[0].shape
    half = rows // 2
    copies = []
    for i, piece in enumerate(pieces):
        where = aligned(y_of(sc, (i + 1) // 2), width)
        some = pl.ds(0, rows) if i == 0 else pl.ds((i - 1) % 2 * half, half)
        copies.append(pltpu.make_async_copy(piece, dst.at[some, where], sem.at[i]))
    return copies


def load_weight(sc, pair, row, dst, sem, at_sem):
    copies = []
    for c, ref in enumerate(pair):
        core = sc[CORE] if c == 0 else 1 - sc[CORE]
        for slot in range(4):
            for flip in range(2):
                xh = 1 - sc[XH] if flip else sc[XH]
                cb = slot % 2 * 4 + xh * 2 + core
                copies.append(
                    pltpu.make_async_copy(
                        ref.at[slot, flip],
                        dst.at[:, pl.ds(row + slot // 2 * HID, HID), aligned(cb, COLS)],
                        sem.at[at_sem + c * 8 + slot * 2 + flip],
                    )
                )
    return copies


def expert_of(sc, block):
    return (block * BLOCK >= sc[FIRST]).astype(jnp.int32)


def by_tile(sc, tile, work):
    low, high = expert_of(sc, 2 * tile), expert_of(sc, 2 * tile + 1)
    start = tile * TILE

    @pl.when(low == high)
    def _():
        work(pl.multiple_of(start, TILE), TILE, low)

    @pl.when(low != high)
    def _():
        work(pl.multiple_of(start, BLOCK), BLOCK, low)
        work(pl.multiple_of(start + BLOCK, BLOCK), BLOCK, high)


def start_all(copies):
    for c in copies:
        c.start()
    return copies


def wait_all(copies):
    for c in copies:
        c.wait()


def pre_kernel(sc, x0, x1, x2, x3, x4, x5, x6, w0, w1, own, send, xv, wv, xsem, wsem):
    wait_all(
        start_all(
            load_weight(sc, (w0, w1), 0, wv, wsem, 0) + load_rows(sc, (x0, x1, x2, x3, x4, x5, x6), xv, xsem)
        )
    )

    def work(start, size, expert):
        at = pl.ds(start, size)
        part = lax.dot_general(xv[at, :], wv[expert], NT, preferred_element_type=F32)
        own[at, :] = part
        send[at, :] = part.astype(BF)

    @pl.loop(0, xv.shape[0] // TILE)
    def _(t):
        by_tile(sc, t, work)


def pre_part(sc, pieces, weight):
    rows, width = pieces[0].shape
    wide, n = 4 * width, 2 * HID
    return pl.pallas_call(
        pre_kernel,
        out_shape=(jax.ShapeDtypeStruct((rows, n), F32), jax.ShapeDtypeStruct((rows, n), BF)),
        in_specs=[SM] + [ANY] * 9,
        out_specs=(VM, VM),
        scratch_shapes=[
            pltpu.VMEM((rows, wide), BF),
            pltpu.VMEM((EXP, n, wide), BF),
            pltpu.SemaphoreType.DMA((7,)),
            pltpu.SemaphoreType.DMA((16,)),
        ],
        compiler_params=pltpu.CompilerParams(vmem_limit_bytes=VMEM),
        cost_estimate=pl.CostEstimate(
            flops=4 * rows * n * wide, bytes_accessed=10 << 20, transcendentals=0
        ),
    )(sc, *pieces, *weight)


def column(row):
    return jnp.transpose(jnp.broadcast_to(row, (BLOCK, BLOCK)))[:, :1]


def transposed_into(dst, sc, b, at, rows, value):
    expert = expert_of(sc, b)
    dst[expert, rows, at] = jnp.transpose(value)
    dst[1 - expert, rows, at] = jnp.zeros((rows.stop - rows.start, BLOCK), value.dtype)


def weight_out(sc, src, row, e, keep, away, w, sem):
    outs = []
    for rel, out in enumerate((keep, away)):
        core = sc[CORE] if rel == 0 else 1 - sc[CORE]
        for h in range(2):
            for zz in range(2):
                for xh in range(2):
                    i = (((w * EXP + e) * 2 + rel) * 2 + h) * 4 + zz * 2 + xh
                    outs.append(
                        pltpu.make_async_copy(
                            src.at[e, pl.ds(row + h * HID, HID), aligned((zz * 2 + xh) * 2 + core, COLS)],
                            out.at[h * 2 + zz, xh, w, e],
                            sem.at[i],
                        )
                    )
    return outs


def down_kernel(
    sc, scores, own_g, got_g, own_u, got_u, g0, g1, g2, g3, g4, g5, g6, keep, away, gv, st, dd, gsem, dsem
):
    rows, width = g0.shape
    gload = start_all(load_rows(sc, (g0, g1, g2, g3, g4, g5, g6), gv, gsem))

    @pl.loop(0, rows // BLOCK)
    def _(b):
        at = aligned(b, BLOCK)
        live = (b * BLOCK < sc[LIVE]).astype(F32)
        gate = own_g[at, :] + got_g[at, :].astype(F32)
        up = own_u[at, :] + got_u[at, :].astype(F32)
        hidden = (gate * jax.nn.sigmoid(gate) * up).astype(BF).astype(F32)
        scaled = (column(scores[pl.ds(b, 1), :]) * live * hidden).astype(BF)
        transposed_into(st, sc, b, at, slice(0, 2 * HID), scaled)

    wait_all(gload)
    outs = []
    for e in range(EXP):
        for n in range(4):
            at = pl.ds(n * width, width)
            dd[e, :, at] = jnp.dot(st[e], gv[:, at], preferred_element_type=F32).astype(BF)
        outs += start_all(weight_out(sc, dd, 0, e, keep, away, 0, dsem))
    wait_all(outs)


def down_part(sc, scores, own_g, got_g, own_u, got_u, grads):
    rows, width = grads[0].shape
    out = jax.ShapeDtypeStruct((4, 2, 1, EXP, HID, COLS), BF)
    return pl.pallas_call(
        down_kernel,
        out_shape=(out, out),
        in_specs=[SM] + [VM] * 5 + [ANY] * 7,
        out_specs=(ANY, ANY),
        scratch_shapes=[
            pltpu.VMEM((rows, 4 * width), BF),
            pltpu.VMEM((EXP, 2 * HID, rows), BF),
            pltpu.VMEM((EXP, 2 * HID, 4 * width), BF),
            pltpu.SemaphoreType.DMA((7,)),
            pltpu.SemaphoreType.DMA((32,)),
        ],
        compiler_params=pltpu.CompilerParams(vmem_limit_bytes=VMEM),
        cost_estimate=pl.CostEstimate(
            flops=8 * rows * HID * 4 * width, bytes_accessed=14 << 20, transcendentals=rows * 384
        ),
    )(sc, scores, own_g, got_g, own_u, got_u, *grads)


def gate_up_kernel(
    sc, scores, own_g, got_g, own_u, got_u, own_b, got_b, x0, x1, x2, x3, x4, x5, x6,
    sgrad, gu, keep, away, xv, gut, dgu, xsem, dsem,
):
    rows, width = x0.shape
    n = 2 * HID
    xload = start_all(load_rows(sc, (x0, x1, x2, x3, x4, x5, x6), xv, xsem))

    @pl.loop(0, rows // BLOCK)
    def _(b):
        at = aligned(b, BLOCK)
        live = (b * BLOCK < sc[LIVE]).astype(F32)
        gate = own_g[at, :] + got_g[at, :].astype(F32)
        up = own_u[at, :] + got_u[at, :].astype(F32)
        back = own_b[at, :] + got_b[at, :].astype(F32)
        sig = jax.nn.sigmoid(gate)
        act = gate * sig
        hidden = (act * up).astype(BF).astype(F32)
        mine = (lax.broadcasted_iota(jnp.int32, hidden.shape, 1) >= HID).astype(jnp.int32) == sc[XL]
        total = jnp.sum(jnp.where(mine, hidden * back, 0.0), axis=1, keepdims=True) * live
        sgrad[pl.ds(b, 1), :] = jnp.transpose(jnp.broadcast_to(total, (BLOCK, BLOCK)))[:1]
        hid_grad = column(scores[pl.ds(b, 1), :]) * live * back
        gate_grad = (hid_grad * up * sig * (1.0 + gate * (1.0 - sig))).astype(BF)
        up_grad = (hid_grad * act).astype(BF)
        gu[at, :n] = gate_grad
        gu[at, n:] = up_grad
        transposed_into(gut, sc, b, at, slice(0, n), gate_grad)
        transposed_into(gut, sc, b, at, slice(n, 2 * n), up_grad)

    wait_all(xload)
    outs = []
    for e in range(EXP):
        for k in range(4):
            at = pl.ds(k * width, width)
            dgu[e, :, at] = jnp.dot(gut[e], xv[:, at], preferred_element_type=F32).astype(BF)
        for w in range(2):
            outs += start_all(weight_out(sc, dgu, w * n, e, keep, away, w, dsem))
    wait_all(outs)


def gate_up_part(sc, scores, own_g, got_g, own_u, got_u, own_b, got_b, feats):
    rows, width = feats[0].shape
    out = jax.ShapeDtypeStruct((4, 2, 2, EXP, HID, COLS), BF)
    return pl.pallas_call(
        gate_up_kernel,
        out_shape=(
            jax.ShapeDtypeStruct((rows // BLOCK, BLOCK), F32),
            jax.ShapeDtypeStruct((rows, 4 * HID), BF),
            out,
            out,
        ),
        in_specs=[SM] + [VM] * 7 + [ANY] * 7,
        out_specs=(VM, VM, ANY, ANY),
        scratch_shapes=[
            pltpu.VMEM((rows, 4 * width), BF),
            pltpu.VMEM((EXP, 4 * HID, rows), BF),
            pltpu.VMEM((EXP, 4 * HID, 4 * width), BF),
            pltpu.SemaphoreType.DMA((7,)),
            pltpu.SemaphoreType.DMA((64,)),
        ],
        compiler_params=pltpu.CompilerParams(vmem_limit_bytes=VMEM),
        cost_estimate=pl.CostEstimate(
            flops=16 * rows * HID * 4 * width, bytes_accessed=20 << 20, transcendentals=rows * 384
        ),
    )(sc, scores, own_g, got_g, own_u, got_u, own_b, got_b, *feats)


def rows_kernel(sc, gu, g0, g1, u0, u1, d0, d1, d2, d3, wv, dxv, wsem, osem):
    rows, wide = dxv.shape
    width = wide // 4
    wait_all(
        start_all(
            load_weight(sc, (g0, g1), 0, wv, wsem, 0) + load_weight(sc, (u0, u1), 2 * HID, wv, wsem, 16)
        )
    )

    def work(start, size, expert):
        at = pl.ds(start, size)
        dxv[at, :] = jnp.dot(gu[at, :], wv[expert], preferred_element_type=F32).astype(BF)

    @pl.loop(0, rows // TILE)
    def _(t):
        by_tile(sc, t, work)

    wait_all(
        start_all(
            [
                pltpu.make_async_copy(dxv.at[:, aligned(y_of(sc, p), width)], d, osem.at[p])
                for p, d in enumerate((d0, d1, d2, d3))
            ]
        )
    )


def rows_part(sc, gu, w_gate, w_up):
    rows, width = gu.shape[0], 512
    return pl.pallas_call(
        rows_kernel,
        out_shape=(jax.ShapeDtypeStruct((rows, width), BF),) * 4,
        in_specs=[SM, VM] + [ANY] * 4,
        out_specs=(ANY,) * 4,
        scratch_shapes=[
            pltpu.VMEM((EXP, 4 * HID, 4 * width), BF),
            pltpu.VMEM((rows, 4 * width), BF),
            pltpu.SemaphoreType.DMA((32,)),
            pltpu.SemaphoreType.DMA((4,)),
        ],
        compiler_params=pltpu.CompilerParams(vmem_limit_bytes=VMEM),
        cost_estimate=pl.CostEstimate(
            flops=8 * rows * HID * 4 * width, bytes_accessed=14 << 20, transcendentals=0
        ),
    )(sc, gu, *w_gate, *w_up)


def halves_over(x):
    half = x.shape[0] // 2
    near = [lax.ppermute(x[:half], "y", ring(4, k)) for k in (1, 3)]
    rest = [lax.ppermute(x[half:], "y", ring(4, k)) for k in (1, 3)]
    return x, near[0], rest[0], near[1], rest[1]


def opposite_over(pieces):
    return lax.ppermute(pieces[1], "y", ring(4, 1)), lax.ppermute(pieces[4], "y", ring(4, 3))


def to_plane(w):
    return (
        lax.ppermute(w, ("xl", "z", "xh"), swap_pairs(0)),
        lax.ppermute(w, ("xl", "z", "xh"), swap_pairs(1)),
    )


def spread_pair(pair, *before):
    here = after(lax.all_gather(pair, "z", axis=0, tiled=False), *before)
    return here, lax.ppermute(here, "core", ring(2, 1))


def over_cores(keep, got):
    return (keep.astype(F32) + got.astype(F32)).astype(BF)


def over_chips(part, xh):
    straight = lax.dynamic_index_in_dim(part, xh, 0, False)
    crossed = lax.dynamic_index_in_dim(part, 1 - xh, 0, False)
    straight = lax.ppermute(straight, ("xl", "z", "xh"), swap_pairs(0))
    crossed = lax.ppermute(crossed, ("xl", "z", "xh"), swap_pairs(1))
    return straight.astype(F32) + crossed.astype(F32)


def on_device(features, grad_out, scores, counts, w_gate, w_up, w_down):
    rows = features.shape[0]
    y, xl, core, xh = (lax.axis_index(a) for a in ("y", "xl", "core", "xh"))
    sc = jnp.stack([y, xl, counts[0, 0], counts[0, 0] + counts[0, 1], core, xh]).astype(jnp.int32)
    scores = scores.reshape(rows // BLOCK, BLOCK)

    feats = halves_over(features)
    feats += opposite_over(feats)
    pair_g = after(jnp.stack(to_plane(w_gate)), feats[1], feats[3])
    straight, crossed = to_plane(after(jnp.stack([w_up, w_down]), feats[2], feats[4]))
    pair_u, pair_d = (jnp.stack([straight[i], crossed[i]]) for i in range(2))
    grads = halves_over(after(grad_out, feats[5], feats[6]))
    gate_all = spread_pair(pair_g, *feats[1:], pair_u, pair_d)

    own_g, send_g = pre_part(sc, feats, gate_all)
    got_g = lax.ppermute(send_g, "xl", ring(2, 1))
    up_all = spread_pair(pair_u, got_g, *grads[1:])
    own_u, send_u = pre_part(after(sc, got_g), feats, up_all)
    got_u = lax.ppermute(send_u, "xl", ring(2, 1))
    grads += opposite_over(after(grads, send_g))
    own_b, send_b = pre_part(sc, grads, spread_pair(pair_d, send_u))
    got_b = lax.ppermute(send_b, "xl", ring(2, 1))

    keep, away = down_part(after(sc, send_b), scores, own_g, got_g, own_u, got_u, grads)
    both_d = over_cores(keep, lax.ppermute(away, "core", ring(2, 1)))
    total, gu, keep, away = gate_up_part(
        sc, scores, own_g, got_g, own_u, got_u, own_b, after(got_b, both_d), feats
    )
    got = lax.ppermute(away, "core", ring(2, 1))
    total = total + lax.ppermute(total, "y", [(i, i ^ 1) for i in range(4)])
    both = jnp.concatenate([over_cores(after(keep, total), got), both_d], axis=2)
    part = lax.psum_scatter(both, "z", scatter_dimension=0, tiled=False)

    dx = rows_part(sc, after(gu, both), gate_all, up_all)
    total = total + lax.ppermute(total, "y", [(i, i ^ 2) for i in range(4)])
    dx, _ = lax.optimization_barrier((dx, total))
    total = total + lax.ppermute(total, "xl", ring(2, 1))
    from_below = lax.ppermute(dx[2], "y", ring(4, 1))
    from_above = lax.ppermute(dx[1], "y", ring(4, 3))
    opposite = lax.ppermute(dx[3], "y", ring(4, 2))
    grad_features = (
        (dx[0].astype(F32) + from_below.astype(F32)) + (from_above.astype(F32) + opposite.astype(F32))
    ).astype(BF)

    weights = over_chips(part, xh)
    return grad_features, total.reshape(rows), weights[0], weights[1], weights[2]


def solution(mesh):
    fine = Mesh(mesh.devices.reshape(2, 4, 4, 2, 2), ("xl", "y", "z", "xh", "core"))
    grp, blk = ("xl", "y"), ("z", "xh", "core")
    weight = P(None, grp, blk)
    return jax.shard_map(
        on_device,
        mesh=fine,
        in_specs=(P(blk, grp), P(blk, grp), P(blk), P(blk, None), weight, weight, weight),
        out_specs=(P(blk, grp), P(blk), weight, weight, weight),
        check_vma=False,
    )
```

```python
import jax
import jax.numpy as jnp
from jax import lax
from jax.experimental import pallas as pl
from jax.experimental.pallas import tpu as pltpu
from jax.sharding import Mesh
from jax.sharding import PartitionSpec as P

EXP = 2
BLOCK = 128
TILE = 256
HID = 192
VMEM = 60 << 20
COLS = 256
BF = jnp.bfloat16
F32 = jnp.float32
NT = (((1,), (1,)), ((), ()))
OFFS = (0, 3, 1, 2)
ANY = pl.BlockSpec(memory_space=pl.ANY)
VM = pl.BlockSpec(memory_space=pltpu.VMEM)
SM = pl.BlockSpec(memory_space=pltpu.SMEM)
Y, XL, FIRST, LIVE, CORE, XH = range(6)


def ring(n, k):
    return [(i, (i + k) % n) for i in range(n)]


def home(xl, z):
    return (xl, z) if z // 2 == xl else (1 - xl, (z + 2) % 4)


def swap_pairs(flip):
    pairs = []
    for xl in range(2):
        for z in range(4):
            for xh in range(2):
                a, b = home(xl, z)
                pairs.append(((xl * 4 + z) * 2 + xh, (a * 4 + b) * 2 + (xh ^ flip)))
    return pairs


def after(x, *others):
    return lax.optimization_barrier((x, *others))[0]


def aligned(i, unit):
    return pl.ds(pl.multiple_of(i * unit, unit), unit)


def y_of(sc, p):
    return lax.rem(sc[Y] + OFFS[p], 4)


def load_rows(sc, pieces, dst, sem):
    rows, width = pieces[0].shape
    half = rows // 2
    copies = []
    for part in range(2):
        some = pl.ds(part * half, half)
        for p in range(4):
            piece = pieces[0].at[some] if p == 0 else pieces[2 * p - 1 + part]
            where = aligned(y_of(sc, p), width)
            copies.append(pltpu.make_async_copy(piece, dst.at[some, where], sem.at[part * 4 + p]))
    return copies


def load_weight(sc, pair, w, row, dst, sem, at_sem):
    copies = []
    for c, ref in enumerate(pair):
        core = sc[CORE] if c == 0 else 1 - sc[CORE]
        for slot in range(4):
            for flip in range(2):
                xh = 1 - sc[XH] if flip else sc[XH]
                cb = slot % 2 * 4 + xh * 2 + core
                copies.append(
                    pltpu.make_async_copy(
                        ref.at[slot, flip, w],
                        dst.at[:, pl.ds(row + slot // 2 * HID, HID), aligned(cb, COLS)],
                        sem.at[at_sem + c * 8 + slot * 2 + flip],
                    )
                )
    return copies


def expert_of(sc, block):
    return (sc[FIRST] <= block * BLOCK).astype(jnp.int32)


def by_tile(sc, tile, work):
    low, high = expert_of(sc, 2 * tile), expert_of(sc, 2 * tile + 1)
    start = tile * TILE

    @pl.when(low == high)
    def _():
        work(start, TILE, low)

    @pl.when(low != high)
    def _():
        work(start, BLOCK, low)
        work(start + BLOCK, BLOCK, high)


def start_all(copies):
    for c in copies:
        c.start()
    return copies


def wait_all(copies):
    for c in copies:
        c.wait()


def pre_kernel(sc, x0, x1, x2, x3, x4, x5, x6, w0, w1, own, send, xv, wv, ov, sv, xsem, wsem, osem):
    n = ov.shape[1] // (2 * HID)
    wload = []
    for w in range(n):
        wload += load_weight(sc, (w0, w1), w, w * 2 * HID, wv, wsem, w * 16)
    xload = load_rows(sc, (x0, x1, x2, x3, x4, x5, x6), xv, xsem)
    start_all(wload + xload)
    wait_all(wload)
    outs = []

    def work(start, size, expert):
        at = pl.ds(start, size)
        part = lax.dot_general(xv[at, :], wv[expert], NT, preferred_element_type=F32)
        ov[at, :] = part
        sv[at, :] = part.astype(BF)

    for t in range(xv.shape[0] // TILE):
        if t % 2 == 0:
            wait_all(xload[t * 2 : t * 2 + 4])
        by_tile(sc, t, work)
        at = pl.ds(t * TILE, TILE)
        outs += start_all(
            [
                pltpu.make_async_copy(ov.at[at], own.at[at], osem.at[2 * t]),
                pltpu.make_async_copy(sv.at[at], send.at[at], osem.at[2 * t + 1]),
            ]
        )
    wait_all(outs)


def pre_part(sc, pieces, weight):
    rows, width = pieces[0].shape
    nw = weight[0].shape[2]
    wide, n = 4 * width, nw * 2 * HID
    return pl.pallas_call(
        pre_kernel,
        out_shape=(jax.ShapeDtypeStruct((rows, n), F32), jax.ShapeDtypeStruct((rows, n), BF)),
        in_specs=[SM] + [ANY] * 9,
        out_specs=(ANY, ANY),
        scratch_shapes=[
            pltpu.VMEM((rows, wide), BF),
            pltpu.VMEM((EXP, n, wide), BF),
            pltpu.VMEM((rows, n), F32),
            pltpu.VMEM((rows, n), BF),
            pltpu.SemaphoreType.DMA((8,)),
            pltpu.SemaphoreType.DMA((nw * 16,)),
            pltpu.SemaphoreType.DMA((rows // TILE * 2,)),
        ],
        compiler_params=pltpu.CompilerParams(vmem_limit_bytes=VMEM),
        cost_estimate=pl.CostEstimate(
            flops=4 * rows * n * wide, bytes_accessed=10 << 20, transcendentals=0
        ),
    )(sc, *pieces, *weight)


def column(row):
    return jnp.transpose(jnp.broadcast_to(row, (BLOCK, BLOCK)))[:, :1]


def transposed_into(dst, sc, b, at, rows, value):
    expert = expert_of(sc, b)
    dst[expert, rows, at] = jnp.transpose(value)
    dst[1 - expert, rows, at] = jnp.zeros((rows.stop - rows.start, BLOCK), value.dtype)


def weight_out(sc, src, row, e, keep, away, w, sem):
    outs = []
    for rel, out in enumerate((keep, away)):
        core = sc[CORE] if rel == 0 else 1 - sc[CORE]
        for h in range(2):
            for zz in range(2):
                for xh in range(2):
                    i = (((w * EXP + e) * 2 + rel) * 2 + h) * 4 + zz * 2 + xh
                    outs.append(
                        pltpu.make_async_copy(
                            src.at[e, pl.ds(row + h * HID, HID), aligned((zz * 2 + xh) * 2 + core, COLS)],
                            out.at[h * 2 + zz, xh, w, e],
                            sem.at[i],
                        )
                    )
    return outs


def down_kernel(
    sc, scores, own_gu, got_gu, g0, g1, g2, g3, g4, g5, g6, keep, away, gv, st, dd, gsem, dsem
):
    rows, width = g0.shape
    gload = start_all(load_rows(sc, (g0, g1, g2, g3, g4, g5, g6), gv, gsem))

    @pl.loop(0, rows // BLOCK)
    def _(b):
        at = aligned(b, BLOCK)
        live = (b * BLOCK < sc[LIVE]).astype(F32)
        both = own_gu[at, :] + got_gu[at, :].astype(F32)
        gate, up = both[:, : 2 * HID], both[:, 2 * HID :]
        hidden = (gate * jax.nn.sigmoid(gate) * up).astype(BF).astype(F32)
        scaled = (column(scores[pl.ds(b, 1), :]) * live * hidden).astype(BF)
        transposed_into(st, sc, b, at, slice(0, 2 * HID), scaled)

    wait_all(gload)
    outs = []
    for e in range(EXP):
        for n in range(4):
            at = pl.ds(n * width, width)
            dd[e, :, at] = jnp.dot(st[e], gv[:, at], preferred_element_type=F32).astype(BF)
        outs += start_all(weight_out(sc, dd, 0, e, keep, away, 0, dsem))
    wait_all(outs)


def down_part(sc, scores, own_gu, got_gu, grads):
    rows, width = grads[0].shape
    out = jax.ShapeDtypeStruct((4, 2, 1, EXP, HID, COLS), BF)
    return pl.pallas_call(
        down_kernel,
        out_shape=(out, out),
        in_specs=[SM] + [VM] * 3 + [ANY] * 7,
        out_specs=(ANY, ANY),
        scratch_shapes=[
            pltpu.VMEM((rows, 4 * width), BF),
            pltpu.VMEM((EXP, 2 * HID, rows), BF),
            pltpu.VMEM((EXP, 2 * HID, 4 * width), BF),
            pltpu.SemaphoreType.DMA((8,)),
            pltpu.SemaphoreType.DMA((32,)),
        ],
        compiler_params=pltpu.CompilerParams(vmem_limit_bytes=VMEM),
        cost_estimate=pl.CostEstimate(
            flops=8 * rows * HID * 4 * width, bytes_accessed=14 << 20, transcendentals=rows * 384
        ),
    )(sc, scores, own_gu, got_gu, *grads)


def gate_up_kernel(
    sc, scores, own_gu, got_gu, own_b, got_b, x0, x1, x2, x3, x4, x5, x6,
    sgrad, gu, keep, away, xv, gut, dgu, ogu, ggu, ob, gb, guv, xsem, dsem, isem, usem,
):
    rows, width = x0.shape
    n = 2 * HID
    per = rows // 4
    iload = []
    for t in range(4):
        at = pl.ds(t * per, per)
        for i, (src, dst) in enumerate(((own_gu, ogu), (got_gu, ggu), (own_b, ob), (got_b, gb))):
            iload.append(pltpu.make_async_copy(src.at[at], dst.at[at], isem.at[t * 4 + i]))
    xload = load_rows(sc, (x0, x1, x2, x3, x4, x5, x6), xv, xsem)
    start_all(iload + xload)
    outs = []

    def block(b):
        at = aligned(b, BLOCK)
        live = (b * BLOCK < sc[LIVE]).astype(F32)
        both = ogu[at, :] + ggu[at, :].astype(F32)
        gate, up = both[:, :n], both[:, n:]
        back = ob[at, :] + gb[at, :].astype(F32)
        sig = jax.nn.sigmoid(gate)
        act = gate * sig
        hidden = (act * up).astype(BF).astype(F32)
        mine = (lax.broadcasted_iota(jnp.int32, hidden.shape, 1) >= HID).astype(jnp.int32) == sc[XL]
        total = jnp.sum(jnp.where(mine, hidden * back, 0.0), axis=1, keepdims=True) * live
        sgrad[pl.ds(b, 1), :] = jnp.transpose(jnp.broadcast_to(total, (BLOCK, BLOCK)))[:1]
        hid_grad = column(scores[pl.ds(b, 1), :]) * live * back
        gate_grad = (hid_grad * up * sig * (1.0 + gate * (1.0 - sig))).astype(BF)
        up_grad = (hid_grad * act).astype(BF)
        guv[at, :n] = gate_grad
        guv[at, n:] = up_grad
        transposed_into(gut, sc, b, at, slice(0, n), gate_grad)
        transposed_into(gut, sc, b, at, slice(n, 2 * n), up_grad)

    for t in range(4):
        wait_all(iload[t * 4 : t * 4 + 4])

        @pl.loop(t * per // BLOCK, (t + 1) * per // BLOCK)
        def _(b):
            block(b)

        at = pl.ds(t * per, per)
        outs += start_all([pltpu.make_async_copy(guv.at[at], gu.at[at], usem.at[t])])

    wait_all(xload)
    for e in range(EXP):
        for k in range(4):
            at = pl.ds(k * width, width)
            dgu[e, :, at] = jnp.dot(gut[e], xv[:, at], preferred_element_type=F32).astype(BF)
        for w in range(2):
            outs += start_all(weight_out(sc, dgu, w * n, e, keep, away, w, dsem))
    wait_all(outs)


def gate_up_part(sc, scores, own_gu, got_gu, own_b, got_b, feats):
    rows, width = feats[0].shape
    out = jax.ShapeDtypeStruct((4, 2, 2, EXP, HID, COLS), BF)
    return pl.pallas_call(
        gate_up_kernel,
        out_shape=(
            jax.ShapeDtypeStruct((rows // BLOCK, BLOCK), F32),
            jax.ShapeDtypeStruct((rows, 4 * HID), BF),
            out,
            out,
        ),
        in_specs=[SM, VM] + [ANY] * 11,
        out_specs=(VM, ANY, ANY, ANY),
        scratch_shapes=[
            pltpu.VMEM((rows, 4 * width), BF),
            pltpu.VMEM((EXP, 4 * HID, rows), BF),
            pltpu.VMEM((EXP, 4 * HID, 4 * width), BF),
            pltpu.VMEM((rows, 4 * HID), F32),
            pltpu.VMEM((rows, 4 * HID), BF),
            pltpu.VMEM((rows, 2 * HID), F32),
            pltpu.VMEM((rows, 2 * HID), BF),
            pltpu.VMEM((rows, 4 * HID), BF),
            pltpu.SemaphoreType.DMA((8,)),
            pltpu.SemaphoreType.DMA((64,)),
            pltpu.SemaphoreType.DMA((16,)),
            pltpu.SemaphoreType.DMA((4,)),
        ],
        compiler_params=pltpu.CompilerParams(vmem_limit_bytes=VMEM),
        cost_estimate=pl.CostEstimate(
            flops=16 * rows * HID * 4 * width, bytes_accessed=20 << 20, transcendentals=rows * 384
        ),
    )(sc, scores, own_gu, got_gu, own_b, got_b, *feats)


def rows_kernel(sc, gu, w0, w1, d0, d1, d2, d3, wv, guv, dxv, wsem, usem, osem):
    rows, wide = dxv.shape
    width = wide // 4
    load = load_weight(sc, (w0, w1), 0, 0, wv, wsem, 0) + load_weight(sc, (w0, w1), 1, 2 * HID, wv, wsem, 16)
    load.append(pltpu.make_async_copy(gu, guv, usem.at[0]))
    wait_all(start_all(load))

    def work(start, size, expert):
        at = pl.ds(start, size)
        dxv[at, :] = jnp.dot(guv[at, :], wv[expert], preferred_element_type=F32).astype(BF)

    outs = []
    for t in range(rows // TILE):
        by_tile(sc, t, work)
        at = pl.ds(t * TILE, TILE)
        for p, d in enumerate((d0, d1, d2, d3)):
            where = aligned(y_of(sc, p), width)
            outs += start_all([pltpu.make_async_copy(dxv.at[at, where], d.at[at], osem.at[t * 4 + p])])
    wait_all(outs)


def rows_part(sc, gu, weight):
    rows, width = gu.shape[0], 512
    return pl.pallas_call(
        rows_kernel,
        out_shape=(jax.ShapeDtypeStruct((rows, width), BF),) * 4,
        in_specs=[SM] + [ANY] * 3,
        out_specs=(ANY,) * 4,
        scratch_shapes=[
            pltpu.VMEM((EXP, 4 * HID, 4 * width), BF),
            pltpu.VMEM((rows, 4 * HID), BF),
            pltpu.VMEM((rows, 4 * width), BF),
            pltpu.SemaphoreType.DMA((32,)),
            pltpu.SemaphoreType.DMA((1,)),
            pltpu.SemaphoreType.DMA((16,)),
        ],
        compiler_params=pltpu.CompilerParams(vmem_limit_bytes=VMEM),
        cost_estimate=pl.CostEstimate(
            flops=8 * rows * HID * 4 * width, bytes_accessed=14 << 20, transcendentals=0
        ),
    )(sc, gu, *weight)


def halves_over(x):
    half = x.shape[0] // 2
    near = [lax.ppermute(x[:half], "y", ring(4, k)) for k in (1, 3)]
    rest = [lax.ppermute(x[half:], "y", ring(4, k)) for k in (1, 3)]
    return x, near[0], rest[0], near[1], rest[1]


def opposite_over(pieces):
    return lax.ppermute(pieces[1], "y", ring(4, 1)), lax.ppermute(pieces[4], "y", ring(4, 3))


def to_plane(w):
    return (
        lax.ppermute(w, ("xl", "z", "xh"), swap_pairs(0)),
        lax.ppermute(w, ("xl", "z", "xh"), swap_pairs(1)),
    )


def spread_pair(pair, *before):
    here = after(lax.all_gather(pair, "z", axis=0, tiled=False), *before)
    return here, lax.ppermute(here, "core", ring(2, 1))


def over_cores(keep, got):
    return (keep.astype(F32) + got.astype(F32)).astype(BF)


def over_chips(part, xh):
    straight = lax.dynamic_index_in_dim(part, xh, 0, False)
    crossed = lax.dynamic_index_in_dim(part, 1 - xh, 0, False)
    straight = lax.ppermute(straight, ("xl", "z", "xh"), swap_pairs(0))
    crossed = lax.ppermute(crossed, ("xl", "z", "xh"), swap_pairs(1))
    return straight.astype(F32) + crossed.astype(F32)


def on_device(features, grad_out, scores, counts, w_gate, w_up, w_down):
    rows = features.shape[0]
    y, xl, core, xh = (lax.axis_index(a) for a in ("y", "xl", "core", "xh"))
    sc = jnp.stack([y, xl, counts[0, 0], counts[0, 0] + counts[0, 1], core, xh]).astype(jnp.int32)
    scores = scores.reshape(rows // BLOCK, BLOCK)

    feats = halves_over(features)
    feats += opposite_over(feats)
    pair_gu = after(jnp.stack(to_plane(jnp.stack([w_gate, w_up]))), feats[1], feats[3])
    pair_d = jnp.stack(to_plane(after(w_down, feats[2], feats[4])[None]))
    grads = halves_over(after(grad_out, feats[5], feats[6]))
    gu_all = spread_pair(pair_gu, *feats[1:], pair_d, grads[1], grads[3])

    own_gu, send_gu = pre_part(after(sc, grads[2], grads[4]), feats, gu_all)
    got_gu = lax.ppermute(send_gu, "xl", ring(2, 1))
    grads += opposite_over(grads)
    own_b, send_b = pre_part(after(sc, send_gu), grads, spread_pair(pair_d, grads[5], grads[6]))
    got_b = lax.ppermute(send_b, "xl", ring(2, 1))

    keep, away = down_part(after(sc, send_b), scores, own_gu, got_gu, grads)
    both_d = over_cores(keep, lax.ppermute(away, "core", ring(2, 1)))
    total, gu, keep, away = gate_up_part(
        sc, scores, own_gu, got_gu, own_b, after(got_b, both_d), feats
    )
    got = lax.ppermute(away, "core", ring(2, 1))
    total = total + lax.ppermute(total, "y", [(i, i ^ 1) for i in range(4)])
    both = jnp.concatenate([over_cores(after(keep, total), got), both_d], axis=2)
    part = lax.psum_scatter(both, "z", scatter_dimension=0, tiled=False)

    dx = rows_part(sc, after(gu, both), gu_all)
    total = total + after(lax.ppermute(total, "y", [(i, i ^ 2) for i in range(4)]), dx[0])
    dx, _ = lax.optimization_barrier((dx, total))
    total = total + lax.ppermute(total, "xl", ring(2, 1))
    from_below = lax.ppermute(dx[2], "y", ring(4, 1))
    from_above = lax.ppermute(dx[1], "y", ring(4, 3))
    opposite = lax.ppermute(dx[3], "y", ring(4, 2))
    grad_features = (
        (dx[0].astype(F32) + from_below.astype(F32)) + (from_above.astype(F32) + opposite.astype(F32))
    ).astype(BF)

    weights = over_chips(part, xh)
    return grad_features, total.reshape(rows), weights[0], weights[1], weights[2]


def solution(mesh):
    fine = Mesh(mesh.devices.reshape(2, 4, 4, 2, 2), ("xl", "y", "z", "xh", "core"))
    grp, blk = ("xl", "y"), ("z", "xh", "core")
    weight = P(None, grp, blk)
    return jax.shard_map(
        on_device,
        mesh=fine,
        in_specs=(P(blk, grp), P(blk, grp), P(blk), P(blk, None), weight, weight, weight),
        out_specs=(P(blk, grp), P(blk), weight, weight, weight),
        check_vma=False,
    )
```

```python
import jax
import jax.numpy as jnp
from jax import lax
from jax.experimental import pallas as pl
from jax.experimental.pallas import tpu as pltpu
from jax.sharding import Mesh
from jax.sharding import PartitionSpec as P

EXP = 2
BLOCK = 128
TILE = 256
HID = 192
VMEM = 60 << 20
COLS = 256
BF = jnp.bfloat16
F32 = jnp.float32
NT = (((1,), (1,)), ((), ()))
OFFS = (0, 3, 1, 2)
ANY = pl.BlockSpec(memory_space=pl.ANY)
VM = pl.BlockSpec(memory_space=pltpu.VMEM)
SM = pl.BlockSpec(memory_space=pltpu.SMEM)
Y, XL, FIRST, LIVE, CORE, XH = range(6)


def ring(n, k):
    return [(i, (i + k) % n) for i in range(n)]


def home(xl, z):
    return (xl, z) if z // 2 == xl else (1 - xl, (z + 2) % 4)


def swap_pairs(flip):
    pairs = []
    for xl in range(2):
        for z in range(4):
            for xh in range(2):
                a, b = home(xl, z)
                pairs.append(((xl * 4 + z) * 2 + xh, (a * 4 + b) * 2 + (xh ^ flip)))
    return pairs


def after(x, *others):
    return lax.optimization_barrier((x, *others))[0]


def aligned(i, unit):
    return pl.ds(pl.multiple_of(i * unit, unit), unit)


def y_of(sc, p):
    return lax.rem(sc[Y] + OFFS[p], 4)


def load_rows(sc, pieces, dst, sem):
    rows, width = pieces[0].shape
    half = rows // 2
    copies = []
    for part in range(2):
        some = pl.ds(part * half, half)
        for p in range(4):
            piece = pieces[0].at[some] if p == 0 else pieces[2 * p - 1 + part]
            where = aligned(y_of(sc, p), width)
            copies.append(pltpu.make_async_copy(piece, dst.at[some, where], sem.at[part * 4 + p]))
    return copies


def load_weight(sc, pair, w, row, dst, sem, at_sem):
    copies = []
    for c, ref in enumerate(pair):
        core = sc[CORE] if c == 0 else 1 - sc[CORE]
        for slot in range(4):
            for flip in range(2):
                xh = 1 - sc[XH] if flip else sc[XH]
                cb = slot % 2 * 4 + xh * 2 + core
                copies.append(
                    pltpu.make_async_copy(
                        ref.at[slot, flip, w],
                        dst.at[:, pl.ds(row + slot // 2 * HID, HID), aligned(cb, COLS)],
                        sem.at[at_sem + c * 8 + slot * 2 + flip],
                    )
                )
    return copies


def expert_of(sc, block):
    return (sc[FIRST] <= block * BLOCK).astype(jnp.int32)


def by_tile(sc, tile, work):
    low, high = expert_of(sc, 2 * tile), expert_of(sc, 2 * tile + 1)
    start = tile * TILE

    @pl.when(low == high)
    def _():
        work(start, TILE, low)

    @pl.when(low != high)
    def _():
        work(start, BLOCK, low)
        work(start + BLOCK, BLOCK, high)


def start_all(copies):
    for c in copies:
        c.start()
    return copies


def wait_all(copies):
    for c in copies:
        c.wait()


def pre_kernel(sc, x0, x1, x2, x3, x4, x5, x6, w0, w1, own, send, xv, wv, ov, sv, xsem, wsem, osem):
    n = ov.shape[1] // (2 * HID)
    wload = []
    for w in range(n):
        wload += load_weight(sc, (w0, w1), w, w * 2 * HID, wv, wsem, w * 16)
    xload = load_rows(sc, (x0, x1, x2, x3, x4, x5, x6), xv, xsem)
    start_all(wload + xload)
    wait_all(wload)
    outs = []

    def work(start, size, expert):
        at = pl.ds(start, size)
        part = lax.dot_general(xv[at, :], wv[expert], NT, preferred_element_type=F32)
        ov[at, :] = part
        sv[at, :] = part.astype(BF)

    for t in range(xv.shape[0] // TILE):
        if t % 2 == 0:
            wait_all(xload[t * 2 : t * 2 + 4])
        by_tile(sc, t, work)
        at = pl.ds(t * TILE, TILE)
        outs += start_all(
            [
                pltpu.make_async_copy(ov.at[at], own.at[at], osem.at[2 * t]),
                pltpu.make_async_copy(sv.at[at], send.at[at], osem.at[2 * t + 1]),
            ]
        )
    wait_all(outs)


def pre_part(sc, pieces, weight):
    rows, width = pieces[0].shape
    nw = weight[0].shape[2]
    wide, n = 4 * width, nw * 2 * HID
    return pl.pallas_call(
        pre_kernel,
        out_shape=(jax.ShapeDtypeStruct((rows, n), F32), jax.ShapeDtypeStruct((rows, n), BF)),
        in_specs=[SM] + [ANY] * 9,
        out_specs=(ANY, ANY),
        scratch_shapes=[
            pltpu.VMEM((rows, wide), BF),
            pltpu.VMEM((EXP, n, wide), BF),
            pltpu.VMEM((rows, n), F32),
            pltpu.VMEM((rows, n), BF),
            pltpu.SemaphoreType.DMA((8,)),
            pltpu.SemaphoreType.DMA((nw * 16,)),
            pltpu.SemaphoreType.DMA((rows // TILE * 2,)),
        ],
        compiler_params=pltpu.CompilerParams(vmem_limit_bytes=VMEM),
        cost_estimate=pl.CostEstimate(
            flops=4 * rows * n * wide, bytes_accessed=10 << 20, transcendentals=0
        ),
    )(sc, *pieces, *weight)


def column(row):
    return jnp.transpose(jnp.broadcast_to(row, (BLOCK, BLOCK)))[:, :1]


def transposed_into(dst, sc, b, at, rows, value):
    expert = expert_of(sc, b)
    dst[expert, rows, at] = jnp.transpose(value)
    dst[1 - expert, rows, at] = jnp.zeros((rows.stop - rows.start, BLOCK), value.dtype)


def weight_out(sc, src, row, e, keep, away, w, sem):
    outs = []
    for rel, out in enumerate((keep, away)):
        core = sc[CORE] if rel == 0 else 1 - sc[CORE]
        for h in range(2):
            for zz in range(2):
                for xh in range(2):
                    i = (((w * EXP + e) * 2 + rel) * 2 + h) * 4 + zz * 2 + xh
                    outs.append(
                        pltpu.make_async_copy(
                            src.at[e, pl.ds(row + h * HID, HID), aligned((zz * 2 + xh) * 2 + core, COLS)],
                            out.at[h * 2 + zz, xh, w, e],
                            sem.at[i],
                        )
                    )
    return outs


def down_kernel(
    sc, scores, own_gu, got_gu, g0, g1, g2, g3, g4, g5, g6, keep, away, gv, st, dd, gsem, dsem
):
    rows, width = g0.shape
    gload = start_all(load_rows(sc, (g0, g1, g2, g3, g4, g5, g6), gv, gsem))

    @pl.loop(0, rows // BLOCK)
    def _(b):
        at = aligned(b, BLOCK)
        live = (b * BLOCK < sc[LIVE]).astype(F32)
        both = own_gu[at, :] + got_gu[at, :].astype(F32)
        gate, up = both[:, : 2 * HID], both[:, 2 * HID :]
        hidden = (gate * jax.nn.sigmoid(gate) * up).astype(BF).astype(F32)
        scaled = (column(scores[pl.ds(b, 1), :]) * live * hidden).astype(BF)
        transposed_into(st, sc, b, at, slice(0, 2 * HID), scaled)

    wait_all(gload)
    outs = []
    for e in range(EXP):
        for n in range(4):
            at = pl.ds(n * width, width)
            dd[e, :, at] = jnp.dot(st[e], gv[:, at], preferred_element_type=F32).astype(BF)
        outs += start_all(weight_out(sc, dd, 0, e, keep, away, 0, dsem))
    wait_all(outs)


def down_part(sc, scores, own_gu, got_gu, grads):
    rows, width = grads[0].shape
    out = jax.ShapeDtypeStruct((4, 2, 1, EXP, HID, COLS), BF)
    return pl.pallas_call(
        down_kernel,
        out_shape=(out, out),
        in_specs=[SM] + [VM] * 3 + [ANY] * 7,
        out_specs=(ANY, ANY),
        scratch_shapes=[
            pltpu.VMEM((rows, 4 * width), BF),
            pltpu.VMEM((EXP, 2 * HID, rows), BF),
            pltpu.VMEM((EXP, 2 * HID, 4 * width), BF),
            pltpu.SemaphoreType.DMA((8,)),
            pltpu.SemaphoreType.DMA((32,)),
        ],
        compiler_params=pltpu.CompilerParams(vmem_limit_bytes=VMEM),
        cost_estimate=pl.CostEstimate(
            flops=8 * rows * HID * 4 * width, bytes_accessed=14 << 20, transcendentals=rows * 384
        ),
    )(sc, scores, own_gu, got_gu, *grads)


def gate_up_kernel(
    sc, scores, own_gu, got_gu, own_b, got_b, x0, x1, x2, x3, x4, x5, x6,
    sgrad, gu, keep, away, xv, gut, dgu, ogu, ggu, ob, gb, guv, xsem, dsem, isem, usem,
):
    rows, width = x0.shape
    n = 2 * HID
    per = rows // 4
    iload = []
    for t in range(4):
        at = pl.ds(t * per, per)
        for i, (src, dst) in enumerate(((own_gu, ogu), (got_gu, ggu), (own_b, ob), (got_b, gb))):
            iload.append(pltpu.make_async_copy(src.at[at], dst.at[at], isem.at[t * 4 + i]))
    xload = load_rows(sc, (x0, x1, x2, x3, x4, x5, x6), xv, xsem)
    start_all(iload + xload)
    outs = []

    def block(b):
        at = aligned(b, BLOCK)
        live = (b * BLOCK < sc[LIVE]).astype(F32)
        both = ogu[at, :] + ggu[at, :].astype(F32)
        gate, up = both[:, :n], both[:, n:]
        back = ob[at, :] + gb[at, :].astype(F32)
        sig = jax.nn.sigmoid(gate)
        act = gate * sig
        hidden = (act * up).astype(BF).astype(F32)
        mine = (lax.broadcasted_iota(jnp.int32, hidden.shape, 1) >= HID).astype(jnp.int32) == sc[XL]
        total = jnp.sum(jnp.where(mine, hidden * back, 0.0), axis=1, keepdims=True) * live
        sgrad[pl.ds(b, 1), :] = jnp.transpose(jnp.broadcast_to(total, (BLOCK, BLOCK)))[:1]
        hid_grad = column(scores[pl.ds(b, 1), :]) * live * back
        gate_grad = (hid_grad * up * sig * (1.0 + gate * (1.0 - sig))).astype(BF)
        up_grad = (hid_grad * act).astype(BF)
        guv[at, :n] = gate_grad
        guv[at, n:] = up_grad
        transposed_into(gut, sc, b, at, slice(0, n), gate_grad)
        transposed_into(gut, sc, b, at, slice(n, 2 * n), up_grad)

    for t in range(4):
        wait_all(iload[t * 4 : t * 4 + 4])

        @pl.loop(t * per // BLOCK, (t + 1) * per // BLOCK)
        def _(b):
            block(b)

        at = pl.ds(t * per, per)
        outs += start_all([pltpu.make_async_copy(guv.at[at], gu.at[at], usem.at[t])])

    wait_all(xload)
    for e in range(EXP):
        for k in range(4):
            at = pl.ds(k * width, width)
            dgu[e, :, at] = jnp.dot(gut[e], xv[:, at], preferred_element_type=F32).astype(BF)
        for w in range(2):
            outs += start_all(weight_out(sc, dgu, w * n, e, keep, away, w, dsem))
    wait_all(outs)


def gate_up_part(sc, scores, own_gu, got_gu, own_b, got_b, feats):
    rows, width = feats[0].shape
    out = jax.ShapeDtypeStruct((4, 2, 2, EXP, HID, COLS), BF)
    return pl.pallas_call(
        gate_up_kernel,
        out_shape=(
            jax.ShapeDtypeStruct((rows // BLOCK, BLOCK), F32),
            jax.ShapeDtypeStruct((rows, 4 * HID), BF),
            out,
            out,
        ),
        in_specs=[SM, VM] + [ANY] * 11,
        out_specs=(VM, ANY, ANY, ANY),
        scratch_shapes=[
            pltpu.VMEM((rows, 4 * width), BF),
            pltpu.VMEM((EXP, 4 * HID, rows), BF),
            pltpu.VMEM((EXP, 4 * HID, 4 * width), BF),
            pltpu.VMEM((rows, 4 * HID), F32),
            pltpu.VMEM((rows, 4 * HID), BF),
            pltpu.VMEM((rows, 2 * HID), F32),
            pltpu.VMEM((rows, 2 * HID), BF),
            pltpu.VMEM((rows, 4 * HID), BF),
            pltpu.SemaphoreType.DMA((8,)),
            pltpu.SemaphoreType.DMA((64,)),
            pltpu.SemaphoreType.DMA((16,)),
            pltpu.SemaphoreType.DMA((4,)),
        ],
        compiler_params=pltpu.CompilerParams(vmem_limit_bytes=VMEM),
        cost_estimate=pl.CostEstimate(
            flops=16 * rows * HID * 4 * width, bytes_accessed=20 << 20, transcendentals=rows * 384
        ),
    )(sc, scores, own_gu, got_gu, own_b, got_b, *feats)


def rows_kernel(sc, gu, w0, w1, d0, d1, d2, d3, wv, guv, dxv, wsem, usem, osem):
    rows, wide = dxv.shape
    width = wide // 4
    load = load_weight(sc, (w0, w1), 0, 0, wv, wsem, 0) + load_weight(sc, (w0, w1), 1, 2 * HID, wv, wsem, 16)
    load.append(pltpu.make_async_copy(gu, guv, usem.at[0]))
    wait_all(start_all(load))

    def work(start, size, expert):
        at = pl.ds(start, size)
        dxv[at, :] = jnp.dot(guv[at, :], wv[expert], preferred_element_type=F32).astype(BF)

    outs = []
    for t in range(rows // TILE):
        by_tile(sc, t, work)
        at = pl.ds(t * TILE, TILE)
        for p, d in enumerate((d0, d1, d2, d3)):
            where = aligned(y_of(sc, p), width)
            outs += start_all([pltpu.make_async_copy(dxv.at[at, where], d.at[at], osem.at[t * 4 + p])])
    wait_all(outs)


def rows_part(sc, gu, weight):
    rows, width = gu.shape[0], 512
    return pl.pallas_call(
        rows_kernel,
        out_shape=(jax.ShapeDtypeStruct((rows, width), BF),) * 4,
        in_specs=[SM] + [ANY] * 3,
        out_specs=(ANY,) * 4,
        scratch_shapes=[
            pltpu.VMEM((EXP, 4 * HID, 4 * width), BF),
            pltpu.VMEM((rows, 4 * HID), BF),
            pltpu.VMEM((rows, 4 * width), BF),
            pltpu.SemaphoreType.DMA((32,)),
            pltpu.SemaphoreType.DMA((1,)),
            pltpu.SemaphoreType.DMA((16,)),
        ],
        compiler_params=pltpu.CompilerParams(vmem_limit_bytes=VMEM),
        cost_estimate=pl.CostEstimate(
            flops=8 * rows * HID * 4 * width, bytes_accessed=14 << 20, transcendentals=0
        ),
    )(sc, gu, *weight)


def halves_over(x):
    half = x.shape[0] // 2
    near = [lax.ppermute(x[:half], "y", ring(4, k)) for k in (1, 3)]
    rest = [lax.ppermute(x[half:], "y", ring(4, k)) for k in (1, 3)]
    return x, near[0], rest[0], near[1], rest[1]


def opposite_over(pieces):
    return lax.ppermute(pieces[1], "y", ring(4, 1)), lax.ppermute(pieces[4], "y", ring(4, 3))


def to_plane(w):
    return (
        lax.ppermute(w, ("xl", "z", "xh"), swap_pairs(0)),
        lax.ppermute(w, ("xl", "z", "xh"), swap_pairs(1)),
    )


def spread_pair(pair, *before):
    here = after(lax.all_gather(pair, "z", axis=0, tiled=False), *before)
    return here, lax.ppermute(here, "core", ring(2, 1))


def over_cores(keep, got):
    return (keep.astype(F32) + got.astype(F32)).astype(BF)


def over_z(both, z):
    slots = [lax.dynamic_index_in_dim(both, lax.rem(z + k, 4), 0, False) for k in range(4)]
    return slots[:1] + [lax.ppermute(slots[k], "z", ring(4, k)) for k in (1, 3, 2)]


def over_chips(part, xh):
    straight = lax.dynamic_index_in_dim(part, xh, 0, False)
    crossed = lax.dynamic_index_in_dim(part, 1 - xh, 0, False)
    straight = lax.ppermute(straight, ("xl", "z", "xh"), swap_pairs(0))
    crossed = lax.ppermute(crossed, ("xl", "z", "xh"), swap_pairs(1))
    return straight.astype(F32) + crossed.astype(F32)


def on_device(features, grad_out, scores, counts, w_gate, w_up, w_down):
    rows = features.shape[0]
    y, xl, core, xh = (lax.axis_index(a) for a in ("y", "xl", "core", "xh"))
    sc = jnp.stack([y, xl, counts[0, 0], counts[0, 0] + counts[0, 1], core, xh]).astype(jnp.int32)
    scores = scores.reshape(rows // BLOCK, BLOCK)

    feats = halves_over(features)
    feats += opposite_over(feats)
    pair_gu = after(jnp.stack(to_plane(jnp.stack([w_gate, w_up]))), feats[1], feats[3])
    pair_d = jnp.stack(to_plane(after(w_down, feats[2], feats[4])[None]))
    grads = halves_over(after(grad_out, feats[5], feats[6]))
    gu_all = spread_pair(pair_gu, *feats[1:], pair_d, *grads[1:])

    own_gu, send_gu = pre_part(sc, feats, gu_all)
    grads += opposite_over(grads)
    got_gu = lax.ppermute(after(send_gu, grads[5], grads[6]), "xl", ring(2, 1))
    own_b, send_b = pre_part(sc, grads, spread_pair(pair_d, got_gu))
    got_b = lax.ppermute(send_b, "xl", ring(2, 1))

    keep, away = down_part(sc, scores, own_gu, got_gu, grads)
    both_d = over_cores(keep, lax.ppermute(away, "core", ring(2, 1)))
    parts_d = over_z(both_d, lax.axis_index("z"))
    total, gu, keep, away = gate_up_part(
        sc, scores, own_gu, got_gu, own_b, after(got_b, both_d), feats
    )
    got = lax.ppermute(after(away, *parts_d), "core", ring(2, 1))
    total = total + lax.ppermute(total, "y", [(i, i ^ 1) for i in range(4)])
    both = over_cores(after(keep, total), got)
    part = lax.psum_scatter(both, "z", scatter_dimension=0, tiled=False)

    dx = rows_part(sc, after(gu, both), gu_all)
    total = total + after(lax.ppermute(total, "y", [(i, i ^ 2) for i in range(4)]), dx[0])
    dx, _ = lax.optimization_barrier((dx, total))
    total = total + lax.ppermute(total, "xl", ring(2, 1))
    from_below = lax.ppermute(dx[2], "y", ring(4, 1))
    from_above = lax.ppermute(dx[1], "y", ring(4, 3))
    opposite = lax.ppermute(dx[3], "y", ring(4, 2))
    grad_features = (
        (dx[0].astype(F32) + from_below.astype(F32)) + (from_above.astype(F32) + opposite.astype(F32))
    ).astype(BF)

    part_d = sum(p.astype(F32) for p in parts_d).astype(BF)
    grad_down = over_chips(after(part_d, both), xh)
    grad_gu = over_chips(after(part, grad_down), xh)
    return grad_features, total.reshape(rows), grad_gu[0], grad_gu[1], grad_down[0]


def solution(mesh):
    fine = Mesh(mesh.devices.reshape(2, 4, 4, 2, 2), ("xl", "y", "z", "xh", "core"))
    grp, blk = ("xl", "y"), ("z", "xh", "core")
    weight = P(None, grp, blk)
    return jax.shard_map(
        on_device,
        mesh=fine,
        in_specs=(P(blk, grp), P(blk, grp), P(blk), P(blk, None), weight, weight, weight),
        out_specs=(P(blk, grp), P(blk), weight, weight, weight),
        check_vma=False,
    )
```

```python
import functools

import jax
import jax.numpy as jnp
from jax import lax
from jax.experimental import pallas as pl
from jax.experimental.pallas import tpu as pltpu
from jax.sharding import Mesh
from jax.sharding import PartitionSpec as P

EXP = 2
BLOCK = 128
TILE = 256
HID = 192
VMEM = 60 << 20
COLS = 256
BF = jnp.bfloat16
F32 = jnp.float32
NT = (((1,), (1,)), ((), ()))
OFFS = (0, 3, 1, 2)
ANY = pl.BlockSpec(memory_space=pl.ANY)
VM = pl.BlockSpec(memory_space=pltpu.VMEM)
SM = pl.BlockSpec(memory_space=pltpu.SMEM)
Y, XL, FIRST, LIVE, CORE, XH = range(6)


def ring(n, k):
    return [(i, (i + k) % n) for i in range(n)]


def home(xl, z):
    return (xl, z) if z // 2 == xl else (1 - xl, (z + 2) % 4)


def swap_pairs(flip):
    pairs = []
    for xl in range(2):
        for z in range(4):
            for xh in range(2):
                a, b = home(xl, z)
                pairs.append(((xl * 4 + z) * 2 + xh, (a * 4 + b) * 2 + (xh ^ flip)))
    return pairs


def after(x, *others):
    return lax.optimization_barrier((x, *others))[0]


def aligned(i, unit):
    return pl.ds(pl.multiple_of(i * unit, unit), unit)


def y_of(sc, p):
    return lax.rem(sc[Y] + OFFS[p], 4)


def load_rows(sc, pieces, dst, sem):
    rows, width = pieces[0].shape
    half = rows // 2
    copies = []
    for part in range(2):
        some = pl.ds(part * half, half)
        for p in range(4):
            piece = pieces[0].at[some] if p == 0 else pieces[2 * p - 1 + part]
            where = aligned(y_of(sc, p), width)
            copies.append(pltpu.make_async_copy(piece, dst.at[some, where], sem.at[part * 4 + p]))
    return copies


def load_weight(sc, pair, w, row, dst, sem, at_sem):
    copies = []
    for c, ref in enumerate(pair):
        core = sc[CORE] if c == 0 else 1 - sc[CORE]
        for slot in range(4):
            for flip in range(2):
                xh = 1 - sc[XH] if flip else sc[XH]
                cb = slot % 2 * 4 + xh * 2 + core
                copies.append(
                    pltpu.make_async_copy(
                        ref.at[slot, flip, w],
                        dst.at[:, pl.ds(row + slot // 2 * HID, HID), aligned(cb, COLS)],
                        sem.at[at_sem + c * 8 + slot * 2 + flip],
                    )
                )
    return copies


def expert_of(sc, block):
    return (sc[FIRST] <= block * BLOCK).astype(jnp.int32)


def by_tile(sc, tile, work):
    low, high = expert_of(sc, 2 * tile), expert_of(sc, 2 * tile + 1)
    start = tile * TILE

    @pl.when(low == high)
    def _():
        work(start, TILE, low)

    @pl.when(low != high)
    def _():
        work(start, BLOCK, low)
        work(start + BLOCK, BLOCK, high)


def start_all(copies):
    for c in copies:
        c.start()
    return copies


def wait_all(copies):
    for c in copies:
        c.wait()


def pre_kernel(n, sc, x0, x1, x2, x3, x4, x5, x6, w0, w1, own, *rest):
    sends, (xv, wv, ov, sv, xsem, wsem, osem) = rest[:n], rest[n:]
    wload = []
    for w in range(n):
        wload += load_weight(sc, (w0, w1), w, w * 2 * HID, wv, wsem, w * 16)
    xload = load_rows(sc, (x0, x1, x2, x3, x4, x5, x6), xv, xsem)
    start_all(wload + xload)
    wait_all(wload)
    outs = []

    def work(start, size, expert):
        at = pl.ds(start, size)
        part = lax.dot_general(xv[at, :], wv[expert], NT, preferred_element_type=F32)
        ov[at, :] = part
        sv[at, :] = part.astype(BF)

    for t in range(xv.shape[0] // TILE):
        if t % 2 == 0:
            wait_all(xload[t * 2 : t * 2 + 4])
        by_tile(sc, t, work)
        at = pl.ds(t * TILE, TILE)
        outs += start_all([pltpu.make_async_copy(ov.at[at], own.at[at], osem.at[3 * t])])
        for w, send in enumerate(sends):
            some = sv.at[at, pl.ds(w * 2 * HID, 2 * HID)]
            outs += start_all([pltpu.make_async_copy(some, send.at[at], osem.at[3 * t + 1 + w])])
    wait_all(outs)


def pre_part(sc, pieces, weight):
    rows, width = pieces[0].shape
    nw = weight[0].shape[2]
    wide, n = 4 * width, nw * 2 * HID
    return pl.pallas_call(
        functools.partial(pre_kernel, nw),
        out_shape=(jax.ShapeDtypeStruct((rows, n), F32),)
        + (jax.ShapeDtypeStruct((rows, 2 * HID), BF),) * nw,
        in_specs=[SM] + [ANY] * 9,
        out_specs=(ANY,) * (1 + nw),
        scratch_shapes=[
            pltpu.VMEM((rows, wide), BF),
            pltpu.VMEM((EXP, n, wide), BF),
            pltpu.VMEM((rows, n), F32),
            pltpu.VMEM((rows, n), BF),
            pltpu.SemaphoreType.DMA((8,)),
            pltpu.SemaphoreType.DMA((nw * 16,)),
            pltpu.SemaphoreType.DMA((rows // TILE * 3,)),
        ],
        compiler_params=pltpu.CompilerParams(vmem_limit_bytes=VMEM),
        cost_estimate=pl.CostEstimate(
            flops=4 * rows * n * wide, bytes_accessed=10 << 20, transcendentals=0
        ),
    )(sc, *pieces, *weight)


def column(row):
    return jnp.transpose(jnp.broadcast_to(row, (BLOCK, BLOCK)))[:, :1]


def transposed_into(dst, sc, b, at, rows, value):
    expert = expert_of(sc, b)
    dst[expert, rows, at] = jnp.transpose(value)
    dst[1 - expert, rows, at] = jnp.zeros((rows.stop - rows.start, BLOCK), value.dtype)


def weight_out(sc, src, row, e, keep, away, w, sem):
    outs = []
    for rel, out in enumerate((keep, away)):
        core = sc[CORE] if rel == 0 else 1 - sc[CORE]
        for h in range(2):
            for zz in range(2):
                for xh in range(2):
                    i = (((w * EXP + e) * 2 + rel) * 2 + h) * 4 + zz * 2 + xh
                    outs.append(
                        pltpu.make_async_copy(
                            src.at[e, pl.ds(row + h * HID, HID), aligned((zz * 2 + xh) * 2 + core, COLS)],
                            out.at[h * 2 + zz, xh, w, e],
                            sem.at[i],
                        )
                    )
    return outs


def down_kernel(
    sc, scores, own_gu, got_g, got_u, g0, g1, g2, g3, g4, g5, g6, keep, away, gv, st, dd, gsem, dsem
):
    rows, width = g0.shape
    gload = start_all(load_rows(sc, (g0, g1, g2, g3, g4, g5, g6), gv, gsem))

    @pl.loop(0, rows // BLOCK)
    def _(b):
        at = aligned(b, BLOCK)
        live = (b * BLOCK < sc[LIVE]).astype(F32)
        gate = own_gu[at, : 2 * HID] + got_g[at, :].astype(F32)
        up = own_gu[at, 2 * HID :] + got_u[at, :].astype(F32)
        hidden = (gate * jax.nn.sigmoid(gate) * up).astype(BF).astype(F32)
        scaled = (column(scores[pl.ds(b, 1), :]) * live * hidden).astype(BF)
        transposed_into(st, sc, b, at, slice(0, 2 * HID), scaled)

    wait_all(gload)
    outs = []
    for e in range(EXP):
        for n in range(4):
            at = pl.ds(n * width, width)
            dd[e, :, at] = jnp.dot(st[e], gv[:, at], preferred_element_type=F32).astype(BF)
        outs += start_all(weight_out(sc, dd, 0, e, keep, away, 0, dsem))
    wait_all(outs)


def down_part(sc, scores, own_gu, got_g, got_u, grads):
    rows, width = grads[0].shape
    out = jax.ShapeDtypeStruct((4, 2, 1, EXP, HID, COLS), BF)
    return pl.pallas_call(
        down_kernel,
        out_shape=(out, out),
        in_specs=[SM] + [VM] * 4 + [ANY] * 7,
        out_specs=(ANY, ANY),
        scratch_shapes=[
            pltpu.VMEM((rows, 4 * width), BF),
            pltpu.VMEM((EXP, 2 * HID, rows), BF),
            pltpu.VMEM((EXP, 2 * HID, 4 * width), BF),
            pltpu.SemaphoreType.DMA((8,)),
            pltpu.SemaphoreType.DMA((32,)),
        ],
        compiler_params=pltpu.CompilerParams(vmem_limit_bytes=VMEM),
        cost_estimate=pl.CostEstimate(
            flops=8 * rows * HID * 4 * width, bytes_accessed=14 << 20, transcendentals=rows * 384
        ),
    )(sc, scores, own_gu, got_g, got_u, *grads)


def gate_up_kernel(
    sc, scores, own_gu, got_g, got_u, own_b, got_b, x0, x1, x2, x3, x4, x5, x6,
    sgrad, gu, keep, away, xv, gut, dgu, ogu, gg, gup, ob, gb, guv, xsem, dsem, isem, usem,
):
    rows, width = x0.shape
    n = 2 * HID
    per = rows // 4
    iload = []
    for t in range(4):
        at = pl.ds(t * per, per)
        for i, (src, dst) in enumerate(((own_gu, ogu), (got_g, gg), (got_u, gup), (own_b, ob), (got_b, gb))):
            iload.append(pltpu.make_async_copy(src.at[at], dst.at[at], isem.at[t * 5 + i]))
    xload = load_rows(sc, (x0, x1, x2, x3, x4, x5, x6), xv, xsem)
    start_all(iload + xload)
    outs = []

    def block(b):
        at = aligned(b, BLOCK)
        live = (b * BLOCK < sc[LIVE]).astype(F32)
        gate = ogu[at, :n] + gg[at, :].astype(F32)
        up = ogu[at, n:] + gup[at, :].astype(F32)
        back = ob[at, :] + gb[at, :].astype(F32)
        sig = jax.nn.sigmoid(gate)
        act = gate * sig
        hidden = (act * up).astype(BF).astype(F32)
        mine = (lax.broadcasted_iota(jnp.int32, hidden.shape, 1) >= HID).astype(jnp.int32) == sc[XL]
        total = jnp.sum(jnp.where(mine, hidden * back, 0.0), axis=1, keepdims=True) * live
        sgrad[pl.ds(b, 1), :] = jnp.transpose(jnp.broadcast_to(total, (BLOCK, BLOCK)))[:1]
        hid_grad = column(scores[pl.ds(b, 1), :]) * live * back
        gate_grad = (hid_grad * up * sig * (1.0 + gate * (1.0 - sig))).astype(BF)
        up_grad = (hid_grad * act).astype(BF)
        guv[at, :n] = gate_grad
        guv[at, n:] = up_grad
        transposed_into(gut, sc, b, at, slice(0, n), gate_grad)
        transposed_into(gut, sc, b, at, slice(n, 2 * n), up_grad)

    for t in range(4):
        wait_all(iload[t * 5 : t * 5 + 5])

        @pl.loop(t * per // BLOCK, (t + 1) * per // BLOCK)
        def _(b):
            block(b)

        at = pl.ds(t * per, per)
        outs += start_all([pltpu.make_async_copy(guv.at[at], gu.at[at], usem.at[t])])

    wait_all(xload)
    for e in range(EXP):
        for k in range(4):
            at = pl.ds(k * width, width)
            dgu[e, :, at] = jnp.dot(gut[e], xv[:, at], preferred_element_type=F32).astype(BF)
        for w in range(2):
            outs += start_all(weight_out(sc, dgu, w * n, e, keep, away, w, dsem))
    wait_all(outs)


def gate_up_part(sc, scores, own_gu, got_g, got_u, own_b, got_b, feats):
    rows, width = feats[0].shape
    out = jax.ShapeDtypeStruct((4, 2, 2, EXP, HID, COLS), BF)
    return pl.pallas_call(
        gate_up_kernel,
        out_shape=(
            jax.ShapeDtypeStruct((rows // BLOCK, BLOCK), F32),
            jax.ShapeDtypeStruct((rows, 4 * HID), BF),
            out,
            out,
        ),
        in_specs=[SM, VM] + [ANY] * 12,
        out_specs=(VM, ANY, ANY, ANY),
        scratch_shapes=[
            pltpu.VMEM((rows, 4 * width), BF),
            pltpu.VMEM((EXP, 4 * HID, rows), BF),
            pltpu.VMEM((EXP, 4 * HID, 4 * width), BF),
            pltpu.VMEM((rows, 4 * HID), F32),
            pltpu.VMEM((rows, 2 * HID), BF),
            pltpu.VMEM((rows, 2 * HID), BF),
            pltpu.VMEM((rows, 2 * HID), F32),
            pltpu.VMEM((rows, 2 * HID), BF),
            pltpu.VMEM((rows, 4 * HID), BF),
            pltpu.SemaphoreType.DMA((8,)),
            pltpu.SemaphoreType.DMA((64,)),
            pltpu.SemaphoreType.DMA((20,)),
            pltpu.SemaphoreType.DMA((4,)),
        ],
        compiler_params=pltpu.CompilerParams(vmem_limit_bytes=VMEM),
        cost_estimate=pl.CostEstimate(
            flops=16 * rows * HID * 4 * width, bytes_accessed=20 << 20, transcendentals=rows * 384
        ),
    )(sc, scores, own_gu, got_g, got_u, own_b, got_b, *feats)


def rows_kernel(sc, gu, w0, w1, d0, d1, d2, d3, wv, guv, dxv, wsem, usem, osem):
    rows, wide = dxv.shape
    width = wide // 4
    load = load_weight(sc, (w0, w1), 0, 0, wv, wsem, 0) + load_weight(sc, (w0, w1), 1, 2 * HID, wv, wsem, 16)
    load.append(pltpu.make_async_copy(gu, guv, usem.at[0]))
    wait_all(start_all(load))

    def work(start, size, expert):
        at = pl.ds(start, size)
        dxv[at, :] = jnp.dot(guv[at, :], wv[expert], preferred_element_type=F32).astype(BF)

    outs = []
    for t in range(rows // TILE):
        by_tile(sc, t, work)
        at = pl.ds(t * TILE, TILE)
        for p, d in enumerate((d0, d1, d2, d3)):
            where = aligned(y_of(sc, p), width)
            outs += start_all([pltpu.make_async_copy(dxv.at[at, where], d.at[at], osem.at[t * 4 + p])])
    wait_all(outs)


def rows_part(sc, gu, weight):
    rows, width = gu.shape[0], 512
    return pl.pallas_call(
        rows_kernel,
        out_shape=(jax.ShapeDtypeStruct((rows, width), BF),) * 4,
        in_specs=[SM] + [ANY] * 3,
        out_specs=(ANY,) * 4,
        scratch_shapes=[
            pltpu.VMEM((EXP, 4 * HID, 4 * width), BF),
            pltpu.VMEM((rows, 4 * HID), BF),
            pltpu.VMEM((rows, 4 * width), BF),
            pltpu.SemaphoreType.DMA((32,)),
            pltpu.SemaphoreType.DMA((1,)),
            pltpu.SemaphoreType.DMA((16,)),
        ],
        compiler_params=pltpu.CompilerParams(vmem_limit_bytes=VMEM),
        cost_estimate=pl.CostEstimate(
            flops=8 * rows * HID * 4 * width, bytes_accessed=14 << 20, transcendentals=0
        ),
    )(sc, gu, *weight)


def halves_over(x):
    half = x.shape[0] // 2
    near = [lax.ppermute(x[:half], "y", ring(4, k)) for k in (1, 3)]
    rest = [lax.ppermute(x[half:], "y", ring(4, k)) for k in (1, 3)]
    return x, near[0], rest[0], near[1], rest[1]


def opposite_over(pieces):
    return lax.ppermute(pieces[1], "y", ring(4, 1)), lax.ppermute(pieces[4], "y", ring(4, 3))


def to_plane(w):
    return (
        lax.ppermute(w, ("xl", "z", "xh"), swap_pairs(0)),
        lax.ppermute(w, ("xl", "z", "xh"), swap_pairs(1)),
    )


def spread_pair(pair, *before):
    here = after(lax.all_gather(pair, "z", axis=0, tiled=False), *before)
    return here, lax.ppermute(here, "core", ring(2, 1))


def over_cores(keep, got):
    return (keep.astype(F32) + got.astype(F32)).astype(BF)


def over_z(both, z):
    slots = [lax.dynamic_index_in_dim(both, lax.rem(z + k, 4), 0, False) for k in range(4)]
    return slots[:1] + [lax.ppermute(slots[k], "z", ring(4, k)) for k in (1, 3, 2)]


def over_chips(part, xh):
    straight = lax.dynamic_index_in_dim(part, xh, 0, False)
    crossed = lax.dynamic_index_in_dim(part, 1 - xh, 0, False)
    straight = lax.ppermute(straight, ("xl", "z", "xh"), swap_pairs(0))
    crossed = lax.ppermute(crossed, ("xl", "z", "xh"), swap_pairs(1))
    return straight.astype(F32) + crossed.astype(F32)


def on_device(features, grad_out, scores, counts, w_gate, w_up, w_down):
    rows = features.shape[0]
    y, xl, core, xh = (lax.axis_index(a) for a in ("y", "xl", "core", "xh"))
    sc = jnp.stack([y, xl, counts[0, 0], counts[0, 0] + counts[0, 1], core, xh]).astype(jnp.int32)
    scores = scores.reshape(rows // BLOCK, BLOCK)

    feats = halves_over(features)
    feats += opposite_over(feats)
    pair_gu = after(jnp.stack(to_plane(jnp.stack([w_gate, w_up]))), feats[1], feats[3])
    pair_d = jnp.stack(to_plane(after(w_down, feats[2], feats[4])[None]))
    grads = halves_over(after(grad_out, feats[5], feats[6]))
    gu_all = spread_pair(pair_gu, *feats[1:], pair_d, grads[1], grads[3])

    own_gu, send_g, send_u = pre_part(sc, feats, gu_all)
    got_g = lax.ppermute(after(send_g, grads[2], grads[4]), "xl", ring(2, 1))
    got_u = lax.ppermute(send_u, "xl", ring(2, 1))
    grads += opposite_over(grads)
    own_b, send_b = pre_part(sc, grads, spread_pair(pair_d, got_g))
    got_b = lax.ppermute(send_b, "xl", ring(2, 1))

    keep, away = down_part(after(sc, send_b), scores, own_gu, got_g, got_u, grads)
    both_d = over_cores(keep, lax.ppermute(away, "core", ring(2, 1)))
    parts_d = over_z(both_d, lax.axis_index("z"))
    total, gu, keep, away = gate_up_part(
        sc, scores, own_gu, got_g, got_u, own_b, after(got_b, both_d), feats
    )
    got = lax.ppermute(after(away, *parts_d), "core", ring(2, 1))
    total = total + lax.ppermute(total, "y", [(i, i ^ 1) for i in range(4)])
    both = over_cores(after(keep, total), got)
    part = lax.psum_scatter(both, "z", scatter_dimension=0, tiled=False)

    dx = rows_part(sc, after(gu, both), gu_all)
    total = total + after(lax.ppermute(total, "y", [(i, i ^ 2) for i in range(4)]), dx[0])
    dx, _ = lax.optimization_barrier((dx, total))
    total = total + lax.ppermute(total, "xl", ring(2, 1))
    from_below = lax.ppermute(dx[2], "y", ring(4, 1))
    from_above = lax.ppermute(dx[1], "y", ring(4, 3))
    opposite = lax.ppermute(dx[3], "y", ring(4, 2))
    grad_features = (
        (dx[0].astype(F32) + from_below.astype(F32)) + (from_above.astype(F32) + opposite.astype(F32))
    ).astype(BF)

    part_d = sum(p.astype(F32) for p in parts_d).astype(BF)
    grad_down = over_chips(after(part_d, both), xh)
    grad_gu = over_chips(after(part, grad_down), xh)
    return grad_features, total.reshape(rows), grad_gu[0], grad_gu[1], grad_down[0]


def solution(mesh):
    fine = Mesh(mesh.devices.reshape(2, 4, 4, 2, 2), ("xl", "y", "z", "xh", "core"))
    grp, blk = ("xl", "y"), ("z", "xh", "core")
    weight = P(None, grp, blk)
    return jax.shard_map(
        on_device,
        mesh=fine,
        in_specs=(P(blk, grp), P(blk, grp), P(blk), P(blk, None), weight, weight, weight),
        out_specs=(P(blk, grp), P(blk), weight, weight, weight),
        check_vma=False,
    )
```

```python
import functools

import jax
import jax.numpy as jnp
from jax import lax
from jax.experimental import pallas as pl
from jax.experimental.pallas import tpu as pltpu
from jax.sharding import Mesh
from jax.sharding import PartitionSpec as P

EXP = 2
BLOCK = 128
TILE = 256
HID = 192
VMEM = 60 << 20
COLS = 256
BF = jnp.bfloat16
F32 = jnp.float32
NT = (((1,), (1,)), ((), ()))
OFFS = (0, 3, 1, 2)
ANY = pl.BlockSpec(memory_space=pl.ANY)
VM = pl.BlockSpec(memory_space=pltpu.VMEM)
SM = pl.BlockSpec(memory_space=pltpu.SMEM)
Y, XL, FIRST, LIVE, CORE, XH = range(6)


def ring(n, k):
    return [(i, (i + k) % n) for i in range(n)]


def home(xl, z):
    return (xl, z) if z // 2 == xl else (1 - xl, (z + 2) % 4)


def swap_pairs(flip):
    pairs = []
    for xl in range(2):
        for z in range(4):
            for xh in range(2):
                a, b = home(xl, z)
                pairs.append(((xl * 4 + z) * 2 + xh, (a * 4 + b) * 2 + (xh ^ flip)))
    return pairs


def after(x, *others):
    return lax.optimization_barrier((x, *others))[0]


def aligned(i, unit):
    return pl.ds(pl.multiple_of(i * unit, unit), unit)


def y_of(sc, p):
    return lax.rem(sc[Y] + OFFS[p], 4)


def load_rows(sc, pieces, dst, sem):
    rows, width = pieces[0].shape
    half = rows // 2
    copies = []
    for part in range(2):
        some = pl.ds(part * half, half)
        for p in range(4):
            piece = pieces[0].at[some] if p == 0 else pieces[2 * p - 1 + part]
            where = aligned(y_of(sc, p), width)
            copies.append(pltpu.make_async_copy(piece, dst.at[some, where], sem.at[part * 4 + p]))
    return copies


def load_weight(sc, pair, w, row, dst, sem, at_sem):
    copies = []
    for c, ref in enumerate(pair):
        core = sc[CORE] if c == 0 else 1 - sc[CORE]
        for slot in range(4):
            for flip in range(2):
                xh = 1 - sc[XH] if flip else sc[XH]
                cb = slot % 2 * 4 + xh * 2 + core
                copies.append(
                    pltpu.make_async_copy(
                        ref.at[slot, flip, w],
                        dst.at[:, pl.ds(row + slot // 2 * HID, HID), aligned(cb, COLS)],
                        sem.at[at_sem + c * 8 + slot * 2 + flip],
                    )
                )
    return copies


def expert_of(sc, block):
    return (sc[FIRST] <= block * BLOCK).astype(jnp.int32)


def by_tile(sc, tile, work):
    low, high = expert_of(sc, 2 * tile), expert_of(sc, 2 * tile + 1)
    start = tile * TILE

    @pl.when(low == high)
    def _():
        work(start, TILE, low)

    @pl.when(low != high)
    def _():
        work(start, BLOCK, low)
        work(start + BLOCK, BLOCK, high)


def start_all(copies):
    for c in copies:
        c.start()
    return copies


def wait_all(copies):
    for c in copies:
        c.wait()


def pre_kernel(n, sc, x0, x1, x2, x3, x4, x5, x6, w0, w1, own, *rest):
    sends, (xv, wv, ov, sv, xsem, wsem, osem) = rest[:n], rest[n:]
    wload = []
    for w in range(n):
        wload += load_weight(sc, (w0, w1), w, w * 2 * HID, wv, wsem, w * 16)
    xload = load_rows(sc, (x0, x1, x2, x3, x4, x5, x6), xv, xsem)
    start_all(wload + xload)
    wait_all(wload)
    outs = []

    def work(start, size, expert):
        at = pl.ds(start, size)
        part = lax.dot_general(xv[at, :], wv[expert], NT, preferred_element_type=F32)
        ov[at, :] = part
        sv[at, :] = part.astype(BF)

    for t in range(xv.shape[0] // TILE):
        if t % 2 == 0:
            wait_all(xload[t * 2 : t * 2 + 4])
        by_tile(sc, t, work)
        at = pl.ds(t * TILE, TILE)
        outs += start_all([pltpu.make_async_copy(ov.at[at], own.at[at], osem.at[3 * t])])
        for w, send in enumerate(sends):
            some = sv.at[at, pl.ds(w * 2 * HID, 2 * HID)]
            outs += start_all([pltpu.make_async_copy(some, send.at[at], osem.at[3 * t + 1 + w])])
    wait_all(outs)


def pre_part(sc, pieces, weight):
    rows, width = pieces[0].shape
    nw = weight[0].shape[2]
    wide, n = 4 * width, nw * 2 * HID
    return pl.pallas_call(
        functools.partial(pre_kernel, nw),
        out_shape=(jax.ShapeDtypeStruct((rows, n), F32),)
        + (jax.ShapeDtypeStruct((rows, 2 * HID), BF),) * nw,
        in_specs=[SM] + [ANY] * 9,
        out_specs=(ANY,) * (1 + nw),
        scratch_shapes=[
            pltpu.VMEM((rows, wide), BF),
            pltpu.VMEM((EXP, n, wide), BF),
            pltpu.VMEM((rows, n), F32),
            pltpu.VMEM((rows, n), BF),
            pltpu.SemaphoreType.DMA((8,)),
            pltpu.SemaphoreType.DMA((nw * 16,)),
            pltpu.SemaphoreType.DMA((rows // TILE * 3,)),
        ],
        compiler_params=pltpu.CompilerParams(vmem_limit_bytes=VMEM),
        cost_estimate=pl.CostEstimate(
            flops=4 * rows * n * wide, bytes_accessed=10 << 20, transcendentals=0
        ),
    )(sc, *pieces, *weight)


def column(row):
    return jnp.transpose(jnp.broadcast_to(row, (BLOCK, BLOCK)))[:, :1]


def transposed_into(dst, sc, b, at, rows, value):
    expert = expert_of(sc, b)
    dst[expert, rows, at] = jnp.transpose(value)
    dst[1 - expert, rows, at] = jnp.zeros((rows.stop - rows.start, BLOCK), value.dtype)


def weight_out(sc, src, row, e, keep, away, w, sem):
    outs = []
    for rel, out in enumerate((keep, away)):
        core = sc[CORE] if rel == 0 else 1 - sc[CORE]
        for h in range(2):
            for zz in range(2):
                for xh in range(2):
                    i = (((w * EXP + e) * 2 + rel) * 2 + h) * 4 + zz * 2 + xh
                    outs.append(
                        pltpu.make_async_copy(
                            src.at[e, pl.ds(row + h * HID, HID), aligned((zz * 2 + xh) * 2 + core, COLS)],
                            out.at[h * 2 + zz, xh, w, e],
                            sem.at[i],
                        )
                    )
    return outs


def down_kernel(
    sc, scores, own_gu, got_g, got_u, g0, g1, g2, g3, g4, g5, g6, keep, away, gv, st, dd, gsem, dsem
):
    rows, width = g0.shape
    gload = start_all(load_rows(sc, (g0, g1, g2, g3, g4, g5, g6), gv, gsem))

    @pl.loop(0, rows // BLOCK)
    def _(b):
        at = aligned(b, BLOCK)
        live = (b * BLOCK < sc[LIVE]).astype(F32)
        gate = own_gu[at, : 2 * HID] + got_g[at, :].astype(F32)
        up = own_gu[at, 2 * HID :] + got_u[at, :].astype(F32)
        hidden = (gate * jax.nn.sigmoid(gate) * up).astype(BF).astype(F32)
        scaled = (column(scores[pl.ds(b, 1), :]) * live * hidden).astype(BF)
        transposed_into(st, sc, b, at, slice(0, 2 * HID), scaled)

    wait_all(gload)
    outs = []
    for e in range(EXP):
        for n in range(4):
            at = pl.ds(n * width, width)
            dd[e, :, at] = jnp.dot(st[e], gv[:, at], preferred_element_type=F32).astype(BF)
        outs += start_all(weight_out(sc, dd, 0, e, keep, away, 0, dsem))
    wait_all(outs)


def down_part(sc, scores, own_gu, got_g, got_u, grads):
    rows, width = grads[0].shape
    out = jax.ShapeDtypeStruct((4, 2, 1, EXP, HID, COLS), BF)
    return pl.pallas_call(
        down_kernel,
        out_shape=(out, out),
        in_specs=[SM] + [VM] * 4 + [ANY] * 7,
        out_specs=(ANY, ANY),
        scratch_shapes=[
            pltpu.VMEM((rows, 4 * width), BF),
            pltpu.VMEM((EXP, 2 * HID, rows), BF),
            pltpu.VMEM((EXP, 2 * HID, 4 * width), BF),
            pltpu.SemaphoreType.DMA((8,)),
            pltpu.SemaphoreType.DMA((32,)),
        ],
        compiler_params=pltpu.CompilerParams(vmem_limit_bytes=VMEM),
        cost_estimate=pl.CostEstimate(
            flops=8 * rows * HID * 4 * width, bytes_accessed=14 << 20, transcendentals=rows * 384
        ),
    )(sc, scores, own_gu, got_g, got_u, *grads)


def gate_up_kernel(
    sc, scores, own_gu, got_g, got_u, own_b, got_b, x0, x1, x2, x3, x4, x5, x6,
    sgrad, gu, keep, away, xv, gut, dgu, ogu, gg, gup, ob, gb, guv, xsem, dsem, isem, usem,
):
    rows, width = x0.shape
    n = 2 * HID
    per = rows // 4
    iload = []
    for t in range(4):
        at = pl.ds(t * per, per)
        for i, (src, dst) in enumerate(((own_gu, ogu), (got_g, gg), (got_u, gup), (own_b, ob), (got_b, gb))):
            iload.append(pltpu.make_async_copy(src.at[at], dst.at[at], isem.at[t * 5 + i]))
    xload = load_rows(sc, (x0, x1, x2, x3, x4, x5, x6), xv, xsem)
    start_all(iload + xload)
    outs = []

    def block(b):
        at = aligned(b, BLOCK)
        live = (b * BLOCK < sc[LIVE]).astype(F32)
        gate = ogu[at, :n] + gg[at, :].astype(F32)
        up = ogu[at, n:] + gup[at, :].astype(F32)
        back = ob[at, :] + gb[at, :].astype(F32)
        sig = jax.nn.sigmoid(gate)
        act = gate * sig
        hidden = (act * up).astype(BF).astype(F32)
        mine = (lax.broadcasted_iota(jnp.int32, hidden.shape, 1) >= HID).astype(jnp.int32) == sc[XL]
        total = jnp.sum(jnp.where(mine, hidden * back, 0.0), axis=1, keepdims=True) * live
        sgrad[pl.ds(b, 1), :] = jnp.transpose(jnp.broadcast_to(total, (BLOCK, BLOCK)))[:1]
        hid_grad = column(scores[pl.ds(b, 1), :]) * live * back
        gate_grad = (hid_grad * up * sig * (1.0 + gate * (1.0 - sig))).astype(BF)
        up_grad = (hid_grad * act).astype(BF)
        guv[at, :n] = gate_grad
        guv[at, n:] = up_grad
        transposed_into(gut, sc, b, at, slice(0, n), gate_grad)
        transposed_into(gut, sc, b, at, slice(n, 2 * n), up_grad)

    for t in range(4):
        wait_all(iload[t * 5 : t * 5 + 5])

        @pl.loop(t * per // BLOCK, (t + 1) * per // BLOCK)
        def _(b):
            block(b)

        at = pl.ds(t * per, per)
        outs += start_all([pltpu.make_async_copy(guv.at[at], gu.at[at], usem.at[t])])

    wait_all(xload)
    for e in range(EXP):
        for k in range(4):
            at = pl.ds(k * width, width)
            dgu[e, :, at] = jnp.dot(gut[e], xv[:, at], preferred_element_type=F32).astype(BF)
        for w in range(2):
            outs += start_all(weight_out(sc, dgu, w * n, e, keep, away, w, dsem))
    wait_all(outs)


def gate_up_part(sc, scores, own_gu, got_g, got_u, own_b, got_b, feats):
    rows, width = feats[0].shape
    out = jax.ShapeDtypeStruct((4, 2, 2, EXP, HID, COLS), BF)
    return pl.pallas_call(
        gate_up_kernel,
        out_shape=(
            jax.ShapeDtypeStruct((rows // BLOCK, BLOCK), F32),
            jax.ShapeDtypeStruct((rows, 4 * HID), BF),
            out,
            out,
        ),
        in_specs=[SM, VM] + [ANY] * 12,
        out_specs=(VM, ANY, ANY, ANY),
        scratch_shapes=[
            pltpu.VMEM((rows, 4 * width), BF),
            pltpu.VMEM((EXP, 4 * HID, rows), BF),
            pltpu.VMEM((EXP, 4 * HID, 4 * width), BF),
            pltpu.VMEM((rows, 4 * HID), F32),
            pltpu.VMEM((rows, 2 * HID), BF),
            pltpu.VMEM((rows, 2 * HID), BF),
            pltpu.VMEM((rows, 2 * HID), F32),
            pltpu.VMEM((rows, 2 * HID), BF),
            pltpu.VMEM((rows, 4 * HID), BF),
            pltpu.SemaphoreType.DMA((8,)),
            pltpu.SemaphoreType.DMA((64,)),
            pltpu.SemaphoreType.DMA((20,)),
            pltpu.SemaphoreType.DMA((4,)),
        ],
        compiler_params=pltpu.CompilerParams(vmem_limit_bytes=VMEM),
        cost_estimate=pl.CostEstimate(
            flops=16 * rows * HID * 4 * width, bytes_accessed=20 << 20, transcendentals=rows * 384
        ),
    )(sc, scores, own_gu, got_g, got_u, own_b, got_b, *feats)


def rows_kernel(sc, gu, w0, w1, d0, d1, d2, d3, wv, guv, dxv, wsem, usem, osem):
    rows, wide = dxv.shape
    width = wide // 4
    load = load_weight(sc, (w0, w1), 0, 0, wv, wsem, 0) + load_weight(sc, (w0, w1), 1, 2 * HID, wv, wsem, 16)
    load.append(pltpu.make_async_copy(gu, guv, usem.at[0]))
    wait_all(start_all(load))

    def work(start, size, expert):
        at = pl.ds(start, size)
        dxv[at, :] = jnp.dot(guv[at, :], wv[expert], preferred_element_type=F32).astype(BF)

    outs = []
    for t in range(rows // TILE):
        by_tile(sc, t, work)
        at = pl.ds(t * TILE, TILE)
        for p, d in enumerate((d0, d1, d2, d3)):
            where = aligned(y_of(sc, p), width)
            outs += start_all([pltpu.make_async_copy(dxv.at[at, where], d.at[at], osem.at[t * 4 + p])])
    wait_all(outs)


def rows_part(sc, gu, weight):
    rows, width = gu.shape[0], 512
    return pl.pallas_call(
        rows_kernel,
        out_shape=(jax.ShapeDtypeStruct((rows, width), BF),) * 4,
        in_specs=[SM] + [ANY] * 3,
        out_specs=(ANY,) * 4,
        scratch_shapes=[
            pltpu.VMEM((EXP, 4 * HID, 4 * width), BF),
            pltpu.VMEM((rows, 4 * HID), BF),
            pltpu.VMEM((rows, 4 * width), BF),
            pltpu.SemaphoreType.DMA((32,)),
            pltpu.SemaphoreType.DMA((1,)),
            pltpu.SemaphoreType.DMA((16,)),
        ],
        compiler_params=pltpu.CompilerParams(vmem_limit_bytes=VMEM),
        cost_estimate=pl.CostEstimate(
            flops=8 * rows * HID * 4 * width, bytes_accessed=14 << 20, transcendentals=0
        ),
    )(sc, gu, *weight)


def halves_over(x):
    half = x.shape[0] // 2
    near = [lax.ppermute(x[:half], "y", ring(4, k)) for k in (1, 3)]
    rest = [lax.ppermute(x[half:], "y", ring(4, k)) for k in (1, 3)]
    return x, near[0], rest[0], near[1], rest[1]


def opposite_over(pieces):
    return lax.ppermute(pieces[1], "y", ring(4, 1)), lax.ppermute(pieces[4], "y", ring(4, 3))


def to_plane(w):
    return (
        lax.ppermute(w, ("xl", "z", "xh"), swap_pairs(0)),
        lax.ppermute(w, ("xl", "z", "xh"), swap_pairs(1)),
    )


def spread_pair(pair, *before):
    here = after(lax.all_gather(pair, "z", axis=0, tiled=False), *before)
    return here, lax.ppermute(here, "core", ring(2, 1))


def over_cores(keep, got):
    return (keep.astype(F32) + got.astype(F32)).astype(BF)


def over_z(both, z):
    slots = [lax.dynamic_index_in_dim(both, lax.rem(z + k, 4), 0, False) for k in range(4)]
    return slots[:1] + [lax.ppermute(slots[k], "z", ring(4, k)) for k in (1, 3, 2)]


def over_chips(part, xh):
    straight = lax.dynamic_index_in_dim(part, xh, 0, False)
    crossed = lax.dynamic_index_in_dim(part, 1 - xh, 0, False)
    straight = lax.ppermute(straight, ("xl", "z", "xh"), swap_pairs(0))
    crossed = lax.ppermute(crossed, ("xl", "z", "xh"), swap_pairs(1))
    return straight.astype(F32) + crossed.astype(F32)


def on_device(features, grad_out, scores, counts, w_gate, w_up, w_down):
    rows = features.shape[0]
    y, xl, core, xh = (lax.axis_index(a) for a in ("y", "xl", "core", "xh"))
    sc = jnp.stack([y, xl, counts[0, 0], counts[0, 0] + counts[0, 1], core, xh]).astype(jnp.int32)
    scores = scores.reshape(rows // BLOCK, BLOCK)

    feats = halves_over(features)
    feats += opposite_over(feats)
    pair_gu = after(jnp.stack(to_plane(jnp.stack([w_gate, w_up]))), feats[1], feats[3])
    pair_d = jnp.stack(to_plane(after(w_down, feats[2], feats[4])[None]))
    grads = halves_over(after(grad_out, feats[5], feats[6]))
    gu_all = spread_pair(pair_gu, *feats[1:], pair_d, grads[1], grads[3])

    own_gu, send_g, send_u = pre_part(sc, feats, gu_all)
    got_g = lax.ppermute(send_g, "xl", ring(2, 1))
    got_u = lax.ppermute(send_u, "xl", ring(2, 1))
    grads += opposite_over(grads)
    own_b, send_b = pre_part(sc, grads, spread_pair(pair_d, got_g, *grads[2:]))
    got_b = lax.ppermute(send_b, "xl", ring(2, 1))

    keep, away = down_part(after(sc, send_b), scores, own_gu, got_g, got_u, grads)
    got_b = after(got_b, away)
    both_d = over_cores(keep, lax.ppermute(away, "core", ring(2, 1)))
    parts_d = over_z(both_d, lax.axis_index("z"))
    total, gu, keep, away = gate_up_part(
        sc, scores, own_gu, got_g, got_u, own_b, got_b, feats
    )
    got = lax.ppermute(away, "core", ring(2, 1))
    total = total + lax.ppermute(total, "y", [(i, i ^ 1) for i in range(4)])
    both = over_cores(after(keep, total, both_d), got)
    part = lax.psum_scatter(both, "z", scatter_dimension=0, tiled=False)

    dx = rows_part(sc, after(gu, both), gu_all)
    total = total + after(lax.ppermute(total, "y", [(i, i ^ 2) for i in range(4)]), dx[0])
    dx, _ = lax.optimization_barrier((dx, total))
    total = total + lax.ppermute(total, "xl", ring(2, 1))
    from_below = lax.ppermute(dx[2], "y", ring(4, 1))
    from_above = lax.ppermute(dx[1], "y", ring(4, 3))
    opposite = lax.ppermute(dx[3], "y", ring(4, 2))
    grad_features = (
        (dx[0].astype(F32) + from_below.astype(F32)) + (from_above.astype(F32) + opposite.astype(F32))
    ).astype(BF)

    part_d = sum(p.astype(F32) for p in parts_d).astype(BF)
    grad_down = over_chips(after(part_d, both), xh)
    grad_gu = over_chips(after(part, grad_down), xh)
    return grad_features, total.reshape(rows), grad_gu[0], grad_gu[1], grad_down[0]


def solution(mesh):
    fine = Mesh(mesh.devices.reshape(2, 4, 4, 2, 2), ("xl", "y", "z", "xh", "core"))
    grp, blk = ("xl", "y"), ("z", "xh", "core")
    weight = P(None, grp, blk)
    return jax.shard_map(
        on_device,
        mesh=fine,
        in_specs=(P(blk, grp), P(blk, grp), P(blk), P(blk, None), weight, weight, weight),
        out_specs=(P(blk, grp), P(blk), weight, weight, weight),
        check_vma=False,
    )
```

```python
import functools

import jax
import jax.numpy as jnp
from jax import lax
from jax.experimental import pallas as pl
from jax.experimental.pallas import tpu as pltpu
from jax.sharding import Mesh
from jax.sharding import PartitionSpec as P

EXP = 2
BLOCK = 128
TILE = 256
HID = 192
VMEM = 60 << 20
COLS = 256
BF = jnp.bfloat16
F32 = jnp.float32
NT = (((1,), (1,)), ((), ()))
OFFS = (0, 3, 1, 2)
ANY = pl.BlockSpec(memory_space=pl.ANY)
VM = pl.BlockSpec(memory_space=pltpu.VMEM)
SM = pl.BlockSpec(memory_space=pltpu.SMEM)
Y, XL, FIRST, LIVE, CORE, XH = range(6)


def ring(n, k):
    return [(i, (i + k) % n) for i in range(n)]


def home(xl, z):
    return (xl, z) if z // 2 == xl else (1 - xl, (z + 2) % 4)


def swap_pairs(flip):
    pairs = []
    for xl in range(2):
        for z in range(4):
            for xh in range(2):
                a, b = home(xl, z)
                pairs.append(((xl * 4 + z) * 2 + xh, (a * 4 + b) * 2 + (xh ^ flip)))
    return pairs


def after(x, *others):
    return lax.optimization_barrier((x, *others))[0]


def aligned(i, unit):
    return pl.ds(pl.multiple_of(i * unit, unit), unit)


def y_of(sc, p):
    return lax.rem(sc[Y] + OFFS[p], 4)


def load_rows(sc, pieces, dst, sem):
    rows, width = pieces[0].shape
    half = rows // 2
    copies = []
    for part in range(2):
        some = pl.ds(part * half, half)
        for p in range(4):
            piece = pieces[0].at[some] if p == 0 else pieces[2 * p - 1 + part]
            where = aligned(y_of(sc, p), width)
            copies.append(pltpu.make_async_copy(piece, dst.at[some, where], sem.at[part * 4 + p]))
    return copies


def load_weight(sc, pair, w, row, dst, sem, at_sem):
    copies = []
    for c, ref in enumerate(pair):
        core = sc[CORE] if c == 0 else 1 - sc[CORE]
        for slot in range(4):
            for flip in range(2):
                xh = 1 - sc[XH] if flip else sc[XH]
                cb = slot % 2 * 4 + xh * 2 + core
                copies.append(
                    pltpu.make_async_copy(
                        ref.at[slot, flip, w],
                        dst.at[:, pl.ds(row + slot // 2 * HID, HID), aligned(cb, COLS)],
                        sem.at[at_sem + c * 8 + slot * 2 + flip],
                    )
                )
    return copies


def expert_of(sc, block):
    return (sc[FIRST] <= block * BLOCK).astype(jnp.int32)


def by_tile(sc, tile, work):
    low, high = expert_of(sc, 2 * tile), expert_of(sc, 2 * tile + 1)
    start = tile * TILE

    @pl.when(low == high)
    def _():
        work(start, TILE, low)

    @pl.when(low != high)
    def _():
        work(start, BLOCK, low)
        work(start + BLOCK, BLOCK, high)


def start_all(copies):
    for c in copies:
        c.start()
    return copies


def wait_all(copies):
    for c in copies:
        c.wait()


def pre_kernel(n, sc, x0, x1, x2, x3, x4, x5, x6, w0, w1, own, *rest):
    sends, (xv, wv, ov, sv, xsem, wsem, osem) = rest[:n], rest[n:]
    wload = []
    for w in range(n):
        wload += load_weight(sc, (w0, w1), w, w * 2 * HID, wv, wsem, w * 16)
    xload = load_rows(sc, (x0, x1, x2, x3, x4, x5, x6), xv, xsem)
    start_all(wload + xload)
    wait_all(wload)
    outs = []

    def work(start, size, expert):
        at = pl.ds(start, size)
        part = lax.dot_general(xv[at, :], wv[expert], NT, preferred_element_type=F32)
        ov[at, :] = part
        sv[at, :] = part.astype(BF)

    for t in range(xv.shape[0] // TILE):
        if t % 2 == 0:
            wait_all(xload[t * 2 : t * 2 + 4])
        by_tile(sc, t, work)
        at = pl.ds(t * TILE, TILE)
        outs += start_all([pltpu.make_async_copy(ov.at[at], own.at[at], osem.at[3 * t])])
        for w, send in enumerate(sends):
            some = sv.at[at, pl.ds(w * 2 * HID, 2 * HID)]
            outs += start_all([pltpu.make_async_copy(some, send.at[at], osem.at[3 * t + 1 + w])])
    wait_all(outs)


def pre_part(sc, pieces, weight):
    rows, width = pieces[0].shape
    nw = weight[0].shape[2]
    wide, n = 4 * width, nw * 2 * HID
    return pl.pallas_call(
        functools.partial(pre_kernel, nw),
        out_shape=(jax.ShapeDtypeStruct((rows, n), F32),)
        + (jax.ShapeDtypeStruct((rows, 2 * HID), BF),) * nw,
        in_specs=[SM] + [ANY] * 9,
        out_specs=(ANY,) * (1 + nw),
        scratch_shapes=[
            pltpu.VMEM((rows, wide), BF),
            pltpu.VMEM((EXP, n, wide), BF),
            pltpu.VMEM((rows, n), F32),
            pltpu.VMEM((rows, n), BF),
            pltpu.SemaphoreType.DMA((8,)),
            pltpu.SemaphoreType.DMA((nw * 16,)),
            pltpu.SemaphoreType.DMA((rows // TILE * 3,)),
        ],
        compiler_params=pltpu.CompilerParams(vmem_limit_bytes=VMEM),
        cost_estimate=pl.CostEstimate(
            flops=4 * rows * n * wide, bytes_accessed=10 << 20, transcendentals=0
        ),
    )(sc, *pieces, *weight)


def column(row):
    return jnp.transpose(jnp.broadcast_to(row, (BLOCK, BLOCK)))[:, :1]


def transposed_into(dst, sc, b, at, rows, value):
    expert = expert_of(sc, b)
    dst[expert, rows, at] = jnp.transpose(value)
    dst[1 - expert, rows, at] = jnp.zeros((rows.stop - rows.start, BLOCK), value.dtype)


def weight_out(sc, src, row, e, keep, away, w, sem):
    outs = []
    for rel, out in enumerate((keep, away)):
        core = sc[CORE] if rel == 0 else 1 - sc[CORE]
        for h in range(2):
            for zz in range(2):
                for xh in range(2):
                    i = (((w * EXP + e) * 2 + rel) * 2 + h) * 4 + zz * 2 + xh
                    outs.append(
                        pltpu.make_async_copy(
                            src.at[e, pl.ds(row + h * HID, HID), aligned((zz * 2 + xh) * 2 + core, COLS)],
                            out.at[h * 2 + zz, xh, w, e],
                            sem.at[i],
                        )
                    )
    return outs


def down_kernel(
    sc, scores, own_gu, got_g, got_u, g0, g1, g2, g3, g4, g5, g6, keep, away, gv, st, dd, gsem, dsem
):
    rows, width = g0.shape
    gload = start_all(load_rows(sc, (g0, g1, g2, g3, g4, g5, g6), gv, gsem))

    @pl.loop(0, rows // BLOCK)
    def _(b):
        at = aligned(b, BLOCK)
        live = (b * BLOCK < sc[LIVE]).astype(F32)
        gate = own_gu[at, : 2 * HID] + got_g[at, :].astype(F32)
        up = own_gu[at, 2 * HID :] + got_u[at, :].astype(F32)
        hidden = (gate * jax.nn.sigmoid(gate) * up).astype(BF).astype(F32)
        scaled = (column(scores[pl.ds(b, 1), :]) * live * hidden).astype(BF)
        transposed_into(st, sc, b, at, slice(0, 2 * HID), scaled)

    wait_all(gload)
    outs = []
    for e in range(EXP):
        for n in range(4):
            at = pl.ds(n * width, width)
            dd[e, :, at] = jnp.dot(st[e], gv[:, at], preferred_element_type=F32).astype(BF)
        outs += start_all(weight_out(sc, dd, 0, e, keep, away, 0, dsem))
    wait_all(outs)


def down_part(sc, scores, own_gu, got_g, got_u, grads):
    rows, width = grads[0].shape
    out = jax.ShapeDtypeStruct((4, 2, 1, EXP, HID, COLS), BF)
    return pl.pallas_call(
        down_kernel,
        out_shape=(out, out),
        in_specs=[SM] + [VM] * 4 + [ANY] * 7,
        out_specs=(ANY, ANY),
        scratch_shapes=[
            pltpu.VMEM((rows, 4 * width), BF),
            pltpu.VMEM((EXP, 2 * HID, rows), BF),
            pltpu.VMEM((EXP, 2 * HID, 4 * width), BF),
            pltpu.SemaphoreType.DMA((8,)),
            pltpu.SemaphoreType.DMA((32,)),
        ],
        compiler_params=pltpu.CompilerParams(vmem_limit_bytes=VMEM),
        cost_estimate=pl.CostEstimate(
            flops=8 * rows * HID * 4 * width, bytes_accessed=14 << 20, transcendentals=rows * 384
        ),
    )(sc, scores, own_gu, got_g, got_u, *grads)


def gate_up_kernel(
    sc, scores, own_gu, got_g, got_u, own_b, got_b, x0, x1, x2, x3, x4, x5, x6,
    sgrad, gu, keep, away, xv, gut, dgu, ogu, gg, gup, ob, gb, guv, xsem, dsem, isem, usem,
):
    rows, width = x0.shape
    n = 2 * HID
    per = rows // 4
    iload = []
    for t in range(4):
        at = pl.ds(t * per, per)
        for i, (src, dst) in enumerate(((own_gu, ogu), (got_g, gg), (got_u, gup), (own_b, ob), (got_b, gb))):
            iload.append(pltpu.make_async_copy(src.at[at], dst.at[at], isem.at[t * 5 + i]))
    xload = load_rows(sc, (x0, x1, x2, x3, x4, x5, x6), xv, xsem)
    start_all(iload + xload)
    outs = []

    def block(b):
        at = aligned(b, BLOCK)
        live = (b * BLOCK < sc[LIVE]).astype(F32)
        gate = ogu[at, :n] + gg[at, :].astype(F32)
        up = ogu[at, n:] + gup[at, :].astype(F32)
        back = ob[at, :] + gb[at, :].astype(F32)
        sig = jax.nn.sigmoid(gate)
        act = gate * sig
        hidden = (act * up).astype(BF).astype(F32)
        mine = (lax.broadcasted_iota(jnp.int32, hidden.shape, 1) >= HID).astype(jnp.int32) == sc[XL]
        total = jnp.sum(jnp.where(mine, hidden * back, 0.0), axis=1, keepdims=True) * live
        sgrad[pl.ds(b, 1), :] = jnp.transpose(jnp.broadcast_to(total, (BLOCK, BLOCK)))[:1]
        hid_grad = column(scores[pl.ds(b, 1), :]) * live * back
        gate_grad = (hid_grad * up * sig * (1.0 + gate * (1.0 - sig))).astype(BF)
        up_grad = (hid_grad * act).astype(BF)
        guv[at, :n] = gate_grad
        guv[at, n:] = up_grad
        transposed_into(gut, sc, b, at, slice(0, n), gate_grad)
        transposed_into(gut, sc, b, at, slice(n, 2 * n), up_grad)

    for t in range(4):
        wait_all(iload[t * 5 : t * 5 + 5])

        @pl.loop(t * per // BLOCK, (t + 1) * per // BLOCK)
        def _(b):
            block(b)

        at = pl.ds(t * per, per)
        outs += start_all([pltpu.make_async_copy(guv.at[at], gu.at[at], usem.at[t])])

    wait_all(xload)
    for e in range(EXP):
        for k in range(4):
            at = pl.ds(k * width, width)
            dgu[e, :, at] = jnp.dot(gut[e], xv[:, at], preferred_element_type=F32).astype(BF)
        for w in range(2):
            outs += start_all(weight_out(sc, dgu, w * n, e, keep, away, w, dsem))
    wait_all(outs)


def gate_up_part(sc, scores, own_gu, got_g, got_u, own_b, got_b, feats):
    rows, width = feats[0].shape
    out = jax.ShapeDtypeStruct((4, 2, 2, EXP, HID, COLS), BF)
    return pl.pallas_call(
        gate_up_kernel,
        out_shape=(
            jax.ShapeDtypeStruct((rows // BLOCK, BLOCK), F32),
            jax.ShapeDtypeStruct((rows, 4 * HID), BF),
            out,
            out,
        ),
        in_specs=[SM, VM] + [ANY] * 12,
        out_specs=(VM, ANY, ANY, ANY),
        scratch_shapes=[
            pltpu.VMEM((rows, 4 * width), BF),
            pltpu.VMEM((EXP, 4 * HID, rows), BF),
            pltpu.VMEM((EXP, 4 * HID, 4 * width), BF),
            pltpu.VMEM((rows, 4 * HID), F32),
            pltpu.VMEM((rows, 2 * HID), BF),
            pltpu.VMEM((rows, 2 * HID), BF),
            pltpu.VMEM((rows, 2 * HID), F32),
            pltpu.VMEM((rows, 2 * HID), BF),
            pltpu.VMEM((rows, 4 * HID), BF),
            pltpu.SemaphoreType.DMA((8,)),
            pltpu.SemaphoreType.DMA((64,)),
            pltpu.SemaphoreType.DMA((20,)),
            pltpu.SemaphoreType.DMA((4,)),
        ],
        compiler_params=pltpu.CompilerParams(vmem_limit_bytes=VMEM),
        cost_estimate=pl.CostEstimate(
            flops=16 * rows * HID * 4 * width, bytes_accessed=20 << 20, transcendentals=rows * 384
        ),
    )(sc, scores, own_gu, got_g, got_u, own_b, got_b, *feats)


def rows_kernel(sc, gu, w0, w1, d0, d1, d2, d3, wv, guv, dxv, wsem, usem, osem):
    rows, wide = dxv.shape
    width = wide // 4
    load = load_weight(sc, (w0, w1), 0, 0, wv, wsem, 0) + load_weight(sc, (w0, w1), 1, 2 * HID, wv, wsem, 16)
    load.append(pltpu.make_async_copy(gu, guv, usem.at[0]))
    wait_all(start_all(load))

    def work(start, size, expert):
        at = pl.ds(start, size)
        dxv[at, :] = jnp.dot(guv[at, :], wv[expert], preferred_element_type=F32).astype(BF)

    outs = []
    for t in range(rows // TILE):
        by_tile(sc, t, work)
        at = pl.ds(t * TILE, TILE)
        for p, d in enumerate((d0, d1, d2, d3)):
            where = aligned(y_of(sc, p), width)
            outs += start_all([pltpu.make_async_copy(dxv.at[at, where], d.at[at], osem.at[t * 4 + p])])
    wait_all(outs)


def rows_part(sc, gu, weight):
    rows, width = gu.shape[0], 512
    return pl.pallas_call(
        rows_kernel,
        out_shape=(jax.ShapeDtypeStruct((rows, width), BF),) * 4,
        in_specs=[SM] + [ANY] * 3,
        out_specs=(ANY,) * 4,
        scratch_shapes=[
            pltpu.VMEM((EXP, 4 * HID, 4 * width), BF),
            pltpu.VMEM((rows, 4 * HID), BF),
            pltpu.VMEM((rows, 4 * width), BF),
            pltpu.SemaphoreType.DMA((32,)),
            pltpu.SemaphoreType.DMA((1,)),
            pltpu.SemaphoreType.DMA((16,)),
        ],
        compiler_params=pltpu.CompilerParams(vmem_limit_bytes=VMEM),
        cost_estimate=pl.CostEstimate(
            flops=8 * rows * HID * 4 * width, bytes_accessed=14 << 20, transcendentals=0
        ),
    )(sc, gu, *weight)


def halves_over(x):
    half = x.shape[0] // 2
    near = [lax.ppermute(x[:half], "y", ring(4, k)) for k in (1, 3)]
    rest = [lax.ppermute(x[half:], "y", ring(4, k)) for k in (1, 3)]
    return x, near[0], rest[0], near[1], rest[1]


def opposite_over(pieces):
    return lax.ppermute(pieces[1], "y", ring(4, 1)), lax.ppermute(pieces[4], "y", ring(4, 3))


def to_plane(w):
    return (
        lax.ppermute(w, ("xl", "z", "xh"), swap_pairs(0)),
        lax.ppermute(w, ("xl", "z", "xh"), swap_pairs(1)),
    )


def spread_pair(pair, *before):
    here = after(lax.all_gather(pair, "z", axis=0, tiled=False), *before)
    return here, lax.ppermute(here, "core", ring(2, 1))


def over_cores_kernel(keep_gu, got_gu, keep_d, got_d, out):
    out[:, :, :2] = (keep_gu[...].astype(F32) + got_gu[...].astype(F32)).astype(BF)
    out[:, :, 2:] = (keep_d[...].astype(F32) + got_d[...].astype(F32)).astype(BF)


def over_cores(keep_gu, got_gu, keep_d, got_d):
    def block(n):
        return pl.BlockSpec((1, 1, n, EXP, HID, COLS), lambda i, j: (i, j, 0, 0, 0, 0))

    return pl.pallas_call(
        over_cores_kernel,
        out_shape=jax.ShapeDtypeStruct((4, 2, 3, EXP, HID, COLS), BF),
        grid=(4, 2),
        in_specs=[block(2), block(2), block(1), block(1)],
        out_specs=block(3),
        compiler_params=pltpu.CompilerParams(vmem_limit_bytes=VMEM),
        cost_estimate=pl.CostEstimate(flops=3 << 20, bytes_accessed=14 << 20, transcendentals=0),
    )(keep_gu, got_gu, keep_d, got_d)


def over_chips(part, xh):
    straight = lax.dynamic_index_in_dim(part, xh, 0, False)
    crossed = lax.dynamic_index_in_dim(part, 1 - xh, 0, False)
    straight = lax.ppermute(straight, ("xl", "z", "xh"), swap_pairs(0))
    crossed = lax.ppermute(crossed, ("xl", "z", "xh"), swap_pairs(1))
    return straight.astype(F32) + crossed.astype(F32)


def on_device(features, grad_out, scores, counts, w_gate, w_up, w_down):
    rows = features.shape[0]
    y, xl, core, xh = (lax.axis_index(a) for a in ("y", "xl", "core", "xh"))
    sc = jnp.stack([y, xl, counts[0, 0], counts[0, 0] + counts[0, 1], core, xh]).astype(jnp.int32)
    scores = scores.reshape(rows // BLOCK, BLOCK)

    feats = halves_over(features)
    feats += opposite_over(feats)
    straight, crossed = to_plane(jnp.stack([w_gate, w_up, w_down]))
    pair_gu = after(jnp.stack([straight[:2], crossed[:2]]), feats[1], feats[3])
    pair_d = jnp.stack([straight[2:], crossed[2:]])
    grads = halves_over(after(grad_out, feats[5], feats[6]))
    gu_all = spread_pair(pair_gu, *feats[1:], pair_d, grads[1], grads[3])

    own_gu, send_g, send_u = pre_part(sc, feats, gu_all)
    got_g = lax.ppermute(send_g, "xl", ring(2, 1))
    got_u = lax.ppermute(send_u, "xl", ring(2, 1))
    grads += opposite_over(grads)
    own_b, send_b = pre_part(sc, grads, spread_pair(pair_d, got_g, *grads[2:]))
    got_b = lax.ppermute(send_b, "xl", ring(2, 1))

    keep, away = down_part(after(sc, send_b), scores, own_gu, got_g, got_u, grads)
    keep_d, got_d = keep, lax.ppermute(away, "core", ring(2, 1))
    got_b = after(got_b, away)
    total, gu, keep, away = gate_up_part(
        sc, scores, own_gu, got_g, got_u, own_b, got_b, feats
    )
    got = lax.ppermute(away, "core", ring(2, 1))
    total = total + lax.ppermute(total, "y", [(i, i ^ 1) for i in range(4)])
    both = over_cores(after(keep, total), got, keep_d, got_d)
    part = lax.psum_scatter(both, "z", scatter_dimension=0, tiled=False)

    dx = rows_part(sc, after(gu, both), gu_all)
    total = total + after(lax.ppermute(total, "y", [(i, i ^ 2) for i in range(4)]), dx[0])
    dx, _ = lax.optimization_barrier((dx, total))
    total = total + lax.ppermute(total, "xl", ring(2, 1))
    from_below = lax.ppermute(dx[2], "y", ring(4, 1))
    from_above = lax.ppermute(dx[1], "y", ring(4, 3))
    opposite = lax.ppermute(dx[3], "y", ring(4, 2))
    grad_features = (
        (dx[0].astype(F32) + from_below.astype(F32)) + (from_above.astype(F32) + opposite.astype(F32))
    ).astype(BF)

    weights = over_chips(part, xh)
    return grad_features, total.reshape(rows), weights[0], weights[1], weights[2]


def solution(mesh):
    fine = Mesh(mesh.devices.reshape(2, 4, 4, 2, 2), ("xl", "y", "z", "xh", "core"))
    grp, blk = ("xl", "y"), ("z", "xh", "core")
    weight = P(None, grp, blk)
    return jax.shard_map(
        on_device,
        mesh=fine,
        in_specs=(P(blk, grp), P(blk, grp), P(blk), P(blk, None), weight, weight, weight),
        out_specs=(P(blk, grp), P(blk), weight, weight, weight),
        check_vma=False,
    )
```

```python
import functools

import jax
import jax.numpy as jnp
from jax import lax
from jax.experimental import pallas as pl
from jax.experimental.pallas import tpu as pltpu
from jax.sharding import Mesh
from jax.sharding import PartitionSpec as P

EXP = 2
BLOCK = 128
TILE = 256
HID = 192
VMEM = 60 << 20
COLS = 256
BF = jnp.bfloat16
F32 = jnp.float32
NT = (((1,), (1,)), ((), ()))
OFFS = (0, 3, 1, 2)
ANY = pl.BlockSpec(memory_space=pl.ANY)
VM = pl.BlockSpec(memory_space=pltpu.VMEM)
SM = pl.BlockSpec(memory_space=pltpu.SMEM)
Y, XL, FIRST, LIVE, CORE, XH = range(6)


def ring(n, k):
    return [(i, (i + k) % n) for i in range(n)]


def home(xl, z):
    return (xl, z) if z // 2 == xl else (1 - xl, (z + 2) % 4)


def swap_pairs(flip):
    pairs = []
    for xl in range(2):
        for z in range(4):
            for xh in range(2):
                a, b = home(xl, z)
                pairs.append(((xl * 4 + z) * 2 + xh, (a * 4 + b) * 2 + (xh ^ flip)))
    return pairs


def after(x, *others):
    return lax.optimization_barrier((x, *others))[0]


def aligned(i, unit):
    return pl.ds(pl.multiple_of(i * unit, unit), unit)


def y_of(sc, p):
    return lax.rem(sc[Y] + OFFS[p], 4)


def load_rows(sc, pieces, dst, sem):
    rows, width = pieces[0].shape
    half = rows // 2
    copies = []
    for part in range(2):
        some = pl.ds(part * half, half)
        for p in range(4):
            piece = pieces[0].at[some] if p == 0 else pieces[2 * p - 1 + part]
            where = aligned(y_of(sc, p), width)
            copies.append(pltpu.make_async_copy(piece, dst.at[some, where], sem.at[part * 4 + p]))
    return copies


def load_weight(sc, pair, w, row, dst, sem, at_sem):
    copies = []
    for c, ref in enumerate(pair):
        core = sc[CORE] if c == 0 else 1 - sc[CORE]
        for slot in range(4):
            for flip in range(2):
                xh = 1 - sc[XH] if flip else sc[XH]
                cb = slot % 2 * 4 + xh * 2 + core
                copies.append(
                    pltpu.make_async_copy(
                        ref.at[slot, flip, w],
                        dst.at[:, pl.ds(row + slot // 2 * HID, HID), aligned(cb, COLS)],
                        sem.at[at_sem + c * 8 + slot * 2 + flip],
                    )
                )
    return copies


def expert_of(sc, block):
    return (sc[FIRST] <= block * BLOCK).astype(jnp.int32)


def by_tile(sc, tile, work):
    low, high = expert_of(sc, 2 * tile), expert_of(sc, 2 * tile + 1)
    start = tile * TILE

    @pl.when(low == high)
    def _():
        work(start, TILE, low)

    @pl.when(low != high)
    def _():
        work(start, BLOCK, low)
        work(start + BLOCK, BLOCK, high)


def start_all(copies):
    for c in copies:
        c.start()
    return copies


def wait_all(copies):
    for c in copies:
        c.wait()


def pre_kernel(n, sc, x0, x1, x2, x3, x4, x5, x6, w0, w1, own, *rest):
    sends, (xv, wv, ov, sv, xsem, wsem, osem) = rest[:n], rest[n:]
    wload = []
    for w in range(n):
        wload += load_weight(sc, (w0, w1), w, w * 2 * HID, wv, wsem, w * 16)
    xload = load_rows(sc, (x0, x1, x2, x3, x4, x5, x6), xv, xsem)
    start_all(wload + xload)
    wait_all(wload)
    outs = []

    def work(start, size, expert):
        at = pl.ds(start, size)
        part = lax.dot_general(xv[at, :], wv[expert], NT, preferred_element_type=F32)
        ov[at, :] = part
        sv[at, :] = part.astype(BF)

    for t in range(xv.shape[0] // TILE):
        if t % 2 == 0:
            wait_all(xload[t * 2 : t * 2 + 4])
        by_tile(sc, t, work)
        at = pl.ds(t * TILE, TILE)
        outs += start_all([pltpu.make_async_copy(ov.at[at], own.at[at], osem.at[3 * t])])
        for w, send in enumerate(sends):
            some = sv.at[at, pl.ds(w * 2 * HID, 2 * HID)]
            outs += start_all([pltpu.make_async_copy(some, send.at[at], osem.at[3 * t + 1 + w])])
    wait_all(outs)


def pre_part(sc, pieces, weight):
    rows, width = pieces[0].shape
    nw = weight[0].shape[2]
    wide, n = 4 * width, nw * 2 * HID
    return pl.pallas_call(
        functools.partial(pre_kernel, nw),
        out_shape=(jax.ShapeDtypeStruct((rows, n), F32),)
        + (jax.ShapeDtypeStruct((rows, 2 * HID), BF),) * nw,
        in_specs=[SM] + [ANY] * 9,
        out_specs=(ANY,) * (1 + nw),
        scratch_shapes=[
            pltpu.VMEM((rows, wide), BF),
            pltpu.VMEM((EXP, n, wide), BF),
            pltpu.VMEM((rows, n), F32),
            pltpu.VMEM((rows, n), BF),
            pltpu.SemaphoreType.DMA((8,)),
            pltpu.SemaphoreType.DMA((nw * 16,)),
            pltpu.SemaphoreType.DMA((rows // TILE * 3,)),
        ],
        compiler_params=pltpu.CompilerParams(vmem_limit_bytes=VMEM),
        cost_estimate=pl.CostEstimate(
            flops=4 * rows * n * wide, bytes_accessed=10 << 20, transcendentals=0
        ),
    )(sc, *pieces, *weight)


def column(row):
    return jnp.transpose(jnp.broadcast_to(row, (BLOCK, BLOCK)))[:, :1]


def transposed_into(dst, sc, b, at, rows, value):
    expert = expert_of(sc, b)
    dst[expert, rows, at] = jnp.transpose(value)
    dst[1 - expert, rows, at] = jnp.zeros((rows.stop - rows.start, BLOCK), value.dtype)


def weight_out(sc, src, row, e, keep, away, w, sem):
    outs = []
    for rel, out in enumerate((keep, away)):
        core = sc[CORE] if rel == 0 else 1 - sc[CORE]
        for h in range(2):
            for zz in range(2):
                for xh in range(2):
                    i = (((w * EXP + e) * 2 + rel) * 2 + h) * 4 + zz * 2 + xh
                    outs.append(
                        pltpu.make_async_copy(
                            src.at[e, pl.ds(row + h * HID, HID), aligned((zz * 2 + xh) * 2 + core, COLS)],
                            out.at[h * 2 + zz, xh, w, e],
                            sem.at[i],
                        )
                    )
    return outs


def down_kernel(
    sc, scores, own_gu, got_g, got_u, g0, g1, g2, g3, g4, g5, g6, keep, away, gv, st, dd, gsem, dsem
):
    rows, width = g0.shape
    gload = start_all(load_rows(sc, (g0, g1, g2, g3, g4, g5, g6), gv, gsem))

    @pl.loop(0, rows // BLOCK)
    def _(b):
        at = aligned(b, BLOCK)
        live = (b * BLOCK < sc[LIVE]).astype(F32)
        gate = own_gu[at, : 2 * HID] + got_g[at, :].astype(F32)
        up = own_gu[at, 2 * HID :] + got_u[at, :].astype(F32)
        hidden = (gate * jax.nn.sigmoid(gate) * up).astype(BF).astype(F32)
        scaled = (column(scores[pl.ds(b, 1), :]) * live * hidden).astype(BF)
        transposed_into(st, sc, b, at, slice(0, 2 * HID), scaled)

    wait_all(gload)
    outs = []
    for e in range(EXP):
        for n in range(4):
            at = pl.ds(n * width, width)
            dd[e, :, at] = jnp.dot(st[e], gv[:, at], preferred_element_type=F32).astype(BF)
        outs += start_all(weight_out(sc, dd, 0, e, keep, away, 0, dsem))
    wait_all(outs)


def down_part(sc, scores, own_gu, got_g, got_u, grads):
    rows, width = grads[0].shape
    out = jax.ShapeDtypeStruct((4, 2, 1, EXP, HID, COLS), BF)
    return pl.pallas_call(
        down_kernel,
        out_shape=(out, out),
        in_specs=[SM] + [VM] * 4 + [ANY] * 7,
        out_specs=(ANY, ANY),
        scratch_shapes=[
            pltpu.VMEM((rows, 4 * width), BF),
            pltpu.VMEM((EXP, 2 * HID, rows), BF),
            pltpu.VMEM((EXP, 2 * HID, 4 * width), BF),
            pltpu.SemaphoreType.DMA((8,)),
            pltpu.SemaphoreType.DMA((32,)),
        ],
        compiler_params=pltpu.CompilerParams(vmem_limit_bytes=VMEM),
        cost_estimate=pl.CostEstimate(
            flops=8 * rows * HID * 4 * width, bytes_accessed=14 << 20, transcendentals=rows * 384
        ),
    )(sc, scores, own_gu, got_g, got_u, *grads)


def gate_up_kernel(
    sc, scores, own_gu, got_g, got_u, own_b, got_b, x0, x1, x2, x3, x4, x5, x6,
    sgrad, gu, keep, away, xv, gut, dgu, ogu, gg, gup, ob, gb, guv, xsem, dsem, isem, usem,
):
    rows, width = x0.shape
    n = 2 * HID
    per = rows // 4
    iload = []
    for t in range(4):
        at = pl.ds(t * per, per)
        for i, (src, dst) in enumerate(((own_gu, ogu), (got_g, gg), (got_u, gup), (own_b, ob), (got_b, gb))):
            iload.append(pltpu.make_async_copy(src.at[at], dst.at[at], isem.at[t * 5 + i]))
    xload = load_rows(sc, (x0, x1, x2, x3, x4, x5, x6), xv, xsem)
    start_all(iload + xload)
    outs = []

    def block(b):
        at = aligned(b, BLOCK)
        live = (b * BLOCK < sc[LIVE]).astype(F32)
        gate = ogu[at, :n] + gg[at, :].astype(F32)
        up = ogu[at, n:] + gup[at, :].astype(F32)
        back = ob[at, :] + gb[at, :].astype(F32)
        sig = jax.nn.sigmoid(gate)
        act = gate * sig
        hidden = (act * up).astype(BF).astype(F32)
        mine = (lax.broadcasted_iota(jnp.int32, hidden.shape, 1) >= HID).astype(jnp.int32) == sc[XL]
        total = jnp.sum(jnp.where(mine, hidden * back, 0.0), axis=1, keepdims=True) * live
        sgrad[pl.ds(b, 1), :] = jnp.transpose(jnp.broadcast_to(total, (BLOCK, BLOCK)))[:1]
        hid_grad = column(scores[pl.ds(b, 1), :]) * live * back
        gate_grad = (hid_grad * up * sig * (1.0 + gate * (1.0 - sig))).astype(BF)
        up_grad = (hid_grad * act).astype(BF)
        guv[at, :n] = gate_grad
        guv[at, n:] = up_grad
        transposed_into(gut, sc, b, at, slice(0, n), gate_grad)
        transposed_into(gut, sc, b, at, slice(n, 2 * n), up_grad)

    for t in range(4):
        wait_all(iload[t * 5 : t * 5 + 5])

        @pl.loop(t * per // BLOCK, (t + 1) * per // BLOCK)
        def _(b):
            block(b)

        at = pl.ds(t * per, per)
        outs += start_all([pltpu.make_async_copy(guv.at[at], gu.at[at], usem.at[t])])

    wait_all(xload)
    for e in range(EXP):
        for k in range(4):
            at = pl.ds(k * width, width)
            dgu[e, :, at] = jnp.dot(gut[e], xv[:, at], preferred_element_type=F32).astype(BF)
        for w in range(2):
            outs += start_all(weight_out(sc, dgu, w * n, e, keep, away, w, dsem))
    wait_all(outs)


def gate_up_part(sc, scores, own_gu, got_g, got_u, own_b, got_b, feats):
    rows, width = feats[0].shape
    out = jax.ShapeDtypeStruct((4, 2, 2, EXP, HID, COLS), BF)
    return pl.pallas_call(
        gate_up_kernel,
        out_shape=(
            jax.ShapeDtypeStruct((rows // BLOCK, BLOCK), F32),
            jax.ShapeDtypeStruct((rows, 4 * HID), BF),
            out,
            out,
        ),
        in_specs=[SM, VM] + [ANY] * 12,
        out_specs=(VM, ANY, ANY, ANY),
        scratch_shapes=[
            pltpu.VMEM((rows, 4 * width), BF),
            pltpu.VMEM((EXP, 4 * HID, rows), BF),
            pltpu.VMEM((EXP, 4 * HID, 4 * width), BF),
            pltpu.VMEM((rows, 4 * HID), F32),
            pltpu.VMEM((rows, 2 * HID), BF),
            pltpu.VMEM((rows, 2 * HID), BF),
            pltpu.VMEM((rows, 2 * HID), F32),
            pltpu.VMEM((rows, 2 * HID), BF),
            pltpu.VMEM((rows, 4 * HID), BF),
            pltpu.SemaphoreType.DMA((8,)),
            pltpu.SemaphoreType.DMA((64,)),
            pltpu.SemaphoreType.DMA((20,)),
            pltpu.SemaphoreType.DMA((4,)),
        ],
        compiler_params=pltpu.CompilerParams(vmem_limit_bytes=VMEM),
        cost_estimate=pl.CostEstimate(
            flops=16 * rows * HID * 4 * width, bytes_accessed=20 << 20, transcendentals=rows * 384
        ),
    )(sc, scores, own_gu, got_g, got_u, own_b, got_b, *feats)


def rows_kernel(sc, gu, w0, w1, d0, d1, d2, d3, wv, guv, dxv, wsem, usem, osem):
    rows, wide = dxv.shape
    width = wide // 4
    load = load_weight(sc, (w0, w1), 0, 0, wv, wsem, 0) + load_weight(sc, (w0, w1), 1, 2 * HID, wv, wsem, 16)
    load.append(pltpu.make_async_copy(gu, guv, usem.at[0]))
    wait_all(start_all(load))

    def work(start, size, expert):
        at = pl.ds(start, size)
        dxv[at, :] = jnp.dot(guv[at, :], wv[expert], preferred_element_type=F32).astype(BF)

    outs = []
    for t in range(rows // TILE):
        by_tile(sc, t, work)
        at = pl.ds(t * TILE, TILE)
        for p, d in enumerate((d0, d1, d2, d3)):
            where = aligned(y_of(sc, p), width)
            outs += start_all([pltpu.make_async_copy(dxv.at[at, where], d.at[at], osem.at[t * 4 + p])])
    wait_all(outs)


def rows_part(sc, gu, weight):
    rows, width = gu.shape[0], 512
    return pl.pallas_call(
        rows_kernel,
        out_shape=(jax.ShapeDtypeStruct((rows, width), BF),) * 4,
        in_specs=[SM] + [ANY] * 3,
        out_specs=(ANY,) * 4,
        scratch_shapes=[
            pltpu.VMEM((EXP, 4 * HID, 4 * width), BF),
            pltpu.VMEM((rows, 4 * HID), BF),
            pltpu.VMEM((rows, 4 * width), BF),
            pltpu.SemaphoreType.DMA((32,)),
            pltpu.SemaphoreType.DMA((1,)),
            pltpu.SemaphoreType.DMA((16,)),
        ],
        compiler_params=pltpu.CompilerParams(vmem_limit_bytes=VMEM),
        cost_estimate=pl.CostEstimate(
            flops=8 * rows * HID * 4 * width, bytes_accessed=14 << 20, transcendentals=0
        ),
    )(sc, gu, *weight)


def halves_over(x):
    half = x.shape[0] // 2
    near = [lax.ppermute(x[:half], "y", ring(4, k)) for k in (1, 3)]
    rest = [lax.ppermute(x[half:], "y", ring(4, k)) for k in (1, 3)]
    return x, near[0], rest[0], near[1], rest[1]


def opposite_over(pieces):
    return lax.ppermute(pieces[1], "y", ring(4, 1)), lax.ppermute(pieces[4], "y", ring(4, 3))


def to_plane(w):
    return (
        lax.ppermute(w, ("xl", "z", "xh"), swap_pairs(0)),
        lax.ppermute(w, ("xl", "z", "xh"), swap_pairs(1)),
    )


def spread_pair(pair, *before):
    here = after(lax.all_gather(pair, "z", axis=0, tiled=False), *before)
    return here, lax.ppermute(here, "core", ring(2, 1))


def over_cores(keep, got):
    return (keep.astype(F32) + got.astype(F32)).astype(BF)


def over_z(both, z):
    slots = [lax.dynamic_index_in_dim(both, lax.rem(z + k, 4), 0, False) for k in range(4)]
    return slots[:1] + [lax.ppermute(slots[k], "z", ring(4, k)) for k in (1, 3, 2)]


def over_chips(part, xh):
    straight = lax.dynamic_index_in_dim(part, xh, 0, False)
    crossed = lax.dynamic_index_in_dim(part, 1 - xh, 0, False)
    straight = lax.ppermute(straight, ("xl", "z", "xh"), swap_pairs(0))
    crossed = lax.ppermute(crossed, ("xl", "z", "xh"), swap_pairs(1))
    return straight.astype(F32) + crossed.astype(F32)


def on_device(features, grad_out, scores, counts, w_gate, w_up, w_down):
    rows = features.shape[0]
    y, xl, core, xh = (lax.axis_index(a) for a in ("y", "xl", "core", "xh"))
    sc = jnp.stack([y, xl, counts[0, 0], counts[0, 0] + counts[0, 1], core, xh]).astype(jnp.int32)
    scores = scores.reshape(rows // BLOCK, BLOCK)

    feats = halves_over(features)
    feats += opposite_over(feats)
    pair_gu = after(jnp.stack(to_plane(jnp.stack([w_gate, w_up]))), feats[1], feats[3])
    grads = halves_over(after(grad_out, feats[5], feats[6]))
    gu_all = spread_pair(pair_gu, *feats[1:], grads[1], grads[3])
    down_moved = to_plane(after(w_down, gu_all[1])[None])

    own_gu, send_g, send_u = pre_part(sc, feats, gu_all)
    got_g = lax.ppermute(send_g, "xl", ring(2, 1))
    pair_d = jnp.stack(after(down_moved, send_g))
    got_u = lax.ppermute(send_u, "xl", ring(2, 1))
    grads += opposite_over(grads)
    own_b, send_b = pre_part(sc, grads, spread_pair(pair_d, got_g, *grads[2:]))
    got_b = lax.ppermute(send_b, "xl", ring(2, 1))

    keep, away = down_part(after(sc, send_b), scores, own_gu, got_g, got_u, grads)
    got_b = after(got_b, away)
    both_d = over_cores(keep, lax.ppermute(away, "core", ring(2, 1)))
    parts_d = over_z(both_d, lax.axis_index("z"))
    total, gu, keep, away = gate_up_part(
        sc, scores, own_gu, got_g, got_u, own_b, got_b, feats
    )
    got = lax.ppermute(away, "core", ring(2, 1))
    total = total + lax.ppermute(total, "y", [(i, i ^ 1) for i in range(4)])
    both = over_cores(after(keep, total, both_d), got)
    part = lax.psum_scatter(both, "z", scatter_dimension=0, tiled=False)

    dx = rows_part(sc, after(gu, both), gu_all)
    total = total + after(lax.ppermute(total, "y", [(i, i ^ 2) for i in range(4)]), dx[0])
    dx, _ = lax.optimization_barrier((dx, total))
    total = total + lax.ppermute(total, "xl", ring(2, 1))
    from_below = lax.ppermute(dx[2], "y", ring(4, 1))
    from_above = lax.ppermute(dx[1], "y", ring(4, 3))
    opposite = lax.ppermute(dx[3], "y", ring(4, 2))
    grad_features = (
        (dx[0].astype(F32) + from_below.astype(F32)) + (from_above.astype(F32) + opposite.astype(F32))
    ).astype(BF)

    part_d = sum(p.astype(F32) for p in parts_d).astype(BF)
    grad_down = over_chips(after(part_d, both), xh)
    grad_gu = over_chips(after(part, grad_down), xh)
    return grad_features, total.reshape(rows), grad_gu[0], grad_gu[1], grad_down[0]


def solution(mesh):
    fine = Mesh(mesh.devices.reshape(2, 4, 4, 2, 2), ("xl", "y", "z", "xh", "core"))
    grp, blk = ("xl", "y"), ("z", "xh", "core")
    weight = P(None, grp, blk)
    return jax.shard_map(
        on_device,
        mesh=fine,
        in_specs=(P(blk, grp), P(blk, grp), P(blk), P(blk, None), weight, weight, weight),
        out_specs=(P(blk, grp), P(blk), weight, weight, weight),
        check_vma=False,
    )
```

```python
import functools

import jax
import jax.numpy as jnp
from jax import lax
from jax.experimental import pallas as pl
from jax.experimental.pallas import tpu as pltpu
from jax.sharding import Mesh
from jax.sharding import PartitionSpec as P

EXP = 2
BLOCK = 128
TILE = 256
HID = 192
VMEM = 60 << 20
COLS = 256
BF = jnp.bfloat16
F32 = jnp.float32
NT = (((1,), (1,)), ((), ()))
OFFS = (0, 3, 1, 2)
ANY = pl.BlockSpec(memory_space=pl.ANY)
VM = pl.BlockSpec(memory_space=pltpu.VMEM)
SM = pl.BlockSpec(memory_space=pltpu.SMEM)
Y, XL, FIRST, LIVE, CORE, XH = range(6)


def ring(n, k):
    return [(i, (i + k) % n) for i in range(n)]


def home(xl, z):
    return (xl, z) if z // 2 == xl else (1 - xl, (z + 2) % 4)


def swap_pairs(flip):
    pairs = []
    for xl in range(2):
        for z in range(4):
            for xh in range(2):
                a, b = home(xl, z)
                pairs.append(((xl * 4 + z) * 2 + xh, (a * 4 + b) * 2 + (xh ^ flip)))
    return pairs


def after(x, *others):
    return lax.optimization_barrier((x, *others))[0]


def aligned(i, unit):
    return pl.ds(pl.multiple_of(i * unit, unit), unit)


def y_of(sc, p):
    return lax.rem(sc[Y] + OFFS[p], 4)


def load_rows(sc, pieces, dst, sem):
    rows, width = pieces[0].shape
    half = rows // 2
    copies = []
    for part in range(2):
        some = pl.ds(part * half, half)
        for p in range(4):
            piece = pieces[0].at[some] if p == 0 else pieces[2 * p - 1 + part]
            where = aligned(y_of(sc, p), width)
            copies.append(pltpu.make_async_copy(piece, dst.at[some, where], sem.at[part * 4 + p]))
    return copies


def load_weight(sc, pair, w, row, dst, sem, at_sem):
    copies = []
    for c, ref in enumerate(pair):
        core = sc[CORE] if c == 0 else 1 - sc[CORE]
        for slot in range(4):
            for flip in range(2):
                xh = 1 - sc[XH] if flip else sc[XH]
                cb = slot % 2 * 4 + xh * 2 + core
                copies.append(
                    pltpu.make_async_copy(
                        ref.at[slot, flip, w],
                        dst.at[:, pl.ds(row + slot // 2 * HID, HID), aligned(cb, COLS)],
                        sem.at[at_sem + c * 8 + slot * 2 + flip],
                    )
                )
    return copies


def expert_of(sc, block):
    return (sc[FIRST] <= block * BLOCK).astype(jnp.int32)


def by_tile(sc, tile, work):
    low, high = expert_of(sc, 2 * tile), expert_of(sc, 2 * tile + 1)
    start = tile * TILE

    @pl.when(low == high)
    def _():
        work(start, TILE, low)

    @pl.when(low != high)
    def _():
        work(start, BLOCK, low)
        work(start + BLOCK, BLOCK, high)


def start_all(copies):
    for c in copies:
        c.start()
    return copies


def wait_all(copies):
    for c in copies:
        c.wait()


def pre_kernel(n, sc, x0, x1, x2, x3, x4, x5, x6, w0, w1, own, *rest):
    sends, (xv, wv, ov, sv, xsem, wsem, osem) = rest[:n], rest[n:]
    wload = []
    for w in range(n):
        wload += load_weight(sc, (w0, w1), w, w * 2 * HID, wv, wsem, w * 16)
    xload = load_rows(sc, (x0, x1, x2, x3, x4, x5, x6), xv, xsem)
    start_all(wload + xload)
    wait_all(wload)
    outs = []

    def work(start, size, expert):
        at = pl.ds(start, size)
        part = lax.dot_general(xv[at, :], wv[expert], NT, preferred_element_type=F32)
        ov[at, :] = part
        sv[at, :] = part.astype(BF)

    for t in range(xv.shape[0] // TILE):
        if t % 2 == 0:
            wait_all(xload[t * 2 : t * 2 + 4])
        by_tile(sc, t, work)
        at = pl.ds(t * TILE, TILE)
        outs += start_all([pltpu.make_async_copy(ov.at[at], own.at[at], osem.at[3 * t])])
        for w, send in enumerate(sends):
            some = sv.at[at, pl.ds(w * 2 * HID, 2 * HID)]
            outs += start_all([pltpu.make_async_copy(some, send.at[at], osem.at[3 * t + 1 + w])])
    wait_all(outs)


def pre_part(sc, pieces, weight):
    rows, width = pieces[0].shape
    nw = weight[0].shape[2]
    wide, n = 4 * width, nw * 2 * HID
    return pl.pallas_call(
        functools.partial(pre_kernel, nw),
        out_shape=(jax.ShapeDtypeStruct((rows, n), F32),)
        + (jax.ShapeDtypeStruct((rows, 2 * HID), BF),) * nw,
        in_specs=[SM] + [ANY] * 9,
        out_specs=(ANY,) * (1 + nw),
        scratch_shapes=[
            pltpu.VMEM((rows, wide), BF),
            pltpu.VMEM((EXP, n, wide), BF),
            pltpu.VMEM((rows, n), F32),
            pltpu.VMEM((rows, n), BF),
            pltpu.SemaphoreType.DMA((8,)),
            pltpu.SemaphoreType.DMA((nw * 16,)),
            pltpu.SemaphoreType.DMA((rows // TILE * 3,)),
        ],
        compiler_params=pltpu.CompilerParams(vmem_limit_bytes=VMEM),
        cost_estimate=pl.CostEstimate(
            flops=4 * rows * n * wide, bytes_accessed=10 << 20, transcendentals=0
        ),
    )(sc, *pieces, *weight)


def column(row):
    return jnp.transpose(jnp.broadcast_to(row, (BLOCK, BLOCK)))[:, :1]


def transposed_into(dst, sc, b, at, rows, value):
    expert = expert_of(sc, b)
    dst[expert, rows, at] = jnp.transpose(value)
    dst[1 - expert, rows, at] = jnp.zeros((rows.stop - rows.start, BLOCK), value.dtype)


def weight_out(sc, src, row, e, keep, away, w, sem):
    outs = []
    for rel, out in enumerate((keep, away)):
        core = sc[CORE] if rel == 0 else 1 - sc[CORE]
        for h in range(2):
            for zz in range(2):
                for xh in range(2):
                    i = (((w * EXP + e) * 2 + rel) * 2 + h) * 4 + zz * 2 + xh
                    outs.append(
                        pltpu.make_async_copy(
                            src.at[e, pl.ds(row + h * HID, HID), aligned((zz * 2 + xh) * 2 + core, COLS)],
                            out.at[h * 2 + zz, xh, w, e],
                            sem.at[i],
                        )
                    )
    return outs


def down_kernel(
    sc, scores, own_gu, got_g, got_u, g0, g1, g2, g3, g4, g5, g6, keep, away, gv, st, dd, gsem, dsem
):
    rows, width = g0.shape
    gload = start_all(load_rows(sc, (g0, g1, g2, g3, g4, g5, g6), gv, gsem))

    @pl.loop(0, rows // BLOCK)
    def _(b):
        at = aligned(b, BLOCK)
        live = (b * BLOCK < sc[LIVE]).astype(F32)
        gate = own_gu[at, : 2 * HID] + got_g[at, :].astype(F32)
        up = own_gu[at, 2 * HID :] + got_u[at, :].astype(F32)
        hidden = (gate * jax.nn.sigmoid(gate) * up).astype(BF).astype(F32)
        scaled = (column(scores[pl.ds(b, 1), :]) * live * hidden).astype(BF)
        transposed_into(st, sc, b, at, slice(0, 2 * HID), scaled)

    wait_all(gload)
    outs = []
    for e in range(EXP):
        for n in range(4):
            at = pl.ds(n * width, width)
            dd[e, :, at] = jnp.dot(st[e], gv[:, at], preferred_element_type=F32).astype(BF)
        outs += start_all(weight_out(sc, dd, 0, e, keep, away, 0, dsem))
    wait_all(outs)


def down_part(sc, scores, own_gu, got_g, got_u, grads):
    rows, width = grads[0].shape
    out = jax.ShapeDtypeStruct((4, 2, 1, EXP, HID, COLS), BF)
    return pl.pallas_call(
        down_kernel,
        out_shape=(out, out),
        in_specs=[SM] + [VM] * 4 + [ANY] * 7,
        out_specs=(ANY, ANY),
        scratch_shapes=[
            pltpu.VMEM((rows, 4 * width), BF),
            pltpu.VMEM((EXP, 2 * HID, rows), BF),
            pltpu.VMEM((EXP, 2 * HID, 4 * width), BF),
            pltpu.SemaphoreType.DMA((8,)),
            pltpu.SemaphoreType.DMA((32,)),
        ],
        compiler_params=pltpu.CompilerParams(vmem_limit_bytes=VMEM),
        cost_estimate=pl.CostEstimate(
            flops=8 * rows * HID * 4 * width, bytes_accessed=14 << 20, transcendentals=rows * 384
        ),
    )(sc, scores, own_gu, got_g, got_u, *grads)


def gate_up_kernel(
    sc, scores, own_gu, got_g, got_u, own_b, got_b, x0, x1, x2, x3, x4, x5, x6,
    sgrad, gu, keep, away, xv, gut, dgu, ogu, gg, gup, ob, gb, guv, xsem, dsem, isem, usem,
):
    rows, width = x0.shape
    n = 2 * HID
    per = rows // 4
    iload = []
    for t in range(4):
        at = pl.ds(t * per, per)
        for i, (src, dst) in enumerate(((own_gu, ogu), (got_g, gg), (got_u, gup), (own_b, ob), (got_b, gb))):
            iload.append(pltpu.make_async_copy(src.at[at], dst.at[at], isem.at[t * 5 + i]))
    xload = load_rows(sc, (x0, x1, x2, x3, x4, x5, x6), xv, xsem)
    start_all(iload + xload)
    outs = []

    def block(b):
        at = aligned(b, BLOCK)
        live = (b * BLOCK < sc[LIVE]).astype(F32)
        gate = ogu[at, :n] + gg[at, :].astype(F32)
        up = ogu[at, n:] + gup[at, :].astype(F32)
        back = ob[at, :] + gb[at, :].astype(F32)
        sig = jax.nn.sigmoid(gate)
        act = gate * sig
        hidden = (act * up).astype(BF).astype(F32)
        mine = (lax.broadcasted_iota(jnp.int32, hidden.shape, 1) >= HID).astype(jnp.int32) == sc[XL]
        total = jnp.sum(jnp.where(mine, hidden * back, 0.0), axis=1, keepdims=True) * live
        sgrad[pl.ds(b, 1), :] = jnp.transpose(jnp.broadcast_to(total, (BLOCK, BLOCK)))[:1]
        hid_grad = column(scores[pl.ds(b, 1), :]) * live * back
        gate_grad = (hid_grad * up * sig * (1.0 + gate * (1.0 - sig))).astype(BF)
        up_grad = (hid_grad * act).astype(BF)
        guv[at, :n] = gate_grad
        guv[at, n:] = up_grad
        transposed_into(gut, sc, b, at, slice(0, n), gate_grad)
        transposed_into(gut, sc, b, at, slice(n, 2 * n), up_grad)

    for t in range(4):
        wait_all(iload[t * 5 : t * 5 + 5])

        @pl.loop(t * per // BLOCK, (t + 1) * per // BLOCK)
        def _(b):
            block(b)

        at = pl.ds(t * per, per)
        outs += start_all([pltpu.make_async_copy(guv.at[at], gu.at[at], usem.at[t])])

    wait_all(xload)
    for e in range(EXP):
        for k in range(4):
            at = pl.ds(k * width, width)
            dgu[e, :, at] = jnp.dot(gut[e], xv[:, at], preferred_element_type=F32).astype(BF)
        for w in range(2):
            outs += start_all(weight_out(sc, dgu, w * n, e, keep, away, w, dsem))
    wait_all(outs)


def gate_up_part(sc, scores, own_gu, got_g, got_u, own_b, got_b, feats):
    rows, width = feats[0].shape
    out = jax.ShapeDtypeStruct((4, 2, 2, EXP, HID, COLS), BF)
    return pl.pallas_call(
        gate_up_kernel,
        out_shape=(
            jax.ShapeDtypeStruct((rows // BLOCK, BLOCK), F32),
            jax.ShapeDtypeStruct((rows, 4 * HID), BF),
            out,
            out,
        ),
        in_specs=[SM, VM] + [ANY] * 12,
        out_specs=(VM, ANY, ANY, ANY),
        scratch_shapes=[
            pltpu.VMEM((rows, 4 * width), BF),
            pltpu.VMEM((EXP, 4 * HID, rows), BF),
            pltpu.VMEM((EXP, 4 * HID, 4 * width), BF),
            pltpu.VMEM((rows, 4 * HID), F32),
            pltpu.VMEM((rows, 2 * HID), BF),
            pltpu.VMEM((rows, 2 * HID), BF),
            pltpu.VMEM((rows, 2 * HID), F32),
            pltpu.VMEM((rows, 2 * HID), BF),
            pltpu.VMEM((rows, 4 * HID), BF),
            pltpu.SemaphoreType.DMA((8,)),
            pltpu.SemaphoreType.DMA((64,)),
            pltpu.SemaphoreType.DMA((20,)),
            pltpu.SemaphoreType.DMA((4,)),
        ],
        compiler_params=pltpu.CompilerParams(vmem_limit_bytes=VMEM),
        cost_estimate=pl.CostEstimate(
            flops=16 * rows * HID * 4 * width, bytes_accessed=20 << 20, transcendentals=rows * 384
        ),
    )(sc, scores, own_gu, got_g, got_u, own_b, got_b, *feats)


def rows_kernel(sc, gu, w0, w1, d0, d1, d2, d3, wv, guv, dxv, wsem, usem, osem):
    rows, wide = dxv.shape
    width = wide // 4
    load = load_weight(sc, (w0, w1), 0, 0, wv, wsem, 0) + load_weight(sc, (w0, w1), 1, 2 * HID, wv, wsem, 16)
    load.append(pltpu.make_async_copy(gu, guv, usem.at[0]))
    wait_all(start_all(load))

    def work(start, size, expert):
        at = pl.ds(start, size)
        dxv[at, :] = jnp.dot(guv[at, :], wv[expert], preferred_element_type=F32).astype(BF)

    outs = []
    for t in range(rows // TILE):
        by_tile(sc, t, work)
        at = pl.ds(t * TILE, TILE)
        for p, d in enumerate((d0, d1, d2, d3)):
            where = aligned(y_of(sc, p), width)
            outs += start_all([pltpu.make_async_copy(dxv.at[at, where], d.at[at], osem.at[t * 4 + p])])
    wait_all(outs)


def rows_part(sc, gu, weight):
    rows, width = gu.shape[0], 512
    return pl.pallas_call(
        rows_kernel,
        out_shape=(jax.ShapeDtypeStruct((rows, width), BF),) * 4,
        in_specs=[SM] + [ANY] * 3,
        out_specs=(ANY,) * 4,
        scratch_shapes=[
            pltpu.VMEM((EXP, 4 * HID, 4 * width), BF),
            pltpu.VMEM((rows, 4 * HID), BF),
            pltpu.VMEM((rows, 4 * width), BF),
            pltpu.SemaphoreType.DMA((32,)),
            pltpu.SemaphoreType.DMA((1,)),
            pltpu.SemaphoreType.DMA((16,)),
        ],
        compiler_params=pltpu.CompilerParams(vmem_limit_bytes=VMEM),
        cost_estimate=pl.CostEstimate(
            flops=8 * rows * HID * 4 * width, bytes_accessed=14 << 20, transcendentals=0
        ),
    )(sc, gu, *weight)


def halves_over(x):
    half = x.shape[0] // 2
    near = [lax.ppermute(x[:half], "y", ring(4, k)) for k in (1, 3)]
    rest = [lax.ppermute(x[half:], "y", ring(4, k)) for k in (1, 3)]
    return x, near[0], rest[0], near[1], rest[1]


def opposite_over(pieces):
    return lax.ppermute(pieces[1], "y", ring(4, 1)), lax.ppermute(pieces[4], "y", ring(4, 3))


def to_plane(w):
    return (
        lax.ppermute(w, ("xl", "z", "xh"), swap_pairs(0)),
        lax.ppermute(w, ("xl", "z", "xh"), swap_pairs(1)),
    )


def spread_pair(pair, *before):
    here = after(lax.all_gather(pair, "z", axis=0, tiled=False), *before)
    return here, lax.ppermute(here, "core", ring(2, 1))


def over_cores(keep, got):
    return (keep.astype(F32) + got.astype(F32)).astype(BF)


def over_z(both, z):
    slots = [lax.dynamic_index_in_dim(both, lax.rem(z + k, 4), 0, False) for k in range(4)]
    return slots[:1] + [lax.ppermute(slots[k], "z", ring(4, k)) for k in (1, 3, 2)]


def over_chips(part, xh):
    straight = lax.dynamic_index_in_dim(part, xh, 0, False)
    crossed = lax.dynamic_index_in_dim(part, 1 - xh, 0, False)
    straight = lax.ppermute(straight, ("xl", "z", "xh"), swap_pairs(0))
    crossed = lax.ppermute(crossed, ("xl", "z", "xh"), swap_pairs(1))
    return straight.astype(F32) + crossed.astype(F32)


def on_device(features, grad_out, scores, counts, w_gate, w_up, w_down):
    rows = features.shape[0]
    y, xl, core, xh = (lax.axis_index(a) for a in ("y", "xl", "core", "xh"))
    sc = jnp.stack([y, xl, counts[0, 0], counts[0, 0] + counts[0, 1], core, xh]).astype(jnp.int32)
    scores = scores.reshape(rows // BLOCK, BLOCK)

    feats = halves_over(features)
    feats += opposite_over(feats)
    pair_gu = after(jnp.stack(to_plane(jnp.stack([w_gate, w_up]))), feats[1], feats[3])
    pair_d = jnp.stack(to_plane(after(w_down, feats[2], feats[4])[None]))
    grads = halves_over(after(grad_out, feats[5], feats[6]))
    gu_all = spread_pair(pair_gu, *feats[1:], pair_d, grads[1], grads[3])

    own_gu, send_g, send_u = pre_part(sc, feats, gu_all)
    got_g = lax.ppermute(send_g, "xl", ring(2, 1))
    got_u = lax.ppermute(send_u, "xl", ring(2, 1))
    grads += opposite_over(grads)
    own_b, send_b = pre_part(sc, grads, spread_pair(pair_d, got_g, *grads[2:]))
    got_b = lax.ppermute(send_b, "xl", ring(2, 1))

    keep, away = down_part(after(sc, send_b), scores, own_gu, got_g, got_u, grads)
    got_b = after(got_b, away)
    both_d = over_cores(keep, lax.ppermute(away, "core", ring(2, 1)))
    parts_d = over_z(both_d, lax.axis_index("z"))
    total, gu, keep, away = gate_up_part(
        sc, scores, own_gu, got_g, got_u, own_b, got_b, feats
    )
    got = lax.ppermute(away, "core", ring(2, 1))
    total = total + lax.ppermute(total, "y", [(i, i ^ 1) for i in range(4)])
    both = over_cores(after(keep, total), got)
    part = lax.psum_scatter(both, "z", scatter_dimension=0, tiled=False)

    dx = rows_part(sc, after(gu, both), gu_all)
    total = total + after(lax.ppermute(total, "y", [(i, i ^ 2) for i in range(4)]), dx[0])
    dx, _ = lax.optimization_barrier((dx, total))
    total = total + lax.ppermute(total, "xl", ring(2, 1))
    from_below = lax.ppermute(dx[2], "y", ring(4, 1))
    from_above = lax.ppermute(dx[1], "y", ring(4, 3))
    opposite = lax.ppermute(dx[3], "y", ring(4, 2))
    grad_features = (
        (dx[0].astype(F32) + from_below.astype(F32)) + (from_above.astype(F32) + opposite.astype(F32))
    ).astype(BF)

    part_d = sum(p.astype(F32) for p in parts_d).astype(BF)
    grad_down = over_chips(after(part_d, both), xh)
    grad_gu = over_chips(after(part, grad_down), xh)
    return grad_features, total.reshape(rows), grad_gu[0], grad_gu[1], grad_down[0]


def solution(mesh):
    fine = Mesh(mesh.devices.reshape(2, 4, 4, 2, 2), ("xl", "y", "z", "xh", "core"))
    grp, blk = ("xl", "y"), ("z", "xh", "core")
    weight = P(None, grp, blk)
    return jax.shard_map(
        on_device,
        mesh=fine,
        in_specs=(P(blk, grp), P(blk, grp), P(blk), P(blk, None), weight, weight, weight),
        out_specs=(P(blk, grp), P(blk), weight, weight, weight),
        check_vma=False,
    )
```

```python
import functools

import jax
import jax.numpy as jnp
from jax import lax
from jax.experimental import pallas as pl
from jax.experimental.pallas import tpu as pltpu
from jax.sharding import Mesh
from jax.sharding import PartitionSpec as P

EXP = 2
BLOCK = 128
TILE = 256
HID = 192
VMEM = 60 << 20
COLS = 256
BF = jnp.bfloat16
F32 = jnp.float32
NT = (((1,), (1,)), ((), ()))
OFFS = (0, 3, 1, 2)
ANY = pl.BlockSpec(memory_space=pl.ANY)
VM = pl.BlockSpec(memory_space=pltpu.VMEM)
SM = pl.BlockSpec(memory_space=pltpu.SMEM)
Y, XL, FIRST, LIVE, CORE, XH = range(6)


def ring(n, k):
    return [(i, (i + k) % n) for i in range(n)]


def home(xl, z):
    return (xl, z) if z // 2 == xl else (1 - xl, (z + 2) % 4)


def swap_pairs(flip):
    pairs = []
    for xl in range(2):
        for z in range(4):
            for xh in range(2):
                a, b = home(xl, z)
                pairs.append(((xl * 4 + z) * 2 + xh, (a * 4 + b) * 2 + (xh ^ flip)))
    return pairs


def after(x, *others):
    return lax.optimization_barrier((x, *others))[0]


def aligned(i, unit):
    return pl.ds(pl.multiple_of(i * unit, unit), unit)


def y_of(sc, p):
    return lax.rem(sc[Y] + OFFS[p], 4)


def load_rows(sc, pieces, dst, sem):
    rows, width = pieces[0].shape
    half = rows // 2
    copies = []
    for part in range(2):
        some = pl.ds(part * half, half)
        for p in range(4):
            piece = pieces[0].at[some] if p == 0 else pieces[2 * p - 1 + part]
            where = aligned(y_of(sc, p), width)
            copies.append(pltpu.make_async_copy(piece, dst.at[some, where], sem.at[part * 4 + p]))
    return copies


def load_weight(sc, pair, w, row, dst, sem, at_sem):
    copies = []
    for c, ref in enumerate(pair):
        core = sc[CORE] if c == 0 else 1 - sc[CORE]
        for slot in range(4):
            for flip in range(2):
                xh = 1 - sc[XH] if flip else sc[XH]
                cb = slot % 2 * 4 + xh * 2 + core
                copies.append(
                    pltpu.make_async_copy(
                        ref.at[slot, flip, w],
                        dst.at[:, pl.ds(row + slot // 2 * HID, HID), aligned(cb, COLS)],
                        sem.at[at_sem + c * 8 + slot * 2 + flip],
                    )
                )
    return copies


def expert_of(sc, block):
    return (sc[FIRST] <= block * BLOCK).astype(jnp.int32)


def by_tile(sc, tile, work):
    low, high = expert_of(sc, 2 * tile), expert_of(sc, 2 * tile + 1)
    start = tile * TILE

    @pl.when(low == high)
    def _():
        work(start, TILE, low)

    @pl.when(low != high)
    def _():
        work(start, BLOCK, low)
        work(start + BLOCK, BLOCK, high)


def start_all(copies):
    for c in copies:
        c.start()
    return copies


def wait_all(copies):
    for c in copies:
        c.wait()


def pre_kernel(n, sc, x0, x1, x2, x3, x4, x5, x6, w0, w1, own, *rest):
    sends, (xv, wv, ov, sv, xsem, wsem, osem) = rest[:n], rest[n:]
    wload = []
    for w in range(n):
        wload += load_weight(sc, (w0, w1), w, w * 2 * HID, wv, wsem, w * 16)
    xload = load_rows(sc, (x0, x1, x2, x3, x4, x5, x6), xv, xsem)
    start_all(wload + xload)
    wait_all(wload)
    outs = []

    def work(start, size, expert):
        at = pl.ds(start, size)
        part = lax.dot_general(xv[at, :], wv[expert], NT, preferred_element_type=F32)
        ov[at, :] = part
        sv[at, :] = part.astype(BF)

    for t in range(xv.shape[0] // TILE):
        if t % 2 == 0:
            wait_all(xload[t * 2 : t * 2 + 4])
        by_tile(sc, t, work)
        at = pl.ds(t * TILE, TILE)
        outs += start_all([pltpu.make_async_copy(ov.at[at], own.at[at], osem.at[3 * t])])
        for w, send in enumerate(sends):
            some = sv.at[at, pl.ds(w * 2 * HID, 2 * HID)]
            outs += start_all([pltpu.make_async_copy(some, send.at[at], osem.at[3 * t + 1 + w])])
    wait_all(outs)


def pre_part(sc, pieces, weight):
    rows, width = pieces[0].shape
    nw = weight[0].shape[2]
    wide, n = 4 * width, nw * 2 * HID
    return pl.pallas_call(
        functools.partial(pre_kernel, nw),
        out_shape=(jax.ShapeDtypeStruct((rows, n), F32),)
        + (jax.ShapeDtypeStruct((rows, 2 * HID), BF),) * nw,
        in_specs=[SM] + [ANY] * 9,
        out_specs=(ANY,) * (1 + nw),
        scratch_shapes=[
            pltpu.VMEM((rows, wide), BF),
            pltpu.VMEM((EXP, n, wide), BF),
            pltpu.VMEM((rows, n), F32),
            pltpu.VMEM((rows, n), BF),
            pltpu.SemaphoreType.DMA((8,)),
            pltpu.SemaphoreType.DMA((nw * 16,)),
            pltpu.SemaphoreType.DMA((rows // TILE * 3,)),
        ],
        compiler_params=pltpu.CompilerParams(vmem_limit_bytes=VMEM),
        cost_estimate=pl.CostEstimate(
            flops=4 * rows * n * wide, bytes_accessed=10 << 20, transcendentals=0
        ),
    )(sc, *pieces, *weight)


def column(row):
    return jnp.transpose(jnp.broadcast_to(row, (BLOCK, BLOCK)))[:, :1]


def transposed_into(dst, sc, b, at, rows, value):
    expert = expert_of(sc, b)
    dst[expert, rows, at] = jnp.transpose(value)
    dst[1 - expert, rows, at] = jnp.zeros((rows.stop - rows.start, BLOCK), value.dtype)


def weight_out(sc, src, row, e, keep, away, w, sem):
    outs = []
    for rel, out in enumerate((keep, away)):
        core = sc[CORE] if rel == 0 else 1 - sc[CORE]
        for h in range(2):
            for zz in range(2):
                for xh in range(2):
                    i = (((w * EXP + e) * 2 + rel) * 2 + h) * 4 + zz * 2 + xh
                    outs.append(
                        pltpu.make_async_copy(
                            src.at[e, pl.ds(row + h * HID, HID), aligned((zz * 2 + xh) * 2 + core, COLS)],
                            out.at[h * 2 + zz, xh, w, e],
                            sem.at[i],
                        )
                    )
    return outs


def expert_dot(sc, e, left, right, out, width):
    rows = right.shape[0]
    half = rows // 2

    def over(start, size):
        @pl.loop(0, right.shape[1] // width)
        def _(n):
            at, some = aligned(n, width), pl.ds(start, size)
            out[e, :, at] = jnp.dot(left[e, :, some], right[some, at], preferred_element_type=F32).astype(BF)

    second = sc[FIRST] > half if e == 0 else sc[LIVE] > half
    pl.when(jnp.logical_not(second))(lambda: over(0, half))
    if e == 0:
        pl.when(second)(lambda: over(0, rows))
    else:
        first = sc[FIRST] < half
        pl.when(jnp.logical_and(first, second))(lambda: over(0, rows))
        pl.when(jnp.logical_and(jnp.logical_not(first), second))(lambda: over(half, half))


def down_kernel(
    sc, scores, own_gu, got_g, got_u, g0, g1, g2, g3, g4, g5, g6, keep, away, gv, st, dd, gsem, dsem
):
    rows, width = g0.shape
    gload = start_all(load_rows(sc, (g0, g1, g2, g3, g4, g5, g6), gv, gsem))

    @pl.loop(0, rows // BLOCK)
    def _(b):
        at = aligned(b, BLOCK)
        live = (b * BLOCK < sc[LIVE]).astype(F32)
        gate = own_gu[at, : 2 * HID] + got_g[at, :].astype(F32)
        up = own_gu[at, 2 * HID :] + got_u[at, :].astype(F32)
        hidden = (gate * jax.nn.sigmoid(gate) * up).astype(BF).astype(F32)
        scaled = (column(scores[pl.ds(b, 1), :]) * live * hidden).astype(BF)
        transposed_into(st, sc, b, at, slice(0, 2 * HID), scaled)

    wait_all(gload)
    outs = []
    for e in range(EXP):
        expert_dot(sc, e, st, gv, dd, width)
        outs += start_all(weight_out(sc, dd, 0, e, keep, away, 0, dsem))
    wait_all(outs)


def down_part(sc, scores, own_gu, got_g, got_u, grads):
    rows, width = grads[0].shape
    out = jax.ShapeDtypeStruct((4, 2, 1, EXP, HID, COLS), BF)
    return pl.pallas_call(
        down_kernel,
        out_shape=(out, out),
        in_specs=[SM] + [VM] * 4 + [ANY] * 7,
        out_specs=(ANY, ANY),
        scratch_shapes=[
            pltpu.VMEM((rows, 4 * width), BF),
            pltpu.VMEM((EXP, 2 * HID, rows), BF),
            pltpu.VMEM((EXP, 2 * HID, 4 * width), BF),
            pltpu.SemaphoreType.DMA((8,)),
            pltpu.SemaphoreType.DMA((32,)),
        ],
        compiler_params=pltpu.CompilerParams(vmem_limit_bytes=VMEM),
        cost_estimate=pl.CostEstimate(
            flops=8 * rows * HID * 4 * width, bytes_accessed=14 << 20, transcendentals=rows * 384
        ),
    )(sc, scores, own_gu, got_g, got_u, *grads)


def gate_up_kernel(
    sc, scores, own_gu, got_g, got_u, own_b, got_b, x0, x1, x2, x3, x4, x5, x6,
    sgrad, gu, keep, away, xv, gut, dgu, ogu, gg, gup, ob, gb, guv, xsem, dsem, isem, usem,
):
    rows, width = x0.shape
    n = 2 * HID
    per = rows // 4
    iload = []
    for t in range(4):
        at = pl.ds(t * per, per)
        for i, (src, dst) in enumerate(((own_gu, ogu), (got_g, gg), (got_u, gup), (own_b, ob), (got_b, gb))):
            iload.append(pltpu.make_async_copy(src.at[at], dst.at[at], isem.at[t * 5 + i]))
    xload = load_rows(sc, (x0, x1, x2, x3, x4, x5, x6), xv, xsem)
    start_all(iload + xload)
    outs = []

    def block(b):
        at = aligned(b, BLOCK)
        live = (b * BLOCK < sc[LIVE]).astype(F32)
        gate = ogu[at, :n] + gg[at, :].astype(F32)
        up = ogu[at, n:] + gup[at, :].astype(F32)
        back = ob[at, :] + gb[at, :].astype(F32)
        sig = jax.nn.sigmoid(gate)
        act = gate * sig
        hidden = (act * up).astype(BF).astype(F32)
        mine = (lax.broadcasted_iota(jnp.int32, hidden.shape, 1) >= HID).astype(jnp.int32) == sc[XL]
        total = jnp.sum(jnp.where(mine, hidden * back, 0.0), axis=1, keepdims=True) * live
        sgrad[pl.ds(b, 1), :] = jnp.transpose(jnp.broadcast_to(total, (BLOCK, BLOCK)))[:1]
        hid_grad = column(scores[pl.ds(b, 1), :]) * live * back
        gate_grad = (hid_grad * up * sig * (1.0 + gate * (1.0 - sig))).astype(BF)
        up_grad = (hid_grad * act).astype(BF)
        guv[at, :n] = gate_grad
        guv[at, n:] = up_grad
        transposed_into(gut, sc, b, at, slice(0, n), gate_grad)
        transposed_into(gut, sc, b, at, slice(n, 2 * n), up_grad)

    for t in range(4):
        wait_all(iload[t * 5 : t * 5 + 5])

        @pl.loop(t * per // BLOCK, (t + 1) * per // BLOCK)
        def _(b):
            block(b)

        at = pl.ds(t * per, per)
        outs += start_all([pltpu.make_async_copy(guv.at[at], gu.at[at], usem.at[t])])

    wait_all(xload)
    for e in range(EXP):
        expert_dot(sc, e, gut, xv, dgu, width)
        for w in range(2):
            outs += start_all(weight_out(sc, dgu, w * n, e, keep, away, w, dsem))
    wait_all(outs)


def gate_up_part(sc, scores, own_gu, got_g, got_u, own_b, got_b, feats):
    rows, width = feats[0].shape
    out = jax.ShapeDtypeStruct((4, 2, 2, EXP, HID, COLS), BF)
    return pl.pallas_call(
        gate_up_kernel,
        out_shape=(
            jax.ShapeDtypeStruct((rows // BLOCK, BLOCK), F32),
            jax.ShapeDtypeStruct((rows, 4 * HID), BF),
            out,
            out,
        ),
        in_specs=[SM, VM] + [ANY] * 12,
        out_specs=(VM, ANY, ANY, ANY),
        scratch_shapes=[
            pltpu.VMEM((rows, 4 * width), BF),
            pltpu.VMEM((EXP, 4 * HID, rows), BF),
            pltpu.VMEM((EXP, 4 * HID, 4 * width), BF),
            pltpu.VMEM((rows, 4 * HID), F32),
            pltpu.VMEM((rows, 2 * HID), BF),
            pltpu.VMEM((rows, 2 * HID), BF),
            pltpu.VMEM((rows, 2 * HID), F32),
            pltpu.VMEM((rows, 2 * HID), BF),
            pltpu.VMEM((rows, 4 * HID), BF),
            pltpu.SemaphoreType.DMA((8,)),
            pltpu.SemaphoreType.DMA((64,)),
            pltpu.SemaphoreType.DMA((20,)),
            pltpu.SemaphoreType.DMA((4,)),
        ],
        compiler_params=pltpu.CompilerParams(vmem_limit_bytes=VMEM),
        cost_estimate=pl.CostEstimate(
            flops=16 * rows * HID * 4 * width, bytes_accessed=20 << 20, transcendentals=rows * 384
        ),
    )(sc, scores, own_gu, got_g, got_u, own_b, got_b, *feats)


def rows_kernel(sc, gu, w0, w1, d0, d1, d2, d3, wv, guv, dxv, wsem, usem, osem):
    rows, wide = dxv.shape
    width = wide // 4
    load = load_weight(sc, (w0, w1), 0, 0, wv, wsem, 0) + load_weight(sc, (w0, w1), 1, 2 * HID, wv, wsem, 16)
    load.append(pltpu.make_async_copy(gu, guv, usem.at[0]))
    wait_all(start_all(load))

    def work(start, size, expert):
        at = pl.ds(start, size)
        dxv[at, :] = jnp.dot(guv[at, :], wv[expert], preferred_element_type=F32).astype(BF)

    outs = []
    for t in range(rows // TILE):
        by_tile(sc, t, work)
        at = pl.ds(t * TILE, TILE)
        for p, d in enumerate((d0, d1, d2, d3)):
            where = aligned(y_of(sc, p), width)
            outs += start_all([pltpu.make_async_copy(dxv.at[at, where], d.at[at], osem.at[t * 4 + p])])
    wait_all(outs)


def rows_part(sc, gu, weight):
    rows, width = gu.shape[0], 512
    return pl.pallas_call(
        rows_kernel,
        out_shape=(jax.ShapeDtypeStruct((rows, width), BF),) * 4,
        in_specs=[SM] + [ANY] * 3,
        out_specs=(ANY,) * 4,
        scratch_shapes=[
            pltpu.VMEM((EXP, 4 * HID, 4 * width), BF),
            pltpu.VMEM((rows, 4 * HID), BF),
            pltpu.VMEM((rows, 4 * width), BF),
            pltpu.SemaphoreType.DMA((32,)),
            pltpu.SemaphoreType.DMA((1,)),
            pltpu.SemaphoreType.DMA((16,)),
        ],
        compiler_params=pltpu.CompilerParams(vmem_limit_bytes=VMEM),
        cost_estimate=pl.CostEstimate(
            flops=8 * rows * HID * 4 * width, bytes_accessed=14 << 20, transcendentals=0
        ),
    )(sc, gu, *weight)


def halves_over(x):
    half = x.shape[0] // 2
    near = [lax.ppermute(x[:half], "y", ring(4, k)) for k in (1, 3)]
    rest = [lax.ppermute(x[half:], "y", ring(4, k)) for k in (1, 3)]
    return x, near[0], rest[0], near[1], rest[1]


def opposite_over(pieces):
    return lax.ppermute(pieces[1], "y", ring(4, 1)), lax.ppermute(pieces[4], "y", ring(4, 3))


def to_plane(w):
    return (
        lax.ppermute(w, ("xl", "z", "xh"), swap_pairs(0)),
        lax.ppermute(w, ("xl", "z", "xh"), swap_pairs(1)),
    )


def spread_pair(pair, *before):
    here = after(lax.all_gather(pair, "z", axis=0, tiled=False), *before)
    return here, lax.ppermute(here, "core", ring(2, 1))


def over_cores(keep, got):
    return (keep.astype(F32) + got.astype(F32)).astype(BF)


def over_z(both, z):
    slots = [lax.dynamic_index_in_dim(both, lax.rem(z + k, 4), 0, False) for k in range(4)]
    return slots[:1] + [lax.ppermute(slots[k], "z", ring(4, k)) for k in (1, 3, 2)]


def over_chips(part, xh):
    straight = lax.dynamic_index_in_dim(part, xh, 0, False)
    crossed = lax.dynamic_index_in_dim(part, 1 - xh, 0, False)
    straight = lax.ppermute(straight, ("xl", "z", "xh"), swap_pairs(0))
    crossed = lax.ppermute(crossed, ("xl", "z", "xh"), swap_pairs(1))
    return straight.astype(F32) + crossed.astype(F32)


def on_device(features, grad_out, scores, counts, w_gate, w_up, w_down):
    rows = features.shape[0]
    y, xl, core, xh = (lax.axis_index(a) for a in ("y", "xl", "core", "xh"))
    sc = jnp.stack([y, xl, counts[0, 0], counts[0, 0] + counts[0, 1], core, xh]).astype(jnp.int32)
    scores = scores.reshape(rows // BLOCK, BLOCK)

    feats = halves_over(features)
    feats += opposite_over(feats)
    pair_gu = after(jnp.stack(to_plane(jnp.stack([w_gate, w_up]))), feats[1], feats[3])
    pair_d = jnp.stack(to_plane(after(w_down, feats[2], feats[4])[None]))
    grads = halves_over(after(grad_out, feats[5], feats[6]))
    gu_all = spread_pair(pair_gu, *feats[1:], pair_d, grads[1], grads[3])

    own_gu, send_g, send_u = pre_part(sc, feats, gu_all)
    got_g = lax.ppermute(send_g, "xl", ring(2, 1))
    got_u = lax.ppermute(send_u, "xl", ring(2, 1))
    grads += opposite_over(grads)
    own_b, send_b = pre_part(sc, grads, spread_pair(pair_d, got_g, *grads[2:]))
    got_b = lax.ppermute(send_b, "xl", ring(2, 1))

    keep, away = down_part(after(sc, send_b), scores, own_gu, got_g, got_u, grads)
    got_b = after(got_b, away)
    both_d = over_cores(keep, lax.ppermute(away, "core", ring(2, 1)))
    parts_d = over_z(both_d, lax.axis_index("z"))
    total, gu, keep, away = gate_up_part(
        sc, scores, own_gu, got_g, got_u, own_b, got_b, feats
    )
    got = lax.ppermute(away, "core", ring(2, 1))
    total = total + lax.ppermute(total, "y", [(i, i ^ 1) for i in range(4)])
    both = over_cores(after(keep, total, both_d), got)
    part = lax.psum_scatter(both, "z", scatter_dimension=0, tiled=False)

    dx = rows_part(sc, after(gu, both), gu_all)
    total = total + after(lax.ppermute(total, "y", [(i, i ^ 2) for i in range(4)]), dx[0])
    dx, _ = lax.optimization_barrier((dx, total))
    total = total + lax.ppermute(total, "xl", ring(2, 1))
    from_below = lax.ppermute(dx[2], "y", ring(4, 1))
    from_above = lax.ppermute(dx[1], "y", ring(4, 3))
    opposite = lax.ppermute(dx[3], "y", ring(4, 2))
    grad_features = (
        (dx[0].astype(F32) + from_below.astype(F32)) + (from_above.astype(F32) + opposite.astype(F32))
    ).astype(BF)

    part_d = sum(p.astype(F32) for p in parts_d).astype(BF)
    grad_down = over_chips(after(part_d, both), xh)
    grad_gu = over_chips(after(part, grad_down), xh)
    return grad_features, total.reshape(rows), grad_gu[0], grad_gu[1], grad_down[0]


def solution(mesh):
    fine = Mesh(mesh.devices.reshape(2, 4, 4, 2, 2), ("xl", "y", "z", "xh", "core"))
    grp, blk = ("xl", "y"), ("z", "xh", "core")
    weight = P(None, grp, blk)
    return jax.shard_map(
        on_device,
        mesh=fine,
        in_specs=(P(blk, grp), P(blk, grp), P(blk), P(blk, None), weight, weight, weight),
        out_specs=(P(blk, grp), P(blk), weight, weight, weight),
        check_vma=False,
    )
```
